32 devices in a mesh: req: 8 (over y, x, core), exp: 4 (over z).
Axes of the slice: x: 2, y: 2, z: 4, core: 2. Of those that a mesh axis runs over, the one named last changes fastest.
Arguments:
- attention_out: bfloat16 [1024, 4096], P('req'), may hold values from -6 to 6
- residual: bfloat16 [1024, 4096], P('req', 'exp'), may hold values from -6 to 6
- w_out: bfloat16 [4096, 4096], P('req', 'exp'), may hold values from -0.09375 to 0.09375
- router_w: float32 [4096, 4], P('exp'), may hold values from -0.09375 to 0.09375
- norm_gain: float32 [4096], P('exp'), may hold values from 0.5 to 1.5
- page_pool: bfloat16 [2048, 8, 2048], P('req', None, 'exp'), may hold values from -6 to 6
- page_table: int32 [1024, 2], P('req'), may hold values from 0 to 255, as said below
- cache_len: int32 [1024], P('req'), may hold values from 1 to 16
- came_from: int32 [1024], replicated, may hold values from 0 to 1023, as said below
- routes: int32 [1024, 2], P('req'), may hold values from 0 to 3, all different within a row; in each aligned block of 128 rows (0 to 127, 128 to 255, ...) at most 64 rows name the same one
- w_gate: bfloat16 [8, 4096, 7168], P('req', None, 'exp'), as said below
- w_up: bfloat16 [8, 4096, 7168], P('req', None, 'exp'), as said below
- w_down: bfloat16 [8, 7168, 4096], P('req', 'exp'), as said below
Outputs:
- mixed: float32 [1024, 4096], P('req', 'exp')
- new_pages: bfloat16 [1024, 2, 8, 2048], P('req', None, None, 'exp')
The draws below stay inside these ranges and needn't reach their ends.
Inputs may be any that keep to these rules, and one draw needn't show every extreme that they name: page_table's entries for the requests of one req group are distinct. came_from is a permutation; from each req group 4 rows go to each of the other 7 groups, each group receives 4 rows from each of them, and all other rows keep their place. `routes`: within the rows of one req group every expert is named by at most 64 rows, and some expert by exactly 64 rows in some group. `w_gate`: slices e and e + 4 along the first dimension are equal. `w_up`: slices e and e + 4 along the first dimension are equal. `w_down`: slices e and e + 4 along the first dimension are equal.
All inputs are finite; a program needn't handle non-finite values.
Results may differ from the reference program's by a relative error of at most 0.0055.
Values may be sent and summed in bfloat16 or wider, within the bound.
No kernel may reach another device: no remote copies, remote signals or barrier semaphores. Data moves between devices by JAX's collectives and lax.ppermute only.
A program may use at most 128 MiB of HBM per device.

```python
import math
import jax
import jax.numpy as jnp
import numpy as np
from jax import lax

D = 4096
KVS = 2048
FF = 7168
SLICE = 1792
EXPERTS = 4
TOP = 2
ROW_REQ = 128
ROWS = 1024
CAP = 32
MIG_PAIR = 4
PAGE = 8
PPR = 2
POOL = 256
N_REQ = 8
N_EXP = 4


def stacked_weight(key, shape, fan):
    base_weight = jax.random.normal(key, shape, jnp.float32) * fan ** (-0.5)
    return jnp.concatenate([base_weight, base_weight], axis=0).astype(jnp.bfloat16)


def draw_w_gate(key, part):
    return stacked_weight(jax.random.fold_in(key, 11), (EXPERTS, D, FF), D)


def draw_w_up(key, part):
    return stacked_weight(jax.random.fold_in(key, 12), (EXPERTS, D, FF), D)


def draw_w_down(key, part):
    return stacked_weight(jax.random.fold_in(key, 13), (EXPERTS, FF, D), FF)


def draw_page_table(key, part):
    groups = ROWS // ROW_REQ
    group_keys = jax.random.split(jax.random.fold_in(key, 21), groups)
    orders = jax.vmap(lambda one_key: jax.random.permutation(one_key, POOL))(group_keys)
    return orders.reshape(ROWS, PPR).astype(jnp.int32)


def draw_came_from(key, part):
    groups = ROWS // ROW_REQ
    senders = groups - 1
    moving = senders * MIG_PAIR
    order_key = jax.random.fold_in(key, 32)
    shifts = jnp.arange(1, groups, dtype=jnp.int32)
    orders = jax.vmap(lambda one_key: jax.random.permutation(one_key, ROW_REQ))(jax.random.split(order_key, groups)).astype(jnp.int32)
    slot_ids = jnp.arange(moving, dtype=jnp.int32)
    block_index = slot_ids // MIG_PAIR
    group_ids = jnp.arange(groups, dtype=jnp.int32)
    source = (group_ids[:, None] - shifts[block_index][None, :]) % groups
    src_rows = source * ROW_REQ + orders[source, slot_ids[None, :]]
    dest_rows = group_ids[:, None] * ROW_REQ + orders[:, :moving]
    identity_rows = jnp.arange(ROWS, dtype=jnp.int32)
    return identity_rows.at[dest_rows.reshape(-1)].set(src_rows.reshape(-1)).astype(jnp.int32)


def place_ends(entries, key, least, top_value):
    spot = [jax.random.randint(jax.random.fold_in(key, axis), (), 0, length) for axis, length in enumerate(entries.shape)]
    main_axis = entries.shape.index(max(entries.shape))
    beside = spot[:main_axis] + [(spot[main_axis] + 1) % entries.shape[main_axis]] + spot[main_axis + 1:]
    return entries.at[tuple(spot)].set(least).at[tuple(beside)].set(top_value)


def steps_of(key, shape, shards, smallest, largest):
    factor_of = 1.0
    for axis_at, parts in shards:
        steps = jax.random.uniform(jax.random.fold_in(jax.random.fold_in(key, 6), axis_at), (parts,), jnp.float32, smallest / len(shards), largest / len(shards))
        factor_of = factor_of * jnp.repeat(jnp.exp(steps), shape[axis_at] // parts).reshape((-1,) + (1,) * (len(shape) - 1 - axis_at))
    return factor_of


def shared_out(own_key, own, number, rows, number_of, top, reach, lean):
    ranking = jax.random.permutation(own_key, number_of)
    crowded, ordinary = load_shares(number_of, rows * top, reach, lean, True), load_shares(number_of, rows * top, reach, lean, False)
    places = jnp.arange(number_of)

    def named(tallies, turn):
        used = int((tallies > 0).sum())
        fixed = max(1, used // 4)
        passed = fixed + (places - fixed + turn * (used - fixed)) % max(1, number_of - fixed)
        return jnp.zeros((number_of,), jnp.int32).at[ranking[jnp.where(places < fixed, places, passed)]].set(jnp.asarray(tallies, jnp.int32))

    tallies = jnp.where(number % 4 == 0, named(crowded, number // 4), named(ordinary, number - number // 4 - 1))
    mixed = jax.random.permutation(jax.random.fold_in(own, 3), number_of)
    giver, receiver = mixed[0:number_of // 2 * 2:2], mixed[1:number_of // 2 * 2:2]
    slack = jnp.minimum(tallies[giver] - 1, reach - tallies[receiver]) // 2
    slack = jnp.where((giver == ranking[0]) | (receiver == ranking[0]) | (tallies[receiver] == 0), 0, jnp.maximum(slack, 0))
    passed = jax.random.randint(jax.random.fold_in(own, 4), (number_of // 2,), 0, 1 << 20) % (slack + 1)
    tallies = tallies.at[giver].add(-passed).at[receiver].add(passed)
    items = jnp.searchsorted(jnp.cumsum(tallies), jnp.arange(rows * top), side="right").astype(jnp.int32)
    listing = items.reshape(top, rows).T
    listing = listing[jax.random.permutation(jax.random.fold_in(own, 1), rows)]
    turn = jax.random.randint(jax.random.fold_in(own, 2), (rows, 1), 0, top)
    return jnp.take_along_axis(listing, (jnp.arange(top)[None, :] + turn) % top, axis=1)


def load_shares(count, total, most, slope, full):
    loads = [(1 << 20) // math.isqrt(standing ** slope) + 1 for standing in range(1, count + 1)]
    largest = most if full else min(most, max(-(-total // count), total * loads[0] // sum(loads)))
    least = 1 if total - largest >= count - 1 else 0
    given, spare = [largest] + [least] * (count - 1), total - largest - least * (count - 1)
    while spare > 0:
        candidates = [i for i in range(1, count) if given[i] < largest] or [i for i in range(1, count) if given[i] < most]
        pool, remaining = sum([loads[i] for i in candidates]), spare
        for i in candidates:
            addition = min(most - given[i], max(1, remaining * loads[i] // pool), spare)
            given[i] = given[i] + addition
            spare = spare - addition
    return np.array(given)


def gaussian(key, shape, width, most, cuts=(), held_as=jnp.bfloat16):
    array = width * jax.random.normal(key, shape, jnp.float32)
    if cuts:
        array = array * steps_of(key, shape, cuts, -0.22, 0.18)
    return jnp.clip(array, -most, most).astype(held_as)


def setup_inputs(seed: int = 0) -> dict:
    key_of = jax.random.split(jax.random.key(seed), 14)
    attention_out = gaussian(key_of[0], (ROWS, D), 1.0, 6.0, ((0, 8),))
    residual = gaussian(key_of[1], (ROWS, D), 1.0, 6.0, ((0, 8), (1, 4)))
    w_out = gaussian(key_of[2], (D, D), D ** -0.5, 0.09375, ((0, 8), (1, 4)))
    router_w = gaussian(key_of[3], (D, EXPERTS), D ** -0.5, 0.09375, ((0, 4),), jnp.float32)
    norm_gain = jnp.clip(1.0 + 0.1 * jax.random.normal(key_of[4], (D,), jnp.float32), 0.5, 1.5)
    page_pool = gaussian(key_of[5], (POOL * N_REQ, PAGE, KVS), 1.0, 6.0, ((0, 8), (2, 4)))
    page_table = draw_page_table(jax.random.fold_in(key_of[13], 71), 0)
    cache_len = place_ends(jax.random.randint(key_of[7], (ROWS,), 1, PPR * PAGE + 1), jax.random.fold_in(key_of[7], 1), 1, PPR * PAGE).astype(jnp.int32)
    came_from = draw_came_from(jax.random.fold_in(key_of[13], 71), 0)
    routes_keys = jax.random.split(jax.random.fold_in(key_of[9], 1), ROWS // ROW_REQ)
    routes_turns = jax.random.permutation(jax.random.fold_in(key_of[9], 3), ROWS // ROW_REQ)
    routes = jax.vmap(lambda own, number: shared_out(jax.random.fold_in(key_of[9], 2), own, number, ROW_REQ, EXPERTS, 2, 2 * CAP, 2))(routes_keys, routes_turns).reshape((ROWS, TOP))
    w_gate = draw_w_gate(jax.random.fold_in(key_of[13], 71), 0)
    w_up = draw_w_up(jax.random.fold_in(key_of[13], 71), 0)
    w_down = draw_w_down(jax.random.fold_in(key_of[13], 71), 0)
    return dict(attention_out=attention_out, residual=residual, w_out=w_out, router_w=router_w, norm_gain=norm_gain, page_pool=page_pool, page_table=page_table, cache_len=cache_len, came_from=came_from, routes=routes, w_gate=w_gate, w_up=w_up, w_down=w_down)


EPSILON = 1e-05

def reference(attention_out, residual, w_out, router_w, norm_gain, page_pool, page_table, cache_len, came_from, routes, w_gate, w_up, w_down):
    experts = N_REQ // 2
    attn_new = jnp.take(attention_out, came_from, axis=0)
    resid_new = jnp.take(residual, came_from, axis=0)
    source_group = came_from // ROW_REQ
    pool_slots = source_group[:, None] * POOL + jnp.take(page_table, came_from, axis=0)
    gathered = jnp.take(page_pool, pool_slots.reshape(-1), axis=0).reshape(ROWS, PPR, PAGE, KVS)
    position = jnp.arange(PPR, dtype=jnp.int32)[:, None] * PAGE + jnp.arange(PAGE, dtype=jnp.int32)[None, :]
    kept_mask = position[None, :, :] < jnp.take(cache_len, came_from)[:, None, None]
    new_pages = jnp.where(kept_mask[..., None], gathered, jnp.zeros((), gathered.dtype))
    projected = jnp.dot(attn_new, w_out, preferred_element_type=jnp.float32)
    hidden = resid_new.astype(jnp.float32) + projected
    mean_sq = lax.optimization_barrier(jnp.sum(hidden * hidden, axis=1)) / D
    normed = hidden * norm_gain[None, :] * lax.rsqrt(mean_sq + EPSILON)[:, None]
    logits = jnp.dot(normed, router_w, precision=lax.Precision.HIGHEST)
    chosen = jnp.take_along_axis(logits, routes, axis=1)
    gate_pair = jax.nn.sigmoid(chosen - chosen[:, ::-1])
    normed_rows = normed.astype(jnp.bfloat16)
    grouped = routes.reshape(N_REQ, ROW_REQ * TOP)
    expert_hot = (grouped[:, :, None] == jnp.arange(experts, dtype=jnp.int32)[None, None, :]).astype(jnp.int32)
    expert_rank = lax.optimization_barrier(jnp.sum((jnp.cumsum(expert_hot, axis=1) - expert_hot) * expert_hot, axis=2)).reshape(-1)
    target_dev = routes.reshape(-1) + experts * (expert_rank % 2)
    count_all = ROWS * TOP
    capacity_all = N_REQ * CAP
    assign_ids = jnp.arange(count_all, dtype=jnp.int32)

    def one_target(device):
        ordered = jnp.sort(jnp.where(target_dev == device, assign_ids, count_all))[:capacity_all]
        rows_in = jnp.take(normed_rows, jnp.minimum(ordered, count_all - 1) // TOP, axis=0)
        gate_h = jnp.dot(rows_in, w_gate[device], preferred_element_type=jnp.float32)
        up_h = jnp.dot(rows_in, w_up[device], preferred_element_type=jnp.float32)
        active = (jax.nn.silu(gate_h) * up_h).astype(jnp.bfloat16)
        down_all = w_down[device]
        summed = jnp.zeros((capacity_all, D), jnp.float32)
        for block_index in range(N_EXP):
            block_out = jnp.dot(active[:, block_index * SLICE:(block_index + 1) * SLICE], down_all[block_index * SLICE:(block_index + 1) * SLICE], preferred_element_type=jnp.float32)
            summed = summed + lax.optimization_barrier(block_out.astype(jnp.bfloat16)).astype(jnp.float32)
        return (ordered, summed)
    ordered_all, outputs = lax.map(one_target, jnp.arange(2 * experts, dtype=jnp.int32))
    expert_out = jnp.zeros((count_all, D), jnp.float32).at[ordered_all.reshape(-1)].set(outputs.reshape(-1, D), mode='drop')
    expert_out = expert_out.reshape(ROWS, TOP, D)
    mixed = hidden + gate_pair[:, 0:1] * expert_out[:, 0] + gate_pair[:, 1:2] * expert_out[:, 1]
    return (mixed, new_pages)
```

```python
import jax
import jax.numpy as jnp
from jax import lax
from jax.experimental import pallas as pl
from jax.experimental.pallas import tpu as pltpu
from jax.sharding import PartitionSpec as P

D = 4096
SLOTS = 64
MIG = 4
EPSILON = 1e-05
BF = jnp.bfloat16
F32 = jnp.float32
I32 = jnp.int32


def swap(x, axis, s):
    n = lax.axis_size(axis)
    return lax.ppermute(x, axis, [(i, i ^ s) for i in range(n)])


def hot(index, count):
    return (index[..., None] == jnp.arange(count, dtype=I32)).astype(BF)


def pick(selector, rows):
    return jnp.dot(selector, rows, preferred_element_type=F32)


def page_kernel(pool, moved, rows, slot, table, length, out):
    count, pages, page_len, width = out.shape
    token = lax.broadcasted_iota(I32, (page_len, width), 0)

    @pl.loop(0, count)
    def _(j):
        at = slot[j]

        @pl.when(at >= 0)
        def _():
            for p in range(pages):
                out[j, p] = moved[at, p]

        @pl.when(at < 0)
        def _():
            i = rows[j]
            for p in range(pages):
                page = pool[table[i * pages + p]].astype(F32)
                out[j, p] = jnp.where(token + p * page_len < length[i], page, 0.0).astype(out.dtype)


def take_pages(pool, moved, rows, slot, table, length):
    pages = table.shape[0] // length.shape[0]
    count = rows.shape[0]
    return pl.pallas_call(
        page_kernel,
        out_shape=jax.ShapeDtypeStruct((count, pages) + pool.shape[1:], pool.dtype),
        in_specs=[pl.BlockSpec(memory_space=pltpu.VMEM)] * 2
        + [pl.BlockSpec(memory_space=pltpu.SMEM)] * 4,
        out_specs=pl.BlockSpec(memory_space=pltpu.VMEM),
        compiler_params=pltpu.CompilerParams(vmem_limit_bytes=16 * 2**20),
        cost_estimate=pl.CostEstimate(flops=0, bytes_accessed=6 * 2**20, transcendentals=0),
    )(pool, moved, rows, slot, table, length)


def body(
    attention_out,
    residual,
    w_out,
    router_w,
    norm_gain,
    page_pool,
    page_table,
    cache_len,
    came_from,
    routes,
    w_gate,
    w_up,
    w_down,
):
    n = lax.axis_size("req")
    ne = lax.axis_size("exp")
    me = lax.axis_index("req")
    ze = lax.axis_index("exp")
    half = n // 2
    q, k = me // 2, me % 2
    rows = attention_out.shape[0]
    feats = residual.shape[1]
    kblock = D // half
    experts = n // 2

    def column_block(x, s):
        return lax.dynamic_slice_in_dim(x, (q ^ s) * kblock, kblock, axis=1)

    attn_blocks = [column_block(attention_out, s) for s in range(half)]
    attn_blocks = attn_blocks[:1] + [swap(attn_blocks[s], "req", 2 * s) for s in range(1, half)]
    w_other = swap(w_out, "req", 1)
    w_pair = jnp.where(
        k == 0,
        jnp.concatenate([w_out, w_other], axis=0),
        jnp.concatenate([w_other, w_out], axis=0),
    )

    local = jnp.arange(rows, dtype=I32)
    in_new = came_from[None, :] == (me * rows + local)[:, None]
    new_ids = jnp.arange(came_from.shape[0], dtype=I32)
    dest = jnp.sum(jnp.where(in_new, new_ids[None, :], 0), axis=1) // rows
    dest_rank = jnp.sum((dest[:, None] == dest[None, :]) & (local[None, :] < local[:, None]), axis=1)
    dest_rel, dest_par = (dest // 2) ^ q, dest % 2
    send_slot = jnp.where(
        dest_par != k,
        dest_rel * MIG + dest_rank,
        jnp.where(dest_rel != 0, (half + dest_rel - 1) * MIG + dest_rank, -1),
    )
    n_pair, n_send = half * MIG, (2 * half - 1) * MIG
    send_hot = (jnp.arange(n_send, dtype=I32)[:, None] == send_slot[None, :])
    send_row = jnp.sum(jnp.where(send_hot, local[None, :], 0), axis=1)
    send_pick = send_hot.astype(BF)

    source = jnp.stack(
        [lax.dynamic_slice_in_dim(came_from, (2 * (q ^ t) + k) * rows, rows) for t in range(half)]
    )
    src_group, src_local = source // rows, source % rows
    src_rank = jnp.sum(
        (src_group[:, :, None] == src_group[:, None, :]) & (source[:, None, :] < source[:, :, None]),
        axis=2,
    )
    src_rel, src_par = (src_group // 2) ^ q, src_group % 2
    t_ids = jnp.arange(half, dtype=I32)[:, None]
    attn_at = jnp.where(
        src_par == k,
        src_rel * rows + src_local,
        half * rows + src_rel * n_pair + (t_ids ^ src_rel) * MIG + src_rank,
    ).reshape(-1)
    own_stays = src_group[0] == me
    own_slot = src_rel[0] * 2 * MIG + jnp.where(src_par[0] == k, 0, MIG) + src_rank[0]
    own_at = jnp.where(own_stays, src_local[0], rows + own_slot)

    pair_attn = swap(pick(send_pick[:n_pair], attention_out).astype(BF), "req", 1)
    late_blocks = [column_block(pair_attn, s) for s in range(half)]
    late_blocks = late_blocks[:1] + [swap(late_blocks[s], "req", 2 * s) for s in range(1, half)]

    def relay(moving):
        pair = swap(moving[:n_pair], "req", 1)
        blocks = []
        for s in range(half):
            first = moving[n_pair + (s - 1) * MIG : n_pair + s * MIG] if s else pair[:MIG]
            both = jnp.concatenate([first, pair[s * MIG : (s + 1) * MIG]], axis=0)
            blocks.append(swap(both, "req", 2 * s) if s else both)
        return jnp.concatenate(blocks, axis=0)

    moved_resid = relay(pick(send_pick, residual).astype(BF))
    resid_new = pick(
        hot(own_at, rows + 2 * MIG * half), jnp.concatenate([residual, moved_resid], axis=0)
    )

    attn_new = pick(
        hot(attn_at, half * (rows + n_pair)), jnp.concatenate(attn_blocks + late_blocks, axis=0)
    ).astype(BF)
    part = jnp.dot(attn_new, w_pair, preferred_element_type=F32).reshape(half, rows, feats)
    hidden = resid_new + part[0]
    for s in range(1, half):
        hidden = hidden + swap(part[s].astype(BF), "req", 2 * s).astype(F32)

    scaled = hidden * norm_gain[None, :]
    scaled_rows = scaled.astype(BF)
    stats = jnp.concatenate(
        [
            jnp.sum(hidden * hidden, axis=1, keepdims=True),
            jnp.dot(scaled, router_w, precision=lax.Precision.HIGHEST),
        ],
        axis=1,
    )
    stats_all = stats
    for s in range(1, ne):
        stats_all = stats_all + swap(stats, "exp", s)
    full = jnp.zeros((rows, D), BF)
    for s in range(ne):
        block = swap(scaled_rows, "exp", s) if s else scaled_rows
        full = lax.dynamic_update_slice_in_dim(full, block, (ze ^ s) * feats, axis=1)
    inverse = lax.rsqrt(stats_all[:, 0] / D + EPSILON)
    logits = stats_all[:, 1:] * inverse[:, None]
    expert_ids = jnp.arange(experts, dtype=I32)
    chosen = jnp.sum(
        jnp.where(routes[:, :, None] == expert_ids[None, None, :], logits[:, None, :], 0.0), axis=2
    )
    gates = jax.nn.sigmoid(chosen - chosen[:, ::-1])

    names = routes[:, :, None] == expert_ids[None, None, :]
    named = jnp.any(names, axis=1)
    before = jnp.sum(
        jnp.where((local[None, :] < local[:, None])[:, :, None], named[None, :, :], False), axis=1
    )
    rank = jnp.sum(jnp.where(names, before[:, None, :], 0), axis=2)
    slot_of = ((routes ^ (me % experts)) * SLOTS + rank).astype(I32)
    slot_ids = jnp.arange(experts * SLOTS, dtype=I32)
    slot_hot = slot_ids[:, None, None] == slot_of[None, :, :]
    slot_pick = jnp.any(slot_hot, axis=2)
    slot_scale = jnp.sum(jnp.where(slot_pick, inverse[None, :], 0.0), axis=1)
    outgoing = (pick(slot_pick.astype(BF), full) * slot_scale[:, None]).astype(BF)
    outgoing = outgoing.reshape(experts, SLOTS, D)
    arrived = jnp.concatenate(
        [swap(outgoing[s], "req", s) if s else outgoing[s] for s in range(experts)], axis=0
    )

    gate_h = jnp.dot(arrived, w_gate[0], preferred_element_type=F32)
    up_h = jnp.dot(arrived, w_up[0], preferred_element_type=F32)
    active = (jax.nn.silu(gate_h) * up_h).astype(BF)
    down = jnp.dot(active, w_down[0], preferred_element_type=F32).astype(BF)
    down = down.reshape(experts, SLOTS, D)
    back = jnp.concatenate(
        [swap(down[s], "req", s) if s else down[s] for s in range(experts)], axis=0
    )
    gate_slots = jnp.sum(
        jnp.where(slot_of[:, :, None] == slot_ids[None, None, :], gates[:, :, None], 0.0), axis=1
    )
    gate_high = gate_slots.astype(BF)
    gate_low = (gate_slots - gate_high.astype(F32)).astype(BF)
    weighted = pick(gate_high, back) + pick(gate_low, back)
    mixed = hidden + lax.dynamic_slice_in_dim(weighted, ze * feats, feats, axis=1)
    weighted = weighted.astype(BF)
    for s in range(1, ne):
        block = lax.dynamic_slice_in_dim(weighted, (ze ^ s) * feats, feats, axis=1)
        mixed = mixed + swap(block, "exp", s).astype(F32)

    table = page_table.reshape(-1)
    none = jnp.full((n_send,), -1, I32)
    moving_pages = take_pages(page_pool, page_pool[:2].reshape((1, 2) + page_pool.shape[1:]), send_row, none, table, cache_len)
    moved_pages = relay(moving_pages)
    new_pages = take_pages(
        page_pool,
        moved_pages,
        jnp.where(own_stays, src_local[0], 0),
        jnp.where(own_stays, -1, own_slot),
        table,
        cache_len,
    )
    return (mixed, new_pages)


def solution(mesh):
    in_specs = (
        P("req", None),
        P("req", "exp"),
        P("req", "exp"),
        P("exp", None),
        P("exp"),
        P("req", None, "exp"),
        P("req", None),
        P("req"),
        P(),
        P("req", None),
        P("req", None, "exp"),
        P("req", None, "exp"),
        P("req", "exp", None),
    )
    out_specs = (P("req", "exp"), P("req", None, None, "exp"))
    return jax.shard_map(body, mesh=mesh, in_specs=in_specs, out_specs=out_specs, check_vma=False)
```

```python
import functools

import jax
import jax.numpy as jnp
from jax import lax
from jax.experimental import pallas as pl
from jax.experimental.pallas import tpu as pltpu
from jax.sharding import PartitionSpec as P

D = 4096
SLOTS = 64
MIG = 4
EPSILON = 1e-05
BF = jnp.bfloat16
F32 = jnp.float32
I32 = jnp.int32
MIB = 2**20
VMEM = pl.BlockSpec(memory_space=pltpu.VMEM)
SMEM = pl.BlockSpec(memory_space=pltpu.SMEM)


def swap(x, axis, s):
    n = lax.axis_size(axis)
    return lax.ppermute(x, axis, [(i, i ^ s) for i in range(n)])


def hot(index, count):
    return (index[..., None] == jnp.arange(count, dtype=I32)).astype(BF)


def pick(selector, rows):
    return jnp.dot(selector, rows, preferred_element_type=F32)


def lanes(start, width):
    return pl.ds(pl.multiple_of(start, 128), width)


def local_call(kernel, in_specs, args, outs, scratch=(), vmem=24, flops=0, moved=0):
    return pl.pallas_call(
        kernel,
        out_shape=outs,
        in_specs=in_specs,
        out_specs=[VMEM] * len(outs),
        scratch_shapes=list(scratch),
        compiler_params=pltpu.CompilerParams(vmem_limit_bytes=vmem * MIB),
        cost_estimate=pl.CostEstimate(flops=flops, bytes_accessed=moved, transcendentals=0),
    )(*args)


def shape(dims, dtype):
    return jax.ShapeDtypeStruct(dims, dtype)


def page_kernel(pool, moved, rows, slot, table, length, out):
    count, pages, page_len, width = out.shape
    token = lax.broadcasted_iota(I32, (page_len, width), 0)

    @pl.loop(0, count)
    def _(j):
        at = slot[j]

        @pl.when(at >= 0)
        def _():
            for p in range(pages):
                out[j, p] = moved[at, p]

        @pl.when(at < 0)
        def _():
            i = rows[j]
            for p in range(pages):
                page = pool[table[i * pages + p]].astype(F32)
                out[j, p] = jnp.where(token + p * page_len < length[i], page, 0.0).astype(out.dtype)


def take_pages(pool, moved, rows, slot, table, length):
    pages = table.shape[0] // length.shape[0]
    outs = [shape((rows.shape[0], pages) + pool.shape[1:], pool.dtype)]
    args = (pool, moved, rows, slot, table, length)
    return local_call(page_kernel, [VMEM] * 2 + [SMEM] * 4, args, outs, moved=5 * MIB)[0]


def project_kernel(half, *refs):
    odd, selector, own, other = refs[:4]
    blocks = refs[4 : 4 + 2 * half]
    outs = refs[4 + 2 * half : 4 + 3 * half]
    buf, left = refs[4 + 3 * half :]
    at = 0
    for block in blocks:
        buf[at : at + block.shape[0]] = block[...]
        at += block.shape[0]
    picked = pick(selector[...], buf[...]).astype(BF)
    first, second = picked[:, : own.shape[0]], picked[:, own.shape[0] :]

    @pl.when(odd[0] == 0)
    def _():
        left[...] = pick(first, own[...]) + pick(second, other[...])

    @pl.when(odd[0] == 1)
    def _():
        left[...] = pick(first, other[...]) + pick(second, own[...])

    rows = outs[0].shape[0]
    for t, out in enumerate(outs):
        out[...] = left[t * rows : (t + 1) * rows].astype(out.dtype)


def norm_kernel(half, experts, wide, *refs):
    resid, gain, selector = refs[:3]
    parts = refs[3 : 3 + half]
    hidden_out, early = refs[3 + half : 5 + half]
    late = refs[5 + half :]
    hidden = resid[...]
    for part in parts:
        hidden = hidden + part[...].astype(F32)
    hidden_out[...] = hidden
    scaled = (hidden * gain[...]).astype(BF)
    early[...] = scaled[:, :wide]
    chosen = pick(selector[...], scaled[:, wide:]).astype(BF)
    for s in range(experts):
        late[s][...] = chosen[s * SLOTS : (s + 1) * SLOTS]


def dispatch_kernel(ne, experts, *refs):
    place, selector = refs[:2]
    blocks, outs = refs[2 : 2 + ne], refs[2 + ne :]
    wide = blocks[0].shape[1]
    for s in range(ne):
        chosen = pick(selector[...], blocks[s][...]).astype(BF)
        columns = lanes((place[0] ^ s) * wide, wide)
        for t in range(experts):
            outs[t][:, columns] = chosen[t * SLOTS : (t + 1) * SLOTS]


def gate_up_kernel(ne, experts, *refs):
    place, inverse_gain = refs[:2]
    early, late = refs[2 : 2 + experts], refs[2 + experts : 2 + experts + ne]
    gate, up, out, rows, scale = refs[2 + experts + ne :]
    wide, rest = early[0].shape[1] // ne, late[0].shape[1]
    feats = wide + rest

    @pl.when(pl.program_id(0) == 0)
    def _():
        for t in range(experts):
            for e in range(ne):
                rows[t * SLOTS : (t + 1) * SLOTS, e * feats : e * feats + wide] = early[t][
                    :, e * wide : (e + 1) * wide
                ]
        for s in range(ne):
            rows[:, lanes((place[0] ^ s) * feats + wide, rest)] = late[s][...]
        total = jnp.zeros((rows.shape[0], 1), F32)
        step = min(1024, rows.shape[1])
        for c in range(0, rows.shape[1], step):
            plain = rows[:, c : c + step].astype(F32) * inverse_gain[:, c : c + step]
            total = total + jnp.sum(plain * plain, axis=1, keepdims=True)
        scale[...] = lax.rsqrt(total / D + EPSILON)

    gate_h = pick(rows[...], gate[0]) * scale[...]
    up_h = pick(rows[...], up[0]) * scale[...]
    out[...] = (gate_h / (1.0 + jnp.exp(-gate_h)) * up_h).astype(out.dtype)


def gate_up(place, inverse_gain, early, late, w_gate, w_up, ne):
    hidden = w_gate.shape[2]
    slots = late[0].shape[0]
    tile = 256 if hidden % 256 == 0 else 128
    whole = lambda a: pl.BlockSpec(a.shape, lambda f: (0,) * a.ndim)
    weight = pl.BlockSpec((1, D, tile), lambda f: (0, 0, f))
    return pl.pallas_call(
        functools.partial(gate_up_kernel, ne, len(early)),
        grid=(hidden // tile,),
        out_shape=shape((slots, hidden), BF),
        in_specs=[SMEM] + [whole(a) for a in (inverse_gain, *early, *late)] + [weight] * 2,
        out_specs=pl.BlockSpec((slots, tile), lambda f: (0, f)),
        scratch_shapes=[pltpu.VMEM((slots, D), BF), pltpu.VMEM((slots, 1), F32)],
        compiler_params=pltpu.CompilerParams(vmem_limit_bytes=40 * MIB),
        cost_estimate=pl.CostEstimate(
            flops=4 * slots * D * hidden, bytes_accessed=4 * D * hidden, transcendentals=0
        ),
    )(place, inverse_gain, *early, *late, w_gate, w_up)


def down_late_kernel(ne, place, active, weight, *outs):
    value = pick(active[...], weight[0]).astype(BF)
    for s in range(ne):

        @pl.when(pl.program_id(0) == s)
        def _(s=s):
            outs[s][...] = value


def down_early_kernel(ne, place, active, weight, *outs):
    value = pick(active[...], weight[0]).astype(BF)
    wide = weight.shape[2]
    for t, out in enumerate(outs):
        out[:, lanes(pl.program_id(0) * wide, wide)] = value[t * SLOTS : (t + 1) * SLOTS]


def down_call(kernel, place, active, w_down, width, column, out_shapes, ne):
    slots, hidden = active.shape
    return pl.pallas_call(
        functools.partial(kernel, ne),
        grid_spec=pltpu.PrefetchScalarGridSpec(
            num_scalar_prefetch=1,
            grid=(ne,),
            in_specs=[
                pl.BlockSpec((slots, hidden), lambda g, place: (0, 0)),
                pl.BlockSpec((1, hidden, width), lambda g, place: (0, 0, column(g, place))),
            ],
            out_specs=[pl.BlockSpec(o.shape, lambda g, place: (0, 0)) for o in out_shapes],
        ),
        out_shape=out_shapes,
        compiler_params=pltpu.CompilerParams(vmem_limit_bytes=32 * MIB),
        cost_estimate=pl.CostEstimate(
            flops=2 * slots * hidden * width * ne,
            bytes_accessed=2 * hidden * width * ne,
            transcendentals=0,
        ),
    )(place, active, w_down)


def weigh_kernel(ne, experts, *refs):
    place, high, low = refs[:3]
    blocks, outs, buf, total = refs[3 : 3 + experts], refs[3 + experts : 3 + experts + ne], *refs[3 + experts + ne :]
    for t in range(experts):
        buf[t * SLOTS : (t + 1) * SLOTS] = blocks[t][...]
    total[...] = pick(high[...], buf[...]) + pick(low[...], buf[...])
    wide = outs[0].shape[1]
    for s in range(ne):
        outs[s][...] = total[:, lanes((place[0] ^ s) * wide, wide)].astype(outs[s].dtype)


def finish_kernel(ne, experts, wide, *refs):
    high, low, hidden = refs[:3]
    early, late = refs[3 : 3 + ne], refs[3 + ne : 3 + ne + experts]
    out, buf = refs[3 + ne + experts :]
    first = hidden[:, :wide]
    for block in early:
        first = first + block[...].astype(F32)
    out[:, :wide] = first
    for t in range(experts):
        buf[t * SLOTS : (t + 1) * SLOTS] = late[t][...]
    out[:, wide:] = hidden[:, wide:] + pick(high[...], buf[...]) + pick(low[...], buf[...])


def body(
    attention_out,
    residual,
    w_out,
    router_w,
    norm_gain,
    page_pool,
    page_table,
    cache_len,
    came_from,
    routes,
    w_gate,
    w_up,
    w_down,
):
    n = lax.axis_size("req")
    ne = lax.axis_size("exp")
    me = lax.axis_index("req")
    ze = lax.axis_index("exp")
    half = n // 2
    q, k = me // 2, me % 2
    rows = attention_out.shape[0]
    feats = residual.shape[1]
    kblock = D // half
    experts = n // 2
    rest = feats // 2
    wide = feats - rest
    place = ze.reshape(1).astype(I32)

    def column_block(x, s):
        return lax.dynamic_slice_in_dim(x, (q ^ s) * kblock, kblock, axis=1)

    attn_blocks = [column_block(attention_out, s) for s in range(half)]
    attn_blocks = list(lax.optimization_barrier(tuple(attn_blocks)))
    came_from, _ = lax.optimization_barrier((came_from, attn_blocks[0]))
    attn_blocks = attn_blocks[:1] + [swap(attn_blocks[s], "req", 2 * s) for s in range(1, half)]
    w_other = swap(w_out, "req", 1)
    gain_all = lax.all_gather(norm_gain, "exp", tiled=True)

    local = jnp.arange(rows, dtype=I32)
    in_new = came_from[None, :] == (me * rows + local)[:, None]
    new_ids = jnp.arange(came_from.shape[0], dtype=I32)
    dest = jnp.sum(jnp.where(in_new, new_ids[None, :], 0), axis=1) // rows
    dest_rank = jnp.sum((dest[:, None] == dest[None, :]) & (local[None, :] < local[:, None]), axis=1)
    dest_rel, dest_par = (dest // 2) ^ q, dest % 2
    send_slot = jnp.where(
        dest_par != k,
        dest_rel * MIG + dest_rank,
        jnp.where(dest_rel != 0, (half + dest_rel - 1) * MIG + dest_rank, -1),
    )
    n_pair, n_send = half * MIG, (2 * half - 1) * MIG
    send_hot = (jnp.arange(n_send, dtype=I32)[:, None] == send_slot[None, :])
    send_row = jnp.sum(jnp.where(send_hot, local[None, :], 0), axis=1)
    send_pick = send_hot.astype(BF)

    source = jnp.stack(
        [lax.dynamic_slice_in_dim(came_from, (2 * (q ^ t) + k) * rows, rows) for t in range(half)]
    )
    src_group, src_local = source // rows, source % rows
    src_rank = jnp.sum(
        (src_group[:, :, None] == src_group[:, None, :]) & (source[:, None, :] < source[:, :, None]),
        axis=2,
    )
    src_rel, src_par = (src_group // 2) ^ q, src_group % 2
    t_ids = jnp.arange(half, dtype=I32)[:, None]
    attn_at = jnp.where(
        src_par == k,
        src_rel * rows + src_local,
        half * rows + src_rel * n_pair + (t_ids ^ src_rel) * MIG + src_rank,
    ).reshape(-1)
    own_stays = src_group[0] == me
    own_slot = src_rel[0] * 2 * MIG + jnp.where(src_par[0] == k, 0, MIG) + src_rank[0]
    own_at = jnp.where(own_stays, src_local[0], rows + own_slot)

    pair_attn = swap(pick(send_pick[:n_pair], attention_out).astype(BF), "req", 1)
    late_blocks = [column_block(pair_attn, s) for s in range(half)]
    late_blocks = late_blocks[:1] + [swap(late_blocks[s], "req", 2 * s) for s in range(1, half)]

    def relay(moving):
        pair = swap(moving[:n_pair], "req", 1)
        blocks = []
        for s in range(half):
            first = moving[n_pair + (s - 1) * MIG : n_pair + s * MIG] if s else pair[:MIG]
            both = jnp.concatenate([first, pair[s * MIG : (s + 1) * MIG]], axis=0)
            blocks.append(swap(both, "req", 2 * s) if s else both)
        return jnp.concatenate(blocks, axis=0)

    moved_resid = relay(pick(send_pick, residual).astype(BF))
    resid_new = pick(
        hot(own_at, rows + 2 * MIG * half), jnp.concatenate([residual, moved_resid], axis=0)
    )

    expert_ids = jnp.arange(experts, dtype=I32)
    names = routes[:, :, None] == expert_ids[None, None, :]
    named = jnp.any(names, axis=1)
    before = jnp.sum(
        jnp.where((local[None, :] < local[:, None])[:, :, None], named[None, :, :], False), axis=1
    )
    rank = jnp.sum(jnp.where(names, before[:, None, :], 0), axis=2)
    slot_of = ((routes ^ (me % experts)) * SLOTS + rank).astype(I32)
    slot_ids = jnp.arange(experts * SLOTS, dtype=I32)
    slot_pick = jnp.any(slot_ids[:, None, None] == slot_of[None, :, :], axis=2).astype(BF)

    total_rows = half * (rows + n_pair)
    selector = hot(attn_at, total_rows)
    parts = local_call(
        functools.partial(project_kernel, half),
        [SMEM] + [VMEM] * (3 + 2 * half),
        (k.reshape(1).astype(I32), selector, w_out, w_other, *attn_blocks, *late_blocks),
        [shape((rows, feats), F32)] + [shape((rows, feats), BF)] * (half - 1),
        [pltpu.VMEM((total_rows, kblock), BF), pltpu.VMEM((half * rows, feats), F32)],
        flops=2 * half * rows * (total_rows + feats) * kblock,
        moved=6 * MIB,
    )
    parts = [parts[0]] + [swap(parts[s], "req", 2 * s) for s in range(1, half)]

    normed = local_call(
        functools.partial(norm_kernel, half, experts, wide),
        [VMEM] * (3 + half),
        (resid_new, norm_gain[None, :], slot_pick, *parts),
        [shape((rows, feats), F32), shape((rows, wide), BF)] + [shape((SLOTS, rest), BF)] * experts,
        flops=2 * experts * SLOTS * rows * rest,
        moved=3 * MIB,
    )
    hidden, early = normed[:2]
    early_blocks = [early] + [swap(early, "exp", s) for s in range(1, ne)]
    late = [normed[2 + s] if s == 0 else swap(normed[2 + s], "req", s) for s in range(experts)]
    late = jnp.concatenate(late, axis=0)
    late_rows = [late] + [swap(late, "exp", s) for s in range(1, ne)]
    outgoing = local_call(
        functools.partial(dispatch_kernel, ne, experts),
        [SMEM] + [VMEM] * (1 + ne),
        (place, slot_pick, *early_blocks),
        [shape((SLOTS, ne * wide), BF)] * experts,
        flops=2 * experts * SLOTS * rows * ne * wide,
        moved=3 * MIB,
    )
    early_rows = [swap(outgoing[s], "req", s) if s else outgoing[s] for s in range(experts)]

    stats = jnp.concatenate(
        [
            jnp.sum(hidden * hidden, axis=1, keepdims=True),
            jnp.dot(hidden * norm_gain[None, :], router_w, precision=lax.Precision.HIGHEST),
        ],
        axis=1,
    )
    stats = jnp.sum(lax.all_gather(stats, "exp"), axis=0)
    logits = stats[:, 1:] * lax.rsqrt(stats[:, :1] / D + EPSILON)
    chosen = jnp.sum(jnp.where(names, logits[:, None, :], 0.0), axis=2)
    gates = jax.nn.sigmoid(chosen - chosen[:, ::-1])
    gate_slots = jnp.sum(
        jnp.where(slot_of[:, :, None] == slot_ids[None, None, :], gates[:, :, None], 0.0), axis=1
    )
    gate_high = gate_slots.astype(BF)
    gate_low = (gate_slots - gate_high.astype(F32)).astype(BF)

    table = page_table.reshape(-1)
    none = jnp.full((n_send,), -1, I32)
    no_rows = page_pool[:2].reshape((1, 2) + page_pool.shape[1:])
    moving_pages = take_pages(page_pool, no_rows, send_row, none, table, cache_len)
    moving_pages, _ = lax.optimization_barrier((moving_pages, outgoing[0]))
    moved_pages = relay(moving_pages)

    active = gate_up(place, 1.0 / gain_all[None, :], early_rows, late_rows, w_gate, w_up, ne)
    per_owner = feats // rest
    down_late = down_call(
        down_late_kernel,
        place,
        active,
        w_down,
        rest,
        lambda g, place: (g ^ place[0]) * per_owner + per_owner - 1,
        [shape((experts * SLOTS, rest), BF)] * ne,
        ne,
    )
    late_sum = down_late[0].astype(F32)
    for s in range(1, ne):
        late_sum = late_sum + swap(down_late[s], "exp", s).astype(F32)
    late_sum = late_sum.astype(BF).reshape(experts, SLOTS, rest)
    late_back = [swap(late_sum[s], "req", s) if s else late_sum[s] for s in range(experts)]
    down_early = down_call(
        down_early_kernel,
        place,
        active,
        w_down,
        wide,
        lambda g, place: g * per_owner,
        [shape((SLOTS, ne * wide), BF)] * experts,
        ne,
    )
    early_back = [swap(down_early[s], "req", s) if s else down_early[s] for s in range(experts)]
    weighted = local_call(
        functools.partial(weigh_kernel, ne, experts),
        [SMEM] + [VMEM] * (2 + experts),
        (place, gate_high, gate_low, *early_back),
        [shape((rows, wide), F32)] + [shape((rows, wide), BF)] * (ne - 1),
        [pltpu.VMEM((experts * SLOTS, ne * wide), BF), pltpu.VMEM((rows, ne * wide), F32)],
        flops=4 * rows * experts * SLOTS * ne * wide,
        moved=3 * MIB,
    )
    early_parts = [weighted[0]] + [swap(weighted[s], "exp", s) for s in range(1, ne)]
    mixed = local_call(
        functools.partial(finish_kernel, ne, experts, wide),
        [VMEM] * (3 + ne + experts),
        (gate_high, gate_low, hidden, *early_parts, *late_back),
        [shape((rows, feats), F32)],
        [pltpu.VMEM((experts * SLOTS, rest), BF)],
        flops=4 * rows * experts * SLOTS * rest,
        moved=2 * MIB,
    )[0]

    new_pages = take_pages(
        page_pool,
        moved_pages,
        jnp.where(own_stays, src_local[0], 0),
        jnp.where(own_stays, -1, own_slot),
        table,
        cache_len,
    )
    return (mixed, new_pages)


def solution(mesh):
    in_specs = (
        P("req", None),
        P("req", "exp"),
        P("req", "exp"),
        P("exp", None),
        P("exp"),
        P("req", None, "exp"),
        P("req", None),
        P("req"),
        P(),
        P("req", None),
        P("req", None, "exp"),
        P("req", None, "exp"),
        P("req", "exp", None),
    )
    out_specs = (P("req", "exp"), P("req", None, None, "exp"))
    return jax.shard_map(body, mesh=mesh, in_specs=in_specs, out_specs=out_specs, check_vma=False)
```

```python
import functools

import jax
import jax.numpy as jnp
from jax import lax
from jax.experimental import pallas as pl
from jax.experimental.pallas import tpu as pltpu
from jax.sharding import PartitionSpec as P

D = 4096
SLOTS = 64
MIG = 4
EPSILON = 1e-05
BF = jnp.bfloat16
F32 = jnp.float32
I32 = jnp.int32
MIB = 2**20
VMEM = pl.BlockSpec(memory_space=pltpu.VMEM)
SMEM = pl.BlockSpec(memory_space=pltpu.SMEM)
HBM = pl.BlockSpec(memory_space=pltpu.HBM)


def swap(x, axis, s):
    n = lax.axis_size(axis)
    return lax.ppermute(x, axis, [(i, i ^ s) for i in range(n)])


def hot(index, count):
    return (index[..., None] == jnp.arange(count, dtype=I32)).astype(BF)


def pick(selector, rows):
    return jnp.dot(selector, rows, preferred_element_type=F32)


def lanes(start, width):
    return pl.ds(pl.multiple_of(start, 128), width)


def local_call(kernel, in_specs, args, outs, scratch=(), vmem=16, flops=0, moved=0):
    return pl.pallas_call(
        kernel,
        out_shape=outs,
        in_specs=in_specs,
        out_specs=[VMEM] * len(outs),
        scratch_shapes=list(scratch),
        compiler_params=pltpu.CompilerParams(vmem_limit_bytes=vmem * MIB),
        cost_estimate=pl.CostEstimate(flops=flops, bytes_accessed=moved, transcendentals=0),
    )(*args)


def shape(dims, dtype):
    return jax.ShapeDtypeStruct(dims, dtype)


def page_kernel(pool, moved, rows, slot, table, length, out):
    count, pages, page_len, width = out.shape
    token = lax.broadcasted_iota(I32, (page_len, width), 0)

    @pl.loop(0, count)
    def _(j):
        at = slot[j]

        @pl.when(at >= 0)
        def _():
            for p in range(pages):
                out[j, p] = moved[at, p]

        @pl.when(at < 0)
        def _():
            i = rows[j]
            for p in range(pages):
                page = pool[table[i * pages + p]].astype(F32)
                out[j, p] = jnp.where(token + p * page_len < length[i], page, 0.0).astype(out.dtype)


def take_pages(pool, moved, rows, slot, table, length):
    pages = table.shape[0] // length.shape[0]
    outs = [shape((rows.shape[0], pages) + pool.shape[1:], pool.dtype)]
    args = (pool, moved, rows, slot, table, length)
    return local_call(page_kernel, [VMEM] * 2 + [SMEM] * 4, args, outs, moved=5 * MIB)[0]


def split_kernel(place, x, *outs):
    width = outs[0].shape[1]
    for s, out in enumerate(outs):
        out[...] = x[:, lanes((place[0] ^ s) * width, width)]


def movers_kernel(n_pair, selector, attention, residual, pair, own):
    pair[:, : attention.shape[1]] = pick(selector[:n_pair], attention[...]).astype(BF)
    moving = pick(selector[...], residual[...]).astype(BF)
    pair[:, attention.shape[1] :] = moving[:n_pair]
    own[...] = moving


def handover_kernel(half, place, pair, own, *outs):
    n_pair = half * MIG
    width = own.shape[1]
    for s, out in enumerate(outs):
        first = own[n_pair + (s - 1) * MIG : n_pair + s * MIG] if s else own[:MIG]
        second = pair[s * MIG : (s + 1) * MIG, half * width :]
        blank = jnp.zeros((out.shape[0] - n_pair - 2 * MIG, width), BF)
        columns = pair[:, lanes((place[0] ^ s) * width, width)]
        out[...] = jnp.concatenate([columns, first, second, blank], axis=0)


def project_kernel(half, *refs):
    odd, selector, resid_selector, residual, own, other = refs[:6]
    blocks = refs[6 : 6 + 2 * half]
    outs = refs[6 + 2 * half : 6 + 3 * half]
    buf, weights, sems = refs[6 + 3 * half :]
    rows = residual.shape[0]
    copies = [
        pltpu.make_async_copy(blocks[s], buf.at[pl.ds(s * rows, rows)], sems.at[s])
        for s in range(half)
    ]
    fetches = [
        pltpu.make_async_copy(own, weights.at[odd[0]], sems.at[half]),
        pltpu.make_async_copy(other, weights.at[1 - odd[0]], sems.at[half + 1]),
    ]
    for copy in copies + fetches:
        copy.start()
    at = half * rows
    for block in blocks[half:]:
        buf[at : at + block.shape[0]] = block[...]
        at += block.shape[0]
    resid = pick(resid_selector[:, :rows], residual[...])
    resid = resid + pick(resid_selector[:, rows:], buf[half * rows :])
    for copy in copies:
        copy.wait()
    picked = pick(selector[...], buf[...]).astype(BF)
    for copy in fetches:
        copy.wait()
    depth = own.shape[0]
    product = pick(picked[:, :depth], weights[0]) + pick(picked[:, depth:], weights[1])
    outs[0][...] = resid + product[:rows]
    for t in range(1, half):
        outs[t][...] = product[t * rows : (t + 1) * rows].astype(BF)


def halves(x):
    high = x.astype(BF)
    return high, (x - high.astype(F32)).astype(BF)


def norm_kernel(half, experts, wide, *refs):
    gain, router, selector, pages = refs[:4]
    parts = refs[4 : 4 + half]
    hidden_out, early = refs[4 + half : 6 + half]
    late = refs[6 + half :]
    hidden = parts[0][...]
    for part in parts[1:]:
        hidden = hidden + part[...].astype(F32)
    hidden_out[...] = hidden
    scaled = hidden * gain[...]
    rows = hidden.shape[0]
    lane = lax.broadcasted_iota(I32, (rows, 128), 1)
    stats = jnp.where(lane == 8, jnp.sum(hidden * hidden, axis=1, keepdims=True), 0.0)
    for e in range(experts):
        logit = jnp.sum(scaled * router[e : e + 1], axis=1, keepdims=True)
        stats = jnp.where(lane == e, logit, stats)
    stats = stats.T[: early.shape[0] - rows]
    scaled = scaled.astype(BF)
    early[:rows] = scaled[:, :wide]
    high, low = halves(stats)
    early[rows:] = jnp.zeros((early.shape[0] - rows, wide), BF)
    early[rows:, :rows] = high
    early[rows:, rows : 2 * rows] = low
    chosen = pick(selector[...], scaled[:, wide:]).astype(BF)
    for s in range(experts):
        late[s][:SLOTS] = chosen[s * SLOTS : (s + 1) * SLOTS]
    late[2][SLOTS:] = pages[...]


def dispatch_kernel(ne, experts, *refs):
    place, selector = refs[:2]
    blocks, outs, stats_out = refs[2 : 2 + ne], refs[2 + ne : -1], refs[-1]
    wide = blocks[0].shape[1]
    rows = selector.shape[1]
    stats = jnp.zeros(stats_out.shape, F32)
    for block in blocks:
        stats = stats + block[rows:, :rows].astype(F32) + block[rows:, rows : 2 * rows].astype(F32)
    stats_out[...] = stats
    inverse = lax.rsqrt(stats[stats.shape[0] // 2 :][:1] / D + EPSILON)
    scale = jnp.sum(selector[...].astype(F32) * inverse, axis=1, keepdims=True)
    high, low = halves(scale)
    lane = lax.broadcasted_iota(I32, (scale.shape[0], 128), 1)
    scale = jnp.where(lane == 0, high.astype(F32), jnp.where(lane == 1, low.astype(F32), 0.0)).astype(BF)
    for t in range(experts):
        outs[t][:, ne * wide :] = scale[t * SLOTS : (t + 1) * SLOTS]
    for s in range(ne):
        chosen = pick(selector[...], blocks[s][:rows]).astype(BF)
        columns = lanes((place[0] ^ s) * wide, wide)
        for t in range(experts):
            outs[t][:, columns] = chosen[t * SLOTS : (t + 1) * SLOTS]


def expert_kernel(ne, experts, tiles, place, *refs):
    early, late = refs[:experts], refs[experts : experts + ne]
    gate, up, down = refs[experts + ne : experts + ne + 3]
    refs = refs[experts + ne + 3 :]
    late_out, early_out = refs[:ne], refs[ne : ne + experts]
    rows, scale, active = refs[ne + experts :]
    step = pl.program_id(0)
    rest = late[0].shape[1]
    wide = (early[0].shape[1] - 128) // ne
    feats = wide + rest
    tile = gate.shape[2]

    @pl.when(step == 0)
    def _():
        for t in range(experts):
            at = slice(t * SLOTS, (t + 1) * SLOTS)
            for e in range(ne):
                rows[at, e * feats : e * feats + wide] = early[t][:, e * wide : (e + 1) * wide]
            pieces = early[t][:, ne * wide :].astype(F32)
            scale[at] = pieces[:, :1] + pieces[:, 1:2]
        for s in range(ne):
            rows[:, lanes((place[0] ^ s) * feats + wide, rest)] = late[s][...]

    @pl.when(step < tiles)
    def _():
        gate_h = pick(rows[...], gate[0]) * scale[...]
        up_h = pick(rows[...], up[0]) * scale[...]
        value = gate_h / (1.0 + jnp.exp(-gate_h)) * up_h
        active[:, lanes(step * tile, tile)] = value.astype(BF)

    @pl.when(step >= tiles)
    def _():
        owner = step - tiles
        value = pick(active[...], down[0]).astype(BF)
        for t in range(experts):
            early_out[t][:, lanes(owner * wide, wide)] = value[t * SLOTS : (t + 1) * SLOTS, :wide]
        for s in range(ne):

            @pl.when(owner ^ place[0] == s)
            def _(s=s):
                late_out[s][...] = value[:, wide:]


def expert_call(place, early, late, w_gate, w_up, w_down, ne):
    hidden = w_gate.shape[2]
    slots, rest = late[0].shape
    experts = len(early)
    wide = (early[0].shape[1] - 128) // ne
    tile = 256 if hidden % 256 == 0 else 128
    tiles = hidden // tile
    whole = lambda a: pl.BlockSpec(a.shape, lambda g, place: (0,) * len(a.shape))
    weight = pl.BlockSpec((1, D, tile), lambda g, place: (0, 0, jnp.minimum(g, tiles - 1)))
    down = pl.BlockSpec(
        (1, hidden, wide + rest), lambda g, place: (0, 0, jnp.maximum(g - tiles, 0))
    )
    outs = [shape((slots, rest), BF)] * ne + [shape((SLOTS, ne * wide), BF)] * experts
    values = pl.pallas_call(
        functools.partial(expert_kernel, ne, experts, tiles),
        grid_spec=pltpu.PrefetchScalarGridSpec(
            num_scalar_prefetch=1,
            grid=(tiles + ne,),
            in_specs=[whole(a) for a in (*early, *late)] + [weight] * 2 + [down],
            out_specs=[whole(o) for o in outs],
            scratch_shapes=[
                pltpu.VMEM((slots, D), BF),
                pltpu.VMEM((slots, 1), F32),
                pltpu.VMEM((slots, hidden), BF),
            ],
        ),
        out_shape=outs,
        compiler_params=pltpu.CompilerParams(vmem_limit_bytes=50 * MIB),
        cost_estimate=pl.CostEstimate(
            flops=6 * slots * D * hidden, bytes_accessed=6 * D * hidden, transcendentals=0
        ),
    )(place, *early, *late, w_gate, w_up, w_down)
    return values[:ne], values[ne:]


def weigh_kernel(ne, experts, *refs):
    place, high, low = refs[:3]
    blocks, outs, buf, total = refs[3 : 3 + experts], refs[3 + experts : 3 + experts + ne], *refs[3 + experts + ne :]
    for t in range(experts):
        buf[t * SLOTS : (t + 1) * SLOTS] = blocks[t][...]
    total[...] = pick(high[...], buf[...]) + pick(low[...], buf[...])
    wide = outs[0].shape[1]
    for s in range(ne):
        outs[s][...] = total[:, lanes((place[0] ^ s) * wide, wide)].astype(outs[s].dtype)


def finish_kernel(ne, experts, wide, *refs):
    high, low, hidden = refs[:3]
    early, late = refs[3 : 3 + ne], refs[3 + ne : 3 + ne + experts]
    out, buf = refs[3 + ne + experts :]
    first = hidden[:, :wide]
    for block in early:
        first = first + block[...].astype(F32)
    out[:, :wide] = first
    for t in range(experts):
        buf[t * SLOTS : (t + 1) * SLOTS] = late[t][...]
    out[:, wide:] = hidden[:, wide:] + pick(high[...], buf[...]) + pick(low[...], buf[...])


def body(
    attention_out,
    residual,
    w_out,
    router_w,
    norm_gain,
    page_pool,
    page_table,
    cache_len,
    came_from,
    routes,
    w_gate,
    w_up,
    w_down,
):
    n = lax.axis_size("req")
    ne = lax.axis_size("exp")
    me = lax.axis_index("req")
    ze = lax.axis_index("exp")
    half = n // 2
    q, k = me // 2, me % 2
    rows = attention_out.shape[0]
    feats = residual.shape[1]
    kblock = D // half
    experts = n // 2
    rest = feats // 2
    wide = feats - rest
    place = ze.reshape(1).astype(I32)

    pair_place = q.reshape(1).astype(I32)
    attn_blocks = local_call(
        split_kernel,
        [SMEM, VMEM],
        (pair_place, attention_out),
        [shape((rows, kblock), BF)] * half,
        moved=2 * MIB,
    )
    attn_blocks = [attn_blocks[0]] + [swap(attn_blocks[s], "req", 2 * s) for s in range(1, half)]
    w_other = swap(w_out, "req", 1)
    came_from, _ = lax.optimization_barrier((came_from, attn_blocks[0]))

    local = jnp.arange(rows, dtype=I32)
    in_new = came_from[None, :] == (me * rows + local)[:, None]
    new_ids = jnp.arange(came_from.shape[0], dtype=I32)
    dest = jnp.sum(jnp.where(in_new, new_ids[None, :], 0), axis=1) // rows
    dest_rank = jnp.sum((dest[:, None] == dest[None, :]) & (local[None, :] < local[:, None]), axis=1)
    dest_rel, dest_par = (dest // 2) ^ q, dest % 2
    send_slot = jnp.where(
        dest_par != k,
        dest_rel * MIG + dest_rank,
        jnp.where(dest_rel != 0, (half + dest_rel - 1) * MIG + dest_rank, -1),
    )
    n_pair, n_send = half * MIG, (2 * half - 1) * MIG
    n_hand = -(-(n_pair + 2 * MIG) // 16) * 16
    send_hot = (jnp.arange(n_send, dtype=I32)[:, None] == send_slot[None, :])
    send_row = jnp.sum(jnp.where(send_hot, local[None, :], 0), axis=1)
    send_pick, w_other = lax.optimization_barrier((send_hot.astype(BF), w_other))

    source = jnp.stack(
        [lax.dynamic_slice_in_dim(came_from, (2 * (q ^ t) + k) * rows, rows) for t in range(half)]
    )
    src_group, src_local = source // rows, source % rows
    src_rank = jnp.sum(
        (src_group[:, :, None] == src_group[:, None, :]) & (source[:, None, :] < source[:, :, None]),
        axis=2,
    )
    src_rel, src_par = (src_group // 2) ^ q, src_group % 2
    t_ids = jnp.arange(half, dtype=I32)[:, None]
    attn_at = jnp.where(
        src_par == k,
        src_rel * rows + src_local,
        half * rows + src_rel * n_hand + (t_ids ^ src_rel) * MIG + src_rank,
    ).reshape(-1)
    own_stays = src_group[0] == me
    own_slot = src_rel[0] * 2 * MIG + jnp.where(src_par[0] == k, 0, MIG) + src_rank[0]
    own_hand = src_rel[0] * n_hand + n_pair + jnp.where(src_par[0] == k, 0, MIG) + src_rank[0]
    own_at = jnp.where(own_stays, src_local[0], rows + own_hand)

    pair_rows, own_rows = local_call(
        functools.partial(movers_kernel, n_pair),
        [VMEM] * 3,
        (send_pick, attention_out, residual),
        [shape((n_pair, D + feats), BF), shape((n_send, feats), BF)],
        moved=2 * MIB,
    )
    pair_rows = swap(pair_rows, "req", 1)
    late_blocks = local_call(
        functools.partial(handover_kernel, half),
        [SMEM, VMEM, VMEM],
        (pair_place, pair_rows, own_rows),
        [shape((n_hand, feats), BF)] * half,
        moved=MIB,
    )
    late_blocks = [late_blocks[0]] + [swap(late_blocks[s], "req", 2 * s) for s in range(1, half)]

    expert_ids = jnp.arange(experts, dtype=I32)
    names = routes[:, :, None] == expert_ids[None, None, :]
    named = jnp.any(names, axis=1)
    before = jnp.sum(
        jnp.where((local[None, :] < local[:, None])[:, :, None], named[None, :, :], False), axis=1
    )
    rank = jnp.sum(jnp.where(names, before[:, None, :], 0), axis=2)
    slot_of = ((routes ^ (me % experts)) * SLOTS + rank).astype(I32)
    slot_ids = jnp.arange(experts * SLOTS, dtype=I32)
    slot_pick = jnp.any(slot_ids[:, None, None] == slot_of[None, :, :], axis=2).astype(BF)

    total_rows = half * (rows + n_hand)
    selector = hot(attn_at, total_rows)
    resid_selector = hot(own_at, rows + half * n_hand)
    parts = local_call(
        functools.partial(project_kernel, half),
        [SMEM] + [VMEM] * 3 + [HBM] * (2 + half) + [VMEM] * half,
        (
            k.reshape(1).astype(I32),
            selector,
            resid_selector,
            residual,
            w_out,
            w_other,
            *attn_blocks,
            *late_blocks,
        ),
        [shape((rows, feats), F32)] + [shape((rows, feats), BF)] * (half - 1),
        [
            pltpu.VMEM((total_rows, kblock), BF),
            pltpu.VMEM((2,) + w_out.shape, BF),
            pltpu.SemaphoreType.DMA((half + 2,)),
        ],
        vmem=58,
        flops=2 * half * rows * (total_rows + feats) * kblock,
        moved=6 * MIB,
    )
    parts = [parts[0]] + [swap(parts[s], "req", 2 * s) for s in range(1, half)]

    table = page_table.reshape(-1)
    none = jnp.full((n_send,), -1, I32)
    no_rows = page_pool[:2].reshape((1, 2) + page_pool.shape[1:])
    send_row, _ = lax.optimization_barrier((send_row, parts[0]))
    moving = take_pages(page_pool, no_rows, send_row, none, table, cache_len)
    page = moving.shape[1:]
    pair_pages = swap(moving[:n_pair], "req", 1).reshape((half, MIG) + page)
    own_pages = jnp.concatenate([moving[:MIG], moving[n_pair:]], axis=0).reshape((half, MIG) + page)
    pages = jnp.concatenate([own_pages, pair_pages], axis=1)
    stages = half.bit_length() - 1
    block = pages.shape[1:]
    pages = pages.reshape((half // 2, 2) + block)
    page_rows = pages[:, 1].reshape(-1, page[-1])

    router = jnp.pad(router_w.T, ((0, 8 - experts), (0, 0)))
    late_rows_of = [SLOTS + (page_rows.shape[0] if s == 2 else 0) for s in range(experts)]
    normed = local_call(
        functools.partial(norm_kernel, half, experts, wide),
        [VMEM] * (4 + half),
        (norm_gain[None, :], router, slot_pick, page_rows, *parts),
        [shape((rows, feats), F32), shape((rows + 16, wide), BF)]
        + [shape((count, rest), BF) for count in late_rows_of],
        flops=2 * experts * SLOTS * rows * rest,
        moved=3 * MIB,
    )
    hidden, early = normed[:2]
    late = [normed[2 + s] if s == 0 else swap(normed[2 + s], "req", s) for s in range(experts)]
    early, _ = lax.optimization_barrier((early, late[1]))
    early_blocks = [early] + [swap(early, "exp", s) for s in range(1, ne)]
    came_pages = late[2][SLOTS:].reshape((half // 2,) + block)
    pages = jnp.stack([pages[:, 0], came_pages], axis=1)
    late = jnp.concatenate([x[:SLOTS] for x in late], axis=0)
    late_rows = [late] + [swap(late, "exp", s) for s in range(1, ne)]

    outgoing = local_call(
        functools.partial(dispatch_kernel, ne, experts),
        [SMEM] + [VMEM] * (1 + ne),
        (place, slot_pick, *early_blocks),
        [shape((SLOTS, ne * wide + 128), BF)] * experts + [shape((16, rows), F32)],
        flops=2 * experts * SLOTS * rows * ne * wide,
        moved=3 * MIB,
    )
    stats = outgoing[-1]
    early_rows = [swap(outgoing[s], "req", s) if s else outgoing[s] for s in range(experts)]

    inverse = lax.rsqrt(stats[8] / D + EPSILON)
    logits = (stats[:experts] * inverse[None, :]).T
    chosen = jnp.sum(jnp.where(names, logits[:, None, :], 0.0), axis=2)
    gates = jax.nn.sigmoid(chosen - chosen[:, ::-1])
    gate_slots = jnp.sum(
        jnp.where(slot_of[:, :, None] == slot_ids[None, None, :], gates[:, :, None], 0.0), axis=1
    )
    gate_high, gate_low = halves(gate_slots)

    pages, _ = lax.optimization_barrier((pages, outgoing[0]))
    for bit in range(1, stages):
        pages = pages.reshape((half >> (bit + 1), 2, 1 << bit) + block)
        came_pages = swap(pages[:, 1], "req", 2 << bit)
        pages = jnp.stack([pages[:, 0], came_pages], axis=1)
    moved_pages = pages.reshape((half * 2 * MIG,) + page)

    down_late, down_early = expert_call(place, early_rows, late_rows, w_gate, w_up, w_down, ne)
    late_sum = down_late[0].astype(F32)
    for s in range(1, ne):
        late_sum = late_sum + swap(down_late[s], "exp", s).astype(F32)
    late_sum = late_sum.astype(BF).reshape(experts, SLOTS, rest)
    late_back = [swap(late_sum[s], "req", s) if s else late_sum[s] for s in range(experts)]
    early_back = [swap(down_early[s], "req", s) if s else down_early[s] for s in range(experts)]
    own_slot, _ = lax.optimization_barrier((own_slot, down_early[0]))
    new_pages = take_pages(
        page_pool,
        moved_pages,
        jnp.where(own_stays, src_local[0], 0),
        jnp.where(own_stays, -1, own_slot),
        table,
        cache_len,
    )
    place, new_pages = lax.optimization_barrier((place, new_pages))
    weighted = local_call(
        functools.partial(weigh_kernel, ne, experts),
        [SMEM] + [VMEM] * (2 + experts),
        (place, gate_high, gate_low, *early_back),
        [shape((rows, wide), F32)] + [shape((rows, wide), BF)] * (ne - 1),
        [pltpu.VMEM((experts * SLOTS, ne * wide), BF), pltpu.VMEM((rows, ne * wide), F32)],
        flops=4 * rows * experts * SLOTS * ne * wide,
        moved=3 * MIB,
    )
    early_parts = [weighted[0]] + [swap(weighted[s], "exp", s) for s in range(1, ne)]
    mixed = local_call(
        functools.partial(finish_kernel, ne, experts, wide),
        [VMEM] * (3 + ne + experts),
        (gate_high, gate_low, hidden, *early_parts, *late_back),
        [shape((rows, feats), F32)],
        [pltpu.VMEM((experts * SLOTS, rest), BF)],
        flops=4 * rows * experts * SLOTS * rest,
        moved=2 * MIB,
    )[0]

    return (mixed, new_pages)


def solution(mesh):
    in_specs = (
        P("req", None),
        P("req", "exp"),
        P("req", "exp"),
        P("exp", None),
        P("exp"),
        P("req", None, "exp"),
        P("req", None),
        P("req"),
        P(),
        P("req", None),
        P("req", None, "exp"),
        P("req", None, "exp"),
        P("req", "exp", None),
    )
    out_specs = (P("req", "exp"), P("req", None, None, "exp"))
    return jax.shard_map(body, mesh=mesh, in_specs=in_specs, out_specs=out_specs, check_vma=False)
```

```python
import functools

import jax
import jax.numpy as jnp
from jax import lax
from jax.experimental import pallas as pl
from jax.experimental.pallas import tpu as pltpu
from jax.sharding import PartitionSpec as P

D = 4096
SLOTS = 64
PART = 3
MIG = 4
EPSILON = 1e-05
BF = jnp.bfloat16
F32 = jnp.float32
I32 = jnp.int32
MIB = 2**20
VMEM = pl.BlockSpec(memory_space=pltpu.VMEM)
SMEM = pl.BlockSpec(memory_space=pltpu.SMEM)
HBM = pl.BlockSpec(memory_space=pltpu.HBM)


def swap(x, axis, s):
    n = lax.axis_size(axis)
    return lax.ppermute(x, axis, [(i, i ^ s) for i in range(n)])


def hot(index, count):
    return (index[..., None] == jnp.arange(count, dtype=I32)).astype(BF)


def pick(selector, rows):
    return jnp.dot(selector, rows, preferred_element_type=F32)


def lanes(start, width):
    return pl.ds(pl.multiple_of(start, 128), width)


def local_call(kernel, in_specs, args, outs, scratch=(), vmem=16, flops=0, moved=0, after=()):
    count, waits = len(args), tuple(after)

    def run(*refs):
        kernel(*refs[:count], *refs[count + len(waits) :])

    return pl.pallas_call(
        run,
        out_shape=outs,
        in_specs=list(in_specs) + [pl.BlockSpec(memory_space=pl.ANY)] * len(waits),
        out_specs=[VMEM] * len(outs),
        scratch_shapes=list(scratch),
        compiler_params=pltpu.CompilerParams(vmem_limit_bytes=vmem * MIB),
        cost_estimate=pl.CostEstimate(flops=flops, bytes_accessed=moved, transcendentals=0),
    )(*args, *waits)


def shape(dims, dtype):
    return jax.ShapeDtypeStruct(dims, dtype)


def far(dims, dtype):
    return pltpu.HBM(dims, dtype)


def page_kernel(pool, moved, rows, slot, table, length, out):
    count, pages, page_len, width = out.shape
    token = lax.broadcasted_iota(I32, (page_len, width), 0)

    @pl.loop(0, count)
    def _(j):
        at = slot[j]

        @pl.when(at >= 0)
        def _():
            for p in range(pages):
                out[j, p] = moved[at, p]

        @pl.when(at < 0)
        def _():
            i = rows[j]
            for p in range(pages):
                page = pool[table[i * pages + p]].astype(F32)
                out[j, p] = jnp.where(token + p * page_len < length[i], page, 0.0).astype(out.dtype)


def take_pages(pool, moved, rows, slot, table, length, after=()):
    pages = table.shape[0] // length.shape[0]
    outs = [shape((rows.shape[0], pages) + pool.shape[1:], pool.dtype)]
    args = (pool, moved, rows, slot, table, length)
    return local_call(page_kernel, [VMEM] * 2 + [SMEM] * 4, args, outs, moved=5 * MIB, after=after)[0]


def split_kernel(place, x, order, *outs):
    blocks, order_out = outs[:-1], outs[-1]
    width = blocks[0].shape[1]
    for s, block in enumerate(blocks):
        block[...] = x[:, lanes((place[0] ^ s) * width, width)]
    order_out[...] = order[...]


def movers_kernel(n_pair, selector, attention, residual, pair, own):
    pair[:, : attention.shape[1]] = pick(selector[:n_pair], attention[...]).astype(BF)
    moving = pick(selector[...], residual[...]).astype(BF)
    pair[:, attention.shape[1] :] = moving[:n_pair]
    own[...] = moving


def handover_kernel(half, place, pair, own, *outs):
    n_pair = half * MIG
    width = own.shape[1]
    for s, out in enumerate(outs):
        first = own[n_pair + (s - 1) * MIG : n_pair + s * MIG] if s else own[:MIG]
        second = pair[s * MIG : (s + 1) * MIG, half * width :]
        blank = jnp.zeros((out.shape[0] - n_pair - 2 * MIG, width), BF)
        columns = pair[:, lanes((place[0] ^ s) * width, width)]
        out[...] = jnp.concatenate([columns, first, second, blank], axis=0)


def project_kernel(half, *refs):
    odd, selector, resid_selector, residual, own, other = refs[:6]
    blocks = refs[6 : 6 + 2 * half]
    outs = refs[6 + 2 * half : 6 + 3 * half]
    buf, weights, sems = refs[6 + 3 * half :]
    rows = residual.shape[0]
    copies = [
        pltpu.make_async_copy(blocks[s], buf.at[pl.ds(s * rows, rows)], sems.at[s])
        for s in range(half)
    ]
    fetches = [
        pltpu.make_async_copy(own, weights.at[odd[0]], sems.at[half]),
        pltpu.make_async_copy(other, weights.at[1 - odd[0]], sems.at[half + 1]),
    ]
    for copy in copies + fetches:
        copy.start()
    at = half * rows
    for block in blocks[half:]:
        buf[at : at + block.shape[0]] = block[...]
        at += block.shape[0]
    resid = pick(resid_selector[:, :rows], residual[...])
    resid = resid + pick(resid_selector[:, rows:], buf[half * rows :])
    for copy in copies:
        copy.wait()
    picked = pick(selector[...], buf[...]).astype(BF)
    for copy in fetches:
        copy.wait()
    depth = own.shape[0]
    product = pick(picked[:, :depth], weights[0]) + pick(picked[:, depth:], weights[1])
    outs[0][...] = resid + product[:rows]
    for t in range(1, half):
        outs[t][...] = product[t * rows : (t + 1) * rows].astype(BF)


def halves(x):
    high = x.astype(BF)
    return high, (x - high.astype(F32)).astype(BF)


def norm_kernel(half, experts, wide, *refs):
    gain, router, selector, pages = refs[:4]
    parts = refs[4 : 4 + half]
    hidden_out, early = refs[4 + half : 6 + half]
    late = refs[6 + half :]
    hidden = parts[0][...]
    for part in parts[1:]:
        hidden = hidden + part[...].astype(F32)
    hidden_out[...] = hidden
    scaled = hidden * gain[...]
    rows = hidden.shape[0]
    lane = lax.broadcasted_iota(I32, (rows, 128), 1)
    stats = jnp.where(lane == 8, jnp.sum(hidden * hidden, axis=1, keepdims=True), 0.0)
    for e in range(experts):
        logit = jnp.sum(scaled * router[e : e + 1], axis=1, keepdims=True)
        stats = jnp.where(lane == e, logit, stats)
    stats = stats.T[: early.shape[0] - rows]
    scaled = scaled.astype(BF)
    early[:rows] = scaled[:, :wide]
    high, low = halves(stats)
    early[rows:] = jnp.zeros((early.shape[0] - rows, wide), BF)
    early[rows:, :rows] = high
    early[rows:, rows : 2 * rows] = low
    chosen = pick(selector[...], scaled[:, wide:]).astype(BF)
    for s in range(experts):
        late[s][:SLOTS, : chosen.shape[1]] = chosen[s * SLOTS : (s + 1) * SLOTS]
    late[2][SLOTS:] = pages[...]


def dispatch_kernel(ne, experts, *refs):
    place, selector = refs[:2]
    blocks, late, refs = refs[2 : 2 + ne], refs[2 + ne : 2 + ne + experts], refs[2 + ne + experts :]
    outs, stats_out, late_out = refs[:experts], refs[experts], refs[experts + 1]
    for t in range(experts):
        late_out[t * SLOTS : (t + 1) * SLOTS] = late[t][:SLOTS, : late_out.shape[1]]
    wide = blocks[0].shape[1]
    rows = selector.shape[1]
    stats = jnp.zeros(stats_out.shape, F32)
    for block in blocks:
        stats = stats + block[rows:, :rows].astype(F32) + block[rows:, rows : 2 * rows].astype(F32)
    stats_out[...] = stats
    inverse = lax.rsqrt(stats[stats.shape[0] // 2 :][:1] / D + EPSILON)
    scale = jnp.sum(selector[...].astype(F32) * inverse, axis=1, keepdims=True)
    high, low = halves(scale)
    lane = lax.broadcasted_iota(I32, (scale.shape[0], 128), 1)
    scale = jnp.where(lane == 0, high.astype(F32), jnp.where(lane == 1, low.astype(F32), 0.0)).astype(BF)
    for t in range(experts):
        outs[t][:, ne * wide :] = scale[t * SLOTS : (t + 1) * SLOTS]
    for s in range(ne):
        chosen = pick(selector[...], blocks[s][:rows]).astype(BF)
        columns = lanes((place[0] ^ s) * wide, wide)
        for t in range(experts):
            outs[t][:, columns] = chosen[t * SLOTS : (t + 1) * SLOTS]


def expert_kernel(ne, experts, tiles, place, *refs):
    early, late = refs[:experts], refs[experts : experts + ne]
    gate, up, down = refs[experts + ne : experts + ne + 3]
    refs = refs[experts + ne + 3 :]
    late_out, early_out = refs[:ne], refs[ne : ne + experts]
    done, rows, scale, active = refs[ne + experts :]
    step = pl.program_id(0)
    done[...] = jnp.zeros(done.shape, I32)
    rest = late[0].shape[1]
    wide = (early[0].shape[1] - 128) // ne
    feats = wide + rest
    tile = gate.shape[2]

    @pl.when(step == 0)
    def _():
        for t in range(experts):
            at = slice(t * SLOTS, (t + 1) * SLOTS)
            for e in range(ne):
                rows[at, e * feats : e * feats + wide] = early[t][:, e * wide : (e + 1) * wide]
            pieces = early[t][:, ne * wide :].astype(F32)
            scale[at] = pieces[:, :1] + pieces[:, 1:2]
        for s in range(ne):
            rows[:, lanes((place[0] ^ s) * feats + wide, rest)] = late[s][...]

    @pl.when(step < tiles)
    def _():
        gate_h = pick(rows[...], gate[0]) * scale[...]
        up_h = pick(rows[...], up[0]) * scale[...]
        value = gate_h / (1.0 + jnp.exp(-gate_h)) * up_h
        active[:, lanes(step * tile, tile)] = value.astype(BF)

    @pl.when(step >= tiles)
    def _():
        owner = step - tiles
        value = pick(active[...], down[0]).astype(BF)
        for t in range(experts):
            early_out[t][:, lanes(owner * wide, wide)] = value[t * SLOTS : (t + 1) * SLOTS, :wide]
        for s in range(ne):

            @pl.when(owner ^ place[0] == s)
            def _(s=s):
                late_out[s][...] = value[:, wide:]


def expert_call(place, early, late, w_gate, w_up, w_down, ne):
    hidden = w_gate.shape[2]
    slots, rest = late[0].shape
    experts = len(early)
    wide = (early[0].shape[1] - 128) // ne
    tile = 256 if hidden % 256 == 0 else 128
    tiles = hidden // tile
    whole = lambda a: pl.BlockSpec(a.shape, lambda g, place: (0,) * len(a.shape))
    weight = pl.BlockSpec((1, D, tile), lambda g, place: (0, 0, jnp.minimum(g, tiles - 1)))
    down = pl.BlockSpec(
        (1, hidden, wide + rest), lambda g, place: (0, 0, jnp.maximum(g - tiles, 0))
    )
    outs = [shape((slots, rest), BF)] * ne + [shape((SLOTS, ne * wide), BF)] * experts
    outs = outs + [shape((8, 128), I32)]
    values = pl.pallas_call(
        functools.partial(expert_kernel, ne, experts, tiles),
        grid_spec=pltpu.PrefetchScalarGridSpec(
            num_scalar_prefetch=1,
            grid=(tiles + ne,),
            in_specs=[whole(a) for a in (*early, *late)] + [weight] * 2 + [down],
            out_specs=[whole(o) for o in outs],
            scratch_shapes=[
                pltpu.VMEM((slots, D), BF),
                pltpu.VMEM((slots, 1), F32),
                pltpu.VMEM((slots, hidden), BF),
            ],
        ),
        out_shape=outs,
        compiler_params=pltpu.CompilerParams(vmem_limit_bytes=50 * MIB),
        cost_estimate=pl.CostEstimate(
            flops=6 * slots * D * hidden, bytes_accessed=6 * D * hidden, transcendentals=0
        ),
    )(place, *early, *late, w_gate, w_up, w_down)
    return values[:ne], values[ne:-1], values[-1]


def weigh_kernel(ne, experts, *refs):
    place, high, low = refs[:3]
    blocks, late = refs[3 : 3 + experts], refs[3 + experts : 3 + experts + ne]
    refs = refs[3 + experts + ne :]
    outs, late_outs, (buf, total) = refs[:ne], refs[ne : ne + experts], refs[ne + experts :]
    for t in range(experts):
        buf[t * SLOTS : (t + 1) * SLOTS] = blocks[t][...]
    total[...] = pick(high[...], buf[...]) + pick(low[...], buf[...])
    wide = outs[0].shape[1]
    for s in range(ne):
        outs[s][...] = total[:, lanes((place[0] ^ s) * wide, wide)].astype(outs[s].dtype)
    late_sum = late[0][...].astype(F32)
    for block in late[1:]:
        late_sum = late_sum + block[...].astype(F32)
    for t in range(experts):
        late_outs[t][...] = late_sum[t * SLOTS : (t + 1) * SLOTS].astype(BF)


def finish_kernel(ne, experts, wide, *refs):
    high, low, hidden = refs[:3]
    early, late = refs[3 : 3 + ne], refs[3 + ne : 3 + ne + experts]
    out, buf = refs[3 + ne + experts :]
    first = hidden[:, :wide]
    for block in early:
        first = first + block[...].astype(F32)
    out[:, :wide] = first
    for t in range(experts):
        buf[t * SLOTS : (t + 1) * SLOTS] = late[t][...]
    out[:, wide:] = hidden[:, wide:] + pick(high[...], buf[...]) + pick(low[...], buf[...])


def body(
    attention_out,
    residual,
    w_out,
    router_w,
    norm_gain,
    page_pool,
    page_table,
    cache_len,
    came_from,
    routes,
    w_gate,
    w_up,
    w_down,
):
    n = lax.axis_size("req")
    ne = lax.axis_size("exp")
    me = lax.axis_index("req")
    ze = lax.axis_index("exp")
    half = n // 2
    q, k = me // 2, me % 2
    rows = attention_out.shape[0]
    feats = residual.shape[1]
    kblock = D // half
    experts = n // 2
    rest = max(128, feats * PART // 8 // 128 * 128)
    wide = feats - rest
    place = ze.reshape(1).astype(I32)

    pair_place = q.reshape(1).astype(I32)
    *attn_blocks, came_from = local_call(
        split_kernel,
        [SMEM, VMEM, VMEM],
        (pair_place, attention_out, came_from.reshape(n, rows)),
        [far((rows, kblock), BF)] * half + [shape((n, rows), I32)],
        vmem=60,
        moved=2 * MIB,
    )
    came_from = came_from.reshape(-1)
    attn_blocks = [attn_blocks[0]] + [swap(attn_blocks[s], "req", 2 * s) for s in range(1, half)]
    w_other = swap(w_out, "req", 1)

    local = jnp.arange(rows, dtype=I32)
    in_new = came_from[None, :] == (me * rows + local)[:, None]
    new_ids = jnp.arange(came_from.shape[0], dtype=I32)
    dest = jnp.sum(jnp.where(in_new, new_ids[None, :], 0), axis=1) // rows
    dest_rank = jnp.sum((dest[:, None] == dest[None, :]) & (local[None, :] < local[:, None]), axis=1)
    dest_rel, dest_par = (dest // 2) ^ q, dest % 2
    send_slot = jnp.where(
        dest_par != k,
        dest_rel * MIG + dest_rank,
        jnp.where(dest_rel != 0, (half + dest_rel - 1) * MIG + dest_rank, -1),
    )
    n_pair, n_send = half * MIG, (2 * half - 1) * MIG
    n_hand = -(-(n_pair + 2 * MIG) // 16) * 16
    send_hot = (jnp.arange(n_send, dtype=I32)[:, None] == send_slot[None, :])
    send_row = jnp.sum(jnp.where(send_hot, local[None, :], 0), axis=1)
    send_pick = send_hot.astype(BF)

    source = jnp.stack(
        [lax.dynamic_slice_in_dim(came_from, (2 * (q ^ t) + k) * rows, rows) for t in range(half)]
    )
    src_group, src_local = source // rows, source % rows
    src_rank = jnp.sum(
        (src_group[:, :, None] == src_group[:, None, :]) & (source[:, None, :] < source[:, :, None]),
        axis=2,
    )
    src_rel, src_par = (src_group // 2) ^ q, src_group % 2
    t_ids = jnp.arange(half, dtype=I32)[:, None]
    attn_at = jnp.where(
        src_par == k,
        src_rel * rows + src_local,
        half * rows + src_rel * n_hand + (t_ids ^ src_rel) * MIG + src_rank,
    ).reshape(-1)
    own_stays = src_group[0] == me
    own_slot = src_rel[0] * 2 * MIG + jnp.where(src_par[0] == k, 0, MIG) + src_rank[0]
    own_hand = src_rel[0] * n_hand + n_pair + jnp.where(src_par[0] == k, 0, MIG) + src_rank[0]
    own_at = jnp.where(own_stays, src_local[0], rows + own_hand)

    pair_rows, own_rows = local_call(
        functools.partial(movers_kernel, n_pair),
        [VMEM] * 3,
        (send_pick, attention_out, residual),
        [shape((n_pair, D + feats), BF), shape((n_send, feats), BF)],
        moved=2 * MIB,
        after=[w_other],
    )
    pair_rows = swap(pair_rows, "req", 1)
    late_blocks = local_call(
        functools.partial(handover_kernel, half),
        [SMEM, VMEM, VMEM],
        (pair_place, pair_rows, own_rows),
        [shape((n_hand, feats), BF)] * half,
        moved=MIB,
    )
    late_blocks = [late_blocks[0]] + [swap(late_blocks[s], "req", 2 * s) for s in range(1, half)]

    expert_ids = jnp.arange(experts, dtype=I32)
    names = routes[:, :, None] == expert_ids[None, None, :]
    named = jnp.any(names, axis=1)
    before = jnp.sum(
        jnp.where((local[None, :] < local[:, None])[:, :, None], named[None, :, :], False), axis=1
    )
    rank = jnp.sum(jnp.where(names, before[:, None, :], 0), axis=2)
    slot_of = ((routes ^ (me % experts)) * SLOTS + rank).astype(I32)
    slot_ids = jnp.arange(experts * SLOTS, dtype=I32)
    slot_pick = jnp.any(slot_ids[:, None, None] == slot_of[None, :, :], axis=2).astype(BF)

    total_rows = half * (rows + n_hand)
    selector = hot(attn_at, total_rows)
    resid_selector = hot(own_at, rows + half * n_hand)
    parts = local_call(
        functools.partial(project_kernel, half),
        [SMEM] + [VMEM] * 3 + [HBM] * (2 + half) + [VMEM] * half,
        (
            k.reshape(1).astype(I32),
            selector,
            resid_selector,
            residual,
            w_out,
            w_other,
            *attn_blocks,
            *late_blocks,
        ),
        [shape((rows, feats), F32)] + [shape((rows, feats), BF)] * (half - 1),
        [
            pltpu.VMEM((total_rows, kblock), BF),
            pltpu.VMEM((2,) + w_out.shape, BF),
            pltpu.SemaphoreType.DMA((half + 2,)),
        ],
        vmem=58,
        flops=2 * half * rows * (total_rows + feats) * kblock,
        moved=6 * MIB,
    )
    parts = [parts[0]] + [swap(parts[s], "req", 2 * s) for s in range(1, half)]

    table = page_table.reshape(-1)
    none = jnp.full((n_send,), -1, I32)
    no_rows = page_pool[:2].reshape((1, 2) + page_pool.shape[1:])
    moving = take_pages(page_pool, no_rows, send_row, none, table, cache_len)
    page = moving.shape[1:]
    pair_pages = swap(moving[:n_pair], "req", 1).reshape((half, MIG) + page)
    own_pages = jnp.concatenate([moving[:MIG], moving[n_pair:]], axis=0).reshape((half, MIG) + page)
    pages = jnp.concatenate([own_pages, pair_pages], axis=1)
    stages = half.bit_length() - 1
    block = pages.shape[1:]
    pages = pages.reshape((half // 2, 2) + block)
    page_rows = pages[:, 1].reshape(-1, page[-1])

    router = jnp.pad(router_w.T, ((0, 8 - experts), (0, 0)))
    late_shapes = [(SLOTS, rest)] * experts
    late_shapes[2] = (SLOTS + page_rows.shape[0], page[-1])
    normed = local_call(
        functools.partial(norm_kernel, half, experts, wide),
        [VMEM] * (4 + half),
        (norm_gain[None, :], router, slot_pick, page_rows, *parts),
        [shape((rows, feats), F32), far((rows + 16, wide), BF)]
        + [far(dims, BF) for dims in late_shapes],
        flops=2 * experts * SLOTS * rows * rest,
        moved=3 * MIB,
    )
    hidden, early = normed[:2]
    late = [normed[2 + s] if s == 0 else swap(normed[2 + s], "req", s) for s in range(experts)]
    early_blocks = [early] + [swap(early, "exp", s) for s in range(1, ne)]
    came_pages = late[2][SLOTS:].reshape((half // 2,) + block)
    pages = jnp.stack([pages[:, 0], came_pages], axis=1)
    outgoing = local_call(
        functools.partial(dispatch_kernel, ne, experts),
        [SMEM] + [VMEM] * (1 + ne + experts),
        (place, slot_pick, *early_blocks, *late),
        [far((SLOTS, ne * wide + 128), BF)] * experts
        + [shape((16, rows), F32), far((experts * SLOTS, rest), BF)],
        vmem=60,
        flops=2 * experts * SLOTS * rows * ne * wide,
        moved=3 * MIB,
    )
    late = outgoing[experts + 1]
    late_rows = [late] + [swap(late, "exp", s) for s in range(1, ne)]

    stats = outgoing[experts]
    early_rows = [swap(outgoing[s], "req", s) if s else outgoing[s] for s in range(experts)]

    inverse = lax.rsqrt(stats[8] / D + EPSILON)
    logits = (stats[:experts] * inverse[None, :]).T
    chosen = jnp.sum(jnp.where(names, logits[:, None, :], 0.0), axis=2)
    gates = jax.nn.sigmoid(chosen - chosen[:, ::-1])
    gate_slots = jnp.sum(
        jnp.where(slot_of[:, :, None] == slot_ids[None, None, :], gates[:, :, None], 0.0), axis=1
    )
    gate_high, gate_low = halves(gate_slots)

    for bit in range(1, stages):
        pages = pages.reshape((half >> (bit + 1), 2, 1 << bit) + block)
        came_pages = swap(pages[:, 1], "req", 2 << bit)
        pages = jnp.stack([pages[:, 0], came_pages], axis=1)
    moved_pages = pages.reshape((half * 2 * MIG,) + page)

    down_late, down_early, done = expert_call(place, early_rows, late_rows, w_gate, w_up, w_down, ne)
    late_blocks = [down_late[0]] + [swap(down_late[s], "exp", s) for s in range(1, ne)]
    early_back = [swap(down_early[s], "req", s) if s else down_early[s] for s in range(experts)]
    new_pages = take_pages(
        page_pool,
        moved_pages,
        jnp.where(own_stays, src_local[0], 0),
        jnp.where(own_stays, -1, own_slot),
        table,
        cache_len,
        [done],
    )
    weighted = local_call(
        functools.partial(weigh_kernel, ne, experts),
        [SMEM] + [VMEM] * (2 + experts + ne),
        (place, gate_high, gate_low, *early_back, *late_blocks),
        [shape((rows, wide), F32)]
        + [shape((rows, wide), BF)] * (ne - 1)
        + [shape((SLOTS, rest), BF)] * experts,
        [pltpu.VMEM((experts * SLOTS, ne * wide), BF), pltpu.VMEM((rows, ne * wide), F32)],
        flops=4 * rows * experts * SLOTS * ne * wide,
        moved=3 * MIB,
    )
    early_parts = [weighted[0]] + [swap(weighted[s], "exp", s) for s in range(1, ne)]
    late_back = [
        swap(weighted[ne + s], "req", s) if s else weighted[ne] for s in range(experts)
    ]
    mixed = local_call(
        functools.partial(finish_kernel, ne, experts, wide),
        [VMEM] * (3 + ne + experts),
        (gate_high, gate_low, hidden, *early_parts, *late_back),
        [shape((rows, feats), F32)],
        [pltpu.VMEM((experts * SLOTS, rest), BF)],
        flops=4 * rows * experts * SLOTS * rest,
        moved=2 * MIB,
    )[0]

    return (mixed, new_pages)


def solution(mesh):
    in_specs = (
        P("req", None),
        P("req", "exp"),
        P("req", "exp"),
        P("exp", None),
        P("exp"),
        P("req", None, "exp"),
        P("req", None),
        P("req"),
        P(),
        P("req", None),
        P("req", None, "exp"),
        P("req", None, "exp"),
        P("req", "exp", None),
    )
    out_specs = (P("req", "exp"), P("req", None, None, "exp"))
    return jax.shard_map(body, mesh=mesh, in_specs=in_specs, out_specs=out_specs, check_vma=False)
```

```python
import functools

import jax
import jax.numpy as jnp
from jax import lax
from jax.experimental import pallas as pl
from jax.experimental.pallas import tpu as pltpu
from jax.sharding import PartitionSpec as P

D = 4096
SLOTS = 64
PART = 3
AHEAD = 3
MIG = 4
EPSILON = 1e-05
BF = jnp.bfloat16
F32 = jnp.float32
I32 = jnp.int32
MIB = 2**20
VMEM = pl.BlockSpec(memory_space=pltpu.VMEM)
SMEM = pl.BlockSpec(memory_space=pltpu.SMEM)
HBM = pl.BlockSpec(memory_space=pltpu.HBM)


def swap(x, axis, s):
    n = lax.axis_size(axis)
    return lax.ppermute(x, axis, [(i, i ^ s) for i in range(n)])


def hot(index, count):
    return (index[..., None] == jnp.arange(count, dtype=I32)).astype(BF)


def pick(selector, rows):
    return jnp.dot(selector, rows, preferred_element_type=F32)


def lanes(start, width):
    return pl.ds(pl.multiple_of(start, 128), width)


def local_call(kernel, in_specs, args, outs, scratch=(), vmem=16, flops=0, moved=0, after=(), out_specs=None):
    count, waits = len(args), tuple(after)

    def run(*refs):
        kernel(*refs[:count], *refs[count + len(waits) :])

    return pl.pallas_call(
        run,
        out_shape=outs,
        in_specs=list(in_specs) + [pl.BlockSpec(memory_space=pl.ANY)] * len(waits),
        out_specs=out_specs or [VMEM] * len(outs),
        scratch_shapes=list(scratch),
        compiler_params=pltpu.CompilerParams(vmem_limit_bytes=vmem * MIB),
        cost_estimate=pl.CostEstimate(flops=flops, bytes_accessed=moved, transcendentals=0),
    )(*args, *waits)


def shape(dims, dtype):
    return jax.ShapeDtypeStruct(dims, dtype)


def far(dims, dtype):
    return pltpu.HBM(dims, dtype)


def page_kernel(pool, moved, rows, slot, table, length, out):
    count, pages, page_len, width = out.shape
    token = lax.broadcasted_iota(I32, (page_len, width), 0)

    @pl.loop(0, count)
    def _(j):
        at = slot[j]

        @pl.when(at >= 0)
        def _():
            for p in range(pages):
                out[j, p] = moved[at, p]

        @pl.when(at < 0)
        def _():
            i = rows[j]
            for p in range(pages):
                page = pool[table[i * pages + p]].astype(F32)
                out[j, p] = jnp.where(token + p * page_len < length[i], page, 0.0).astype(out.dtype)


def take_pages(pool, moved, rows, slot, table, length, after=()):
    pages = table.shape[0] // length.shape[0]
    outs = [shape((rows.shape[0], pages) + pool.shape[1:], pool.dtype)]
    args = (pool, moved, rows, slot, table, length)
    return local_call(page_kernel, [VMEM] * 2 + [SMEM] * 4, args, outs, moved=5 * MIB, after=after)[0]


def split_kernel(place, x, order, *outs):
    blocks, order_out = outs[:-1], outs[-1]
    width = blocks[0].shape[1]
    for s, block in enumerate(blocks):
        block[...] = x[:, lanes((place[0] ^ s) * width, width)]
    order_out[...] = order[...]


def movers_kernel(half, spot, order, attention, residual, pair, own, row_out):
    n, rows = order.shape
    down, across = (lax.broadcasted_iota(I32, (rows, rows), d) for d in (0, 1))
    mine = (2 * spot[0] + spot[1]) * rows + down
    found = jnp.zeros((rows, rows), F32)
    for g in range(1, n):
        found = found + jnp.where(order[g : g + 1] == mine, float(g), 0.0)
    dest = jnp.broadcast_to(jnp.sum(found, axis=1, keepdims=True), (rows, rows))
    dest_row = dest.T
    rank = jnp.sum(jnp.where((dest == dest_row) & (down < across), 1.0, 0.0), axis=0, keepdims=True)
    rank = rank.astype(I32)
    to = dest_row[:1].astype(I32)
    far_off, core = (to >> 1) ^ spot[0], to & 1
    kept = jnp.where(far_off != 0, (half + far_off - 1) * MIG + rank, -1)
    slot = jnp.where(core != spot[1], far_off * MIG + rank, kept)
    chosen = lax.broadcasted_iota(I32, (own.shape[0], rows), 0) == slot
    selector = jnp.where(chosen, 1.0, 0.0)
    numbers = lax.broadcasted_iota(I32, selector.shape, 1).astype(F32)
    number = jnp.sum(selector * numbers, axis=1, keepdims=True)
    row_out[...] = jnp.broadcast_to(number, row_out.shape).astype(I32)
    selector = selector.astype(BF)
    n_pair = pair.shape[0]
    pair[:, : attention.shape[1]] = pick(selector[:n_pair], attention[...]).astype(BF)
    moving = pick(selector, residual[...]).astype(BF)
    pair[:, attention.shape[1] :] = moving[:n_pair]
    own[...] = moving


def handover_kernel(half, place, pair, own, order, *outs):
    outs[-1][...] = order[...]
    outs = outs[:-1]
    n_pair = half * MIG
    width = own.shape[1]
    for s, out in enumerate(outs):
        first = own[n_pair + (s - 1) * MIG : n_pair + s * MIG] if s else own[:MIG]
        second = pair[s * MIG : (s + 1) * MIG, half * width :]
        blank = jnp.zeros((out.shape[0] - n_pair - 2 * MIG, width), BF)
        columns = pair[:, lanes((place[0] ^ s) * width, width)]
        out[...] = jnp.concatenate([columns, first, second, blank], axis=0)


def slots_kernel(experts, spot, routes, picked, slots):
    rows = routes.shape[1]
    ids = lax.broadcasted_iota(I32, (8, rows), 0)
    named = jnp.where((ids == routes[0:1]) | (ids == routes[1:2]), 1.0, 0.0)
    down, across = (lax.broadcasted_iota(I32, (rows, rows), d) for d in (0, 1))
    before = pick(named.astype(BF), jnp.where(down < across, 1.0, 0.0).astype(BF))
    at = lax.broadcasted_iota(I32, picked.shape, 0)
    chosen = jnp.zeros(picked.shape, F32)
    for top in range(2):
        route = routes[top : top + 1]
        rank = jnp.sum(jnp.where(ids == route, before, 0.0), axis=0, keepdims=True).astype(I32)
        slot = (route ^ spot[0]) * SLOTS + rank
        slots[top : top + 1] = slot
        chosen = chosen + jnp.where(at == slot, 1.0, 0.0)
    picked[...] = chosen.astype(BF)


def project_kernel(half, *refs):
    odd, selector, resid_selector, residual, own, other = refs[:6]
    blocks = refs[6 : 6 + 2 * half]
    outs = refs[6 + 2 * half : 6 + 3 * half]
    buf, weights, sems = refs[6 + 3 * half :]
    rows = residual.shape[0]
    copies = [
        pltpu.make_async_copy(blocks[s], buf.at[pl.ds(s * rows, rows)], sems.at[s])
        for s in range(half)
    ]
    fetches = [
        pltpu.make_async_copy(own, weights.at[odd[0]], sems.at[half]),
        pltpu.make_async_copy(other, weights.at[1 - odd[0]], sems.at[half + 1]),
    ]
    for copy in copies + fetches:
        copy.start()
    at = half * rows
    for block in blocks[half:]:
        buf[at : at + block.shape[0]] = block[...]
        at += block.shape[0]
    resid = pick(resid_selector[:, :rows], residual[...])
    resid = resid + pick(resid_selector[:, rows:], buf[half * rows :])
    for copy in copies:
        copy.wait()
    picked = pick(selector[...], buf[...]).astype(BF)
    for copy in fetches:
        copy.wait()
    depth = own.shape[0]
    product = pick(picked[:, :depth], weights[0]) + pick(picked[:, depth:], weights[1])
    outs[0][...] = resid + product[:rows]
    for t in range(1, half):
        outs[t][...] = product[t * rows : (t + 1) * rows].astype(BF)


def halves(x):
    high = x.astype(BF)
    return high, (x - high.astype(F32)).astype(BF)


def norm_kernel(half, experts, wide, *refs):
    gain, router, selector, pages = refs[:4]
    parts = refs[4 : 4 + half]
    hidden_out, early = refs[4 + half : 6 + half]
    late = refs[6 + half :]
    hidden = parts[0][...]
    for part in parts[1:]:
        hidden = hidden + part[...].astype(F32)
    hidden_out[...] = hidden
    scaled = hidden * gain[...]
    rows = hidden.shape[0]
    lane = lax.broadcasted_iota(I32, (rows, 128), 1)
    stats = jnp.where(lane == 8, jnp.sum(hidden * hidden, axis=1, keepdims=True), 0.0)
    for e in range(experts):
        logit = jnp.sum(scaled * router[e : e + 1], axis=1, keepdims=True)
        stats = jnp.where(lane == e, logit, stats)
    stats = stats.T[: early.shape[0] - rows]
    scaled = scaled.astype(BF)
    early[:rows] = scaled[:, :wide]
    high, low = halves(stats)
    early[rows:] = jnp.zeros((early.shape[0] - rows, wide), BF)
    early[rows:, :rows] = high
    early[rows:, rows : 2 * rows] = low
    chosen = pick(selector[...], scaled[:, wide:]).astype(BF)
    for s in range(experts):
        late[s][:SLOTS, : chosen.shape[1]] = chosen[s * SLOTS : (s + 1) * SLOTS]
    late[2][SLOTS:] = pages[...]


def hold_kernel(x, out):
    out[...] = x[...]


def hold(x, after):
    return local_call(hold_kernel, [VMEM], (x,), [far(x.shape, x.dtype)], after=[after])[0]


def dispatch_kernel(ne, experts, *refs):
    place, selector = refs[:2]
    blocks, late, refs = refs[2 : 2 + ne], refs[2 + ne : 2 + ne + experts], refs[2 + ne + experts :]
    outs, stats_out, late_out = refs[:experts], refs[experts], refs[experts + 1]
    for t in range(experts):
        late_out[t * SLOTS : (t + 1) * SLOTS] = late[t][:SLOTS, : late_out.shape[1]]
    wide = blocks[0].shape[1]
    rows = selector.shape[1]
    stats = jnp.zeros(stats_out.shape, F32)
    for block in blocks:
        stats = stats + block[rows:, :rows].astype(F32) + block[rows:, rows : 2 * rows].astype(F32)
    stats_out[...] = stats
    inverse = lax.rsqrt(stats[stats.shape[0] // 2 :][:1] / D + EPSILON)
    scale = jnp.sum(selector[...].astype(F32) * inverse, axis=1, keepdims=True)
    high, low = halves(scale)
    lane = lax.broadcasted_iota(I32, (scale.shape[0], 128), 1)
    scale = jnp.where(lane == 0, high.astype(F32), jnp.where(lane == 1, low.astype(F32), 0.0)).astype(BF)
    for t in range(experts):
        outs[t][:, ne * wide :] = scale[t * SLOTS : (t + 1) * SLOTS]
    for s in range(ne):
        chosen = pick(selector[...], blocks[s][:rows]).astype(BF)
        columns = lanes((place[0] ^ s) * wide, wide)
        for t in range(experts):
            outs[t][:, columns] = chosen[t * SLOTS : (t + 1) * SLOTS]


def expert_kernel(ne, experts, tile, spot, *refs):
    early, late = refs[:experts], refs[experts : experts + ne]
    gate, up, down, stats = refs[experts + ne : experts + ne + 4]
    refs = refs[experts + ne + 4 :]
    late_out, early_out = refs[:ne], refs[ne : ne + experts]
    stats_out = refs[ne + experts]
    rows, pieces, active, gate_buf, up_buf, down_buf, late_buf, early_buf = refs[ne + experts + 1 : -3]
    sems, load_sems, out_sems = refs[-3:]
    place = spot[0]
    rest = late[0].shape[1]
    wide = (early[0].shape[1] - 128) // ne
    feats = wide + rest
    tiles = gate.shape[2] // tile

    def copies(f):
        columns = lanes(f * tile, tile)
        return [
            pltpu.make_async_copy(gate.at[0, :, columns], gate_buf.at[:, columns], sems.at[0, f]),
            pltpu.make_async_copy(up.at[0, :, columns], up_buf.at[:, columns], sems.at[1, f]),
        ]

    def down_copy(e):
        return pltpu.make_async_copy(down.at[0, :, lanes(e * feats, feats)], down_buf.at[e], sems.at[2, e])

    def early_copy(e, t):
        columns = lanes(e * wide, wide)
        return pltpu.make_async_copy(
            early_buf.at[t, :, columns], early_out[t].at[:, columns], out_sems.at[e, t]
        )

    def late_copy(e, s):
        return pltpu.make_async_copy(late_buf.at[e], late_out[s], out_sems.at[e, experts])

    def start(unit):
        @pl.when(unit < tiles)
        def _():
            for copy in copies(unit):
                copy.start()

        @pl.when((unit >= tiles) & (unit < tiles + ne))
        def _():
            down_copy(unit - tiles).start()

    loads = []

    def load(source, target):
        loads.append(pltpu.make_async_copy(source, target, load_sems.at[len(loads)]))

    for t in range(experts):
        at = pl.ds(t * SLOTS, SLOTS)
        load(early[t].at[:, pl.ds(ne * wide, 128)], pieces.at[at])
        for e in range(ne):
            load(early[t].at[:, pl.ds(e * wide, wide)], rows.at[at, pl.ds(e * feats, wide)])
    for s in range(ne):
        load(late[s], rows.at[:, lanes((place ^ s) * feats + wide, rest)])
    for copy in loads:
        copy.start()
    start(jnp.int32(0))
    stats_out[...] = stats[...]
    for copy in loads:
        copy.wait()
    for unit in range(1, AHEAD):
        start(jnp.int32(unit))
    scale = pieces[:, :1].astype(F32) + pieces[:, 1:2].astype(F32)

    @pl.loop(0, tiles)
    def _(f):
        for copy in copies(f):
            copy.wait()
        start(f + AHEAD)
        columns = lanes(f * tile, tile)
        gate_h = pick(rows[...], gate_buf[:, columns]) * scale
        up_h = pick(rows[...], up_buf[:, columns]) * scale
        active[:, columns] = (gate_h / (1.0 + jnp.exp(-gate_h)) * up_h).astype(BF)

    @pl.loop(0, ne)
    def _(e):
        down_copy(e).wait()
        start(e + tiles + AHEAD)
        value = pick(active[...], down_buf[e]).astype(BF)
        late_buf[e] = value[:, wide:]
        for t in range(experts):
            early_buf[t, :, lanes(e * wide, wide)] = value[t * SLOTS : (t + 1) * SLOTS, :wide]
            early_copy(e, t).start()
        for s in range(ne):

            @pl.when(e ^ place == s)
            def _():
                late_copy(e, s).start()

    @pl.loop(0, ne)
    def _(e):
        late_copy(e, 0).wait()
        for t in range(experts):
            early_copy(e, t).wait()


def expert_call(place, early, late, w_gate, w_up, w_down, stats, ne):
    hidden = w_gate.shape[2]
    slots, rest = late[0].shape
    experts = len(early)
    wide = (early[0].shape[1] - 128) // ne
    tile = 256 if hidden % 256 == 0 else 128
    values = local_call(
        functools.partial(expert_kernel, ne, experts, tile),
        [SMEM] + [HBM] * (experts + ne + 3) + [VMEM],
        (place, *early, *late, w_gate, w_up, w_down, stats),
        [far((slots, rest), BF)] * ne
        + [far((SLOTS, ne * wide), BF)] * experts
        + [shape(stats.shape, F32)],
        [
            pltpu.VMEM((slots, D), BF),
            pltpu.VMEM((slots, 128), BF),
            pltpu.VMEM((slots, hidden), BF),
            pltpu.VMEM((D, hidden), BF),
            pltpu.VMEM((D, hidden), BF),
            pltpu.VMEM((ne, hidden, wide + rest), BF),
            pltpu.VMEM((ne, slots, rest), BF),
            pltpu.VMEM((experts, SLOTS, ne * wide), BF),
            pltpu.SemaphoreType.DMA((3, max(hidden // tile, ne))),
            pltpu.SemaphoreType.DMA((experts * (ne + 1) + ne,)),
            pltpu.SemaphoreType.DMA((ne, experts + 1)),
        ],
        vmem=60,
        out_specs=[HBM] * (ne + experts) + [VMEM],
        flops=6 * slots * D * hidden,
        moved=6 * D * hidden,
    )
    return values[:ne], values[ne:-1], values[-1]


def weigh_kernel(ne, experts, *refs):
    place, stats, routes, slots = refs[:4]
    blocks, late = refs[4 : 4 + experts], refs[4 + experts : 4 + experts + ne]
    refs = refs[4 + experts + ne :]
    outs, late_outs, (high, low, buf, total) = refs[:ne], refs[ne : ne + experts], refs[ne + experts :]
    rows = routes.shape[1]
    logits = stats[:8] * lax.rsqrt(stats[8:9] / D + EPSILON)
    ids = lax.broadcasted_iota(I32, (8, rows), 0)
    chosen = [
        jnp.sum(jnp.where(ids == routes[top : top + 1], logits, 0.0), axis=0, keepdims=True)
        for top in range(2)
    ]
    at = lax.broadcasted_iota(I32, (experts * SLOTS, rows), 0)
    gates = jnp.zeros(at.shape, F32)
    for top in range(2):
        gate = 1.0 / (1.0 + jnp.exp(chosen[1 - top] - chosen[top]))
        gates = gates + jnp.where(at == slots[top : top + 1], gate, 0.0)
    high[...], low[...] = halves(gates.T)
    for t in range(experts):
        buf[t * SLOTS : (t + 1) * SLOTS] = blocks[t][...]
    total[...] = pick(high[...], buf[...]) + pick(low[...], buf[...])
    wide = outs[0].shape[1]
    for s in range(ne):
        outs[s][...] = total[:, lanes((place[0] ^ s) * wide, wide)].astype(outs[s].dtype)
    late_sum = late[0][...].astype(F32)
    for block in late[1:]:
        late_sum = late_sum + block[...].astype(F32)
    for t in range(experts):
        late_outs[t][...] = late_sum[t * SLOTS : (t + 1) * SLOTS].astype(BF)


def finish_kernel(ne, experts, wide, *refs):
    high, low, hidden = refs[:3]
    early, late = refs[3 : 3 + ne], refs[3 + ne : 3 + ne + experts]
    out, buf = refs[3 + ne + experts :]
    first = hidden[:, :wide]
    for block in early:
        first = first + block[...].astype(F32)
    out[:, :wide] = first
    for t in range(experts):
        buf[t * SLOTS : (t + 1) * SLOTS] = late[t][...]
    out[:, wide:] = hidden[:, wide:] + pick(high[...], buf[...]) + pick(low[...], buf[...])


def body(
    attention_out,
    residual,
    w_out,
    router_w,
    norm_gain,
    page_pool,
    page_table,
    cache_len,
    came_from,
    routes,
    w_gate,
    w_up,
    w_down,
):
    n = lax.axis_size("req")
    ne = lax.axis_size("exp")
    me = lax.axis_index("req")
    ze = lax.axis_index("exp")
    half = n // 2
    q, k = me // 2, me % 2
    rows = attention_out.shape[0]
    feats = residual.shape[1]
    kblock = D // half
    experts = n // 2
    rest = max(128, feats * PART // 8 // 128 * 128)
    wide = feats - rest
    place = ze.reshape(1).astype(I32)

    pair_place = q.reshape(1).astype(I32)
    *attn_blocks, came_from = local_call(
        split_kernel,
        [SMEM, VMEM, VMEM],
        (pair_place, attention_out, came_from.reshape(n, rows)),
        [far((rows, kblock), BF)] * half + [shape((n, rows), I32)],
        vmem=60,
        moved=2 * MIB,
    )
    came_from = came_from.reshape(-1)
    attn_blocks = [attn_blocks[0]] + [swap(attn_blocks[s], "req", 2 * s) for s in range(1, half)]
    w_other = swap(w_out, "req", 1)

    n_pair, n_send = half * MIG, (2 * half - 1) * MIG
    n_hand = -(-(n_pair + 2 * MIG) // 16) * 16
    pair_rows, own_rows, send_row = local_call(
        functools.partial(movers_kernel, half),
        [SMEM] + [VMEM] * 3,
        (jnp.stack([q, k]).astype(I32), came_from.reshape(n, rows), attention_out, residual),
        [
            shape((n_pair, D + feats), BF),
            shape((2 * n_pair, feats), BF),
            shape((2 * n_pair, 128), I32),
        ],
        vmem=60,
        moved=2 * MIB,
        after=[w_other],
    )
    send_row = send_row[:n_send, 0]
    pair_rows = swap(pair_rows, "req", 1)
    *late_blocks, order = local_call(
        functools.partial(handover_kernel, half),
        [SMEM, VMEM, VMEM, VMEM],
        (pair_place, pair_rows, own_rows, came_from.reshape(n, rows)),
        [shape((n_hand, feats), BF)] * half + [shape((n, rows), I32)],
        moved=MIB,
    )
    late_blocks = [late_blocks[0]] + [swap(late_blocks[s], "req", 2 * s) for s in range(1, half)]
    came_from = order.reshape(-1)

    source = jnp.stack(
        [lax.dynamic_slice_in_dim(came_from, (2 * (q ^ t) + k) * rows, rows) for t in range(half)]
    )
    src_group, src_local = source // rows, source % rows
    src_rank = jnp.sum(
        (src_group[:, :, None] == src_group[:, None, :]) & (source[:, None, :] < source[:, :, None]),
        axis=2,
    )
    src_rel, src_par = (src_group // 2) ^ q, src_group % 2
    t_ids = jnp.arange(half, dtype=I32)[:, None]
    attn_at = jnp.where(
        src_par == k,
        src_rel * rows + src_local,
        half * rows + src_rel * n_hand + (t_ids ^ src_rel) * MIG + src_rank,
    ).reshape(-1)
    own_stays = src_group[0] == me
    own_slot = src_rel[0] * 2 * MIG + jnp.where(src_par[0] == k, 0, MIG) + src_rank[0]
    own_hand = src_rel[0] * n_hand + n_pair + jnp.where(src_par[0] == k, 0, MIG) + src_rank[0]
    own_at = jnp.where(own_stays, src_local[0], rows + own_hand)

    slot_pick, slot_of = local_call(
        functools.partial(slots_kernel, experts),
        [SMEM, VMEM],
        ((me % experts).reshape(1).astype(I32), routes.T),
        [shape((experts * SLOTS, rows), BF), shape((2, rows), I32)],
        after=[order],
    )

    total_rows = half * (rows + n_hand)
    selector = hot(attn_at, total_rows)
    resid_selector = hot(own_at, rows + half * n_hand)
    parts = local_call(
        functools.partial(project_kernel, half),
        [SMEM] + [VMEM] * 3 + [HBM] * (2 + half) + [VMEM] * half,
        (
            k.reshape(1).astype(I32),
            selector,
            resid_selector,
            residual,
            w_out,
            w_other,
            *attn_blocks,
            *late_blocks,
        ),
        [shape((rows, feats), F32)] + [shape((rows, feats), BF)] * (half - 1),
        [
            pltpu.VMEM((total_rows, kblock), BF),
            pltpu.VMEM((2,) + w_out.shape, BF),
            pltpu.SemaphoreType.DMA((half + 2,)),
        ],
        vmem=58,
        flops=2 * half * rows * (total_rows + feats) * kblock,
        moved=6 * MIB,
    )
    parts = [parts[0]] + [swap(parts[s], "req", 2 * s) for s in range(1, half)]

    table = page_table.reshape(-1)
    none = jnp.full((n_send,), -1, I32)
    no_rows = page_pool[:2].reshape((1, 2) + page_pool.shape[1:])
    moving = take_pages(page_pool, no_rows, send_row, none, table, cache_len, [order])
    page = moving.shape[1:]
    pair_pages = swap(moving[:n_pair], "req", 1).reshape((half, MIG) + page)
    own_pages = jnp.concatenate([moving[:MIG], moving[n_pair:]], axis=0).reshape((half, MIG) + page)
    pages = jnp.concatenate([own_pages, pair_pages], axis=1)
    stages = half.bit_length() - 1
    block = pages.shape[1:]
    pages = pages.reshape((half // 2, 2) + block)
    page_rows = pages[:, 1].reshape(-1, page[-1])

    router = jnp.pad(router_w.T, ((0, 8 - experts), (0, 0)))
    late_shapes = [(SLOTS, rest)] * experts
    late_shapes[2] = (SLOTS + page_rows.shape[0], page[-1])
    normed = local_call(
        functools.partial(norm_kernel, half, experts, wide),
        [VMEM] * (4 + half),
        (norm_gain[None, :], router, slot_pick, page_rows, *parts),
        [shape((rows, feats), F32), far((rows + 16, wide), BF)]
        + [far(dims, BF) for dims in late_shapes],
        flops=2 * experts * SLOTS * rows * rest,
        moved=3 * MIB,
    )
    hidden, early = normed[:2]
    late = [normed[2 + s] if s == 0 else swap(normed[2 + s], "req", s) for s in range(experts)]
    early_blocks = [early] + [swap(early, "exp", s) for s in range(1, ne)]
    came_pages = late[2][SLOTS:].reshape((half // 2,) + block)
    pages = jnp.stack([pages[:, 0], came_pages], axis=1)
    outgoing = local_call(
        functools.partial(dispatch_kernel, ne, experts),
        [SMEM] + [VMEM] * (1 + ne + experts),
        (place, slot_pick, *early_blocks, *late),
        [far((SLOTS, ne * wide + 128), BF)] * experts
        + [shape((16, rows), F32), far((experts * SLOTS, rest), BF)],
        vmem=60,
        flops=2 * experts * SLOTS * rows * ne * wide,
        moved=3 * MIB,
    )
    late = outgoing[experts + 1]
    late_rows = [late] + [swap(late, "exp", s) for s in range(1, ne)]

    early_rows = [swap(outgoing[s], "req", s) if s else outgoing[s] for s in range(experts)]

    for bit in range(1, stages):
        pages = pages.reshape((half >> (bit + 1), 2, 1 << bit) + block)
        came_pages = swap(pages[:, 1], "req", 2 << bit)
        pages = jnp.stack([pages[:, 0], came_pages], axis=1)
    moved_pages = pages.reshape((half * 2 * MIG,) + page)

    down_late, down_early, stats = expert_call(
        place, early_rows, late_rows, w_gate, w_up, w_down, outgoing[experts], ne
    )
    late_blocks = [down_late[0]] + [swap(down_late[s], "exp", s) for s in range(1, ne)]
    near_back = hold(down_early[1], late_blocks[1])
    early_back = [
        swap(down_early[s] if s > 1 else near_back, "req", s) if s else down_early[s]
        for s in range(experts)
    ]
    new_pages = take_pages(
        page_pool,
        moved_pages,
        jnp.where(own_stays, src_local[0], 0),
        jnp.where(own_stays, -1, own_slot),
        table,
        cache_len,
        [stats],
    )
    weighted = local_call(
        functools.partial(weigh_kernel, ne, experts),
        [SMEM] + [VMEM] * (3 + experts + ne),
        (place, stats, routes.T, slot_of, *early_back, *late_blocks),
        [shape((rows, wide), F32)]
        + [shape((rows, wide), BF)] * (ne - 1)
        + [shape((SLOTS, rest), BF)] * experts
        + [shape((rows, experts * SLOTS), BF)] * 2,
        [pltpu.VMEM((experts * SLOTS, ne * wide), BF), pltpu.VMEM((rows, ne * wide), F32)],
        flops=4 * rows * experts * SLOTS * ne * wide,
        moved=3 * MIB,
    )
    early_parts = [weighted[0]] + [swap(weighted[s], "exp", s) for s in range(1, ne)]
    late_back = [
        swap(weighted[ne + s], "req", s) if s else weighted[ne] for s in range(experts)
    ]
    mixed = local_call(
        functools.partial(finish_kernel, ne, experts, wide),
        [VMEM] * (3 + ne + experts),
        (*weighted[-2:], hidden, *early_parts, *late_back),
        [shape((rows, feats), F32)],
        [pltpu.VMEM((experts * SLOTS, rest), BF)],
        flops=4 * rows * experts * SLOTS * rest,
        moved=2 * MIB,
    )[0]

    return (mixed, new_pages)


def solution(mesh):
    in_specs = (
        P("req", None),
        P("req", "exp"),
        P("req", "exp"),
        P("exp", None),
        P("exp"),
        P("req", None, "exp"),
        P("req", None),
        P("req"),
        P(),
        P("req", None),
        P("req", None, "exp"),
        P("req", None, "exp"),
        P("req", "exp", None),
    )
    out_specs = (P("req", "exp"), P("req", None, None, "exp"))
    return jax.shard_map(body, mesh=mesh, in_specs=in_specs, out_specs=out_specs, check_vma=False)
```

```python
import functools

import jax
import jax.numpy as jnp
from jax import lax
from jax.experimental import pallas as pl
from jax.experimental.pallas import tpu as pltpu
from jax.sharding import PartitionSpec as P

D = 4096
SLOTS = 64
PART = 3
AHEAD = 3
MIG = 4
EPSILON = 1e-05
BF = jnp.bfloat16
F32 = jnp.float32
I32 = jnp.int32
MIB = 2**20
VMEM = pl.BlockSpec(memory_space=pltpu.VMEM)
SMEM = pl.BlockSpec(memory_space=pltpu.SMEM)
HBM = pl.BlockSpec(memory_space=pltpu.HBM)
ANY = pl.BlockSpec(memory_space=pl.ANY)


def swap(x, axis, s):
    n = lax.axis_size(axis)
    return lax.ppermute(x, axis, [(i, i ^ s) for i in range(n)])


def hot(index, count):
    return (index[..., None] == jnp.arange(count, dtype=I32)).astype(BF)


def pick(selector, rows):
    return jnp.dot(selector, rows, preferred_element_type=F32)


def lanes(start, width):
    return pl.ds(pl.multiple_of(start, 128), width)


def local_call(kernel, in_specs, args, outs, scratch=(), vmem=16, flops=0, moved=0, after=(), out_specs=None):
    count, waits = len(args), tuple(after)

    def run(*refs):
        kernel(*refs[:count], *refs[count + len(waits) :])

    return pl.pallas_call(
        run,
        out_shape=outs,
        in_specs=list(in_specs) + [pl.BlockSpec(memory_space=pl.ANY)] * len(waits),
        out_specs=out_specs or [VMEM] * len(outs),
        scratch_shapes=list(scratch),
        compiler_params=pltpu.CompilerParams(vmem_limit_bytes=vmem * MIB),
        cost_estimate=pl.CostEstimate(flops=flops, bytes_accessed=moved, transcendentals=0),
    )(*args, *waits)


def shape(dims, dtype):
    return jax.ShapeDtypeStruct(dims, dtype)


def near(dims, dtype):
    return pltpu.VMEM(dims, dtype)


def far(dims, dtype):
    return pltpu.HBM(dims, dtype)


def page_kernel(pool, moved, rows, slot, table, length, out):
    count, pages, page_len, width = out.shape
    token = lax.broadcasted_iota(I32, (page_len, width), 0)

    @pl.loop(0, count)
    def _(j):
        at = slot[j]

        @pl.when(at >= 0)
        def _():
            for p in range(pages):
                out[j, p] = moved[at, p]

        @pl.when(at < 0)
        def _():
            i = rows[j]
            for p in range(pages):
                page = pool[table[p, i]].astype(F32)
                out[j, p] = jnp.where(token + p * page_len < length[i], page, 0.0).astype(out.dtype)


def send_pages_kernel(pool, rows, table, length, out):
    count, pages, page_len, width = out.shape
    position = lax.broadcasted_iota(I32, (page_len, width), 0)

    @pl.loop(0, count)
    def _(j):
        i = rows[j, 0]
        for p in range(pages):
            page = pool[table[p, i]].astype(F32)
            out[j, p] = jnp.where(position + p * page_len < length[i], page, 0.0).astype(out.dtype)


def take_pages(pool, moved, rows, slot, table, length, after=()):
    outs = [shape(slot.shape + table.shape[:1] + pool.shape[1:], pool.dtype)]
    args = (pool, moved, rows, slot, table, length)
    return local_call(page_kernel, [VMEM] * 2 + [SMEM] * 4, args, outs, moved=5 * MIB, after=after)[0]


def movers_kernel(half, spot, order, attention, residual, *outs):
    chip, side = spot[0] // 2, spot[0] % 2
    pair, own, row_out = outs[half:]
    for s, block in enumerate(outs[:half]):
        width = block.shape[1]
        block[...] = attention[:, lanes((chip ^ s) * width, width)]
    n, rows = order.shape
    down, across = (lax.broadcasted_iota(I32, (rows, rows), d) for d in (0, 1))
    mine = spot[0] * rows + down
    found = jnp.zeros((rows, rows), F32)
    for g in range(1, n):
        found = found + jnp.where(order[g : g + 1] == mine, float(g), 0.0)
    dest = jnp.broadcast_to(jnp.sum(found, axis=1, keepdims=True), (rows, rows))
    dest_row = dest.T
    rank = jnp.sum(jnp.where((dest == dest_row) & (down < across), 1.0, 0.0), axis=0, keepdims=True)
    rank = rank.astype(I32)
    to = dest_row[:1].astype(I32)
    far_off, core = (to >> 1) ^ chip, to & 1
    kept = jnp.where(far_off != 0, (half + far_off - 1) * MIG + rank, -1)
    slot = jnp.where(core != side, far_off * MIG + rank, kept)
    chosen = lax.broadcasted_iota(I32, (own.shape[0], rows), 0) == slot
    selector = jnp.where(chosen, 1.0, 0.0)
    numbers = lax.broadcasted_iota(I32, selector.shape, 1).astype(F32)
    number = jnp.sum(selector * numbers, axis=1, keepdims=True)
    row_out[...] = jnp.broadcast_to(number, row_out.shape).astype(I32)
    selector = selector.astype(BF)
    n_pair = pair.shape[0]
    pair[:, : attention.shape[1]] = pick(selector[:n_pair], attention[...]).astype(BF)
    moving = pick(selector, residual[...]).astype(BF)
    pair[:, attention.shape[1] :] = moving[:n_pair]
    own[...] = moving


def handover_kernel(half, place, pair, own, order, *outs):
    outs[-1][...] = order[...]
    outs = outs[:-1]
    n_pair = half * MIG
    width = own.shape[1]
    for s, out in enumerate(outs):
        first = own[n_pair + (s - 1) * MIG : n_pair + s * MIG] if s else own[:MIG]
        second = pair[s * MIG : (s + 1) * MIG, half * width :]
        blank = jnp.zeros((out.shape[0] - n_pair - 2 * MIG, width), BF)
        columns = pair[:, lanes((place[0] ^ s) * width, width)]
        out[...] = jnp.concatenate([columns, first, second, blank], axis=0)


def slots_kernel(experts, spot, routes, picked, slots):
    rows = routes.shape[1]
    ids = lax.broadcasted_iota(I32, (8, rows), 0)
    named = jnp.where((ids == routes[0:1]) | (ids == routes[1:2]), 1.0, 0.0)
    down, across = (lax.broadcasted_iota(I32, (rows, rows), d) for d in (0, 1))
    before = pick(named.astype(BF), jnp.where(down < across, 1.0, 0.0).astype(BF))
    at = lax.broadcasted_iota(I32, picked.shape, 0)
    chosen = jnp.zeros(picked.shape, F32)
    for top in range(2):
        route = routes[top : top + 1]
        rank = jnp.sum(jnp.where(ids == route, before, 0.0), axis=0, keepdims=True).astype(I32)
        slot = (route ^ spot[0]) * SLOTS + rank
        slots[top : top + 1] = slot
        chosen = chosen + jnp.where(at == slot, 1.0, 0.0)
    picked[...] = chosen.astype(BF)


def project_kernel(half, *refs):
    odd, selector_far, resid_selector, residual, own, other = refs[:6]
    blocks = refs[6 : 6 + 2 * half]
    outs = refs[6 + 2 * half : 6 + 3 * half]
    buf, weights, selector, sems = refs[6 + 3 * half :]
    rows = residual.shape[0]
    copies = [
        pltpu.make_async_copy(blocks[s], buf.at[pl.ds(s * rows, rows)], sems.at[s])
        for s in range(half)
    ]
    copies.append(pltpu.make_async_copy(selector_far, selector, sems.at[half + 2]))
    fetches = [
        pltpu.make_async_copy(own, weights.at[odd[0]], sems.at[half]),
        pltpu.make_async_copy(other, weights.at[1 - odd[0]], sems.at[half + 1]),
    ]
    for copy in copies + fetches:
        copy.start()
    at = half * rows
    for block in blocks[half:]:
        buf[at : at + block.shape[0]] = block[...]
        at += block.shape[0]
    resid = pick(resid_selector[:, :rows], residual[...])
    resid = resid + pick(resid_selector[:, rows:], buf[half * rows :])
    for copy in copies:
        copy.wait()
    picked = pick(selector[...], buf[...]).astype(BF)
    for copy in fetches:
        copy.wait()
    depth = own.shape[0]
    product = pick(picked[:, :depth], weights[0]) + pick(picked[:, depth:], weights[1])
    outs[0][...] = resid + product[:rows]
    for t in range(1, half):
        outs[t][...] = product[t * rows : (t + 1) * rows].astype(BF)


def halves(x):
    high = x.astype(BF)
    return high, (x - high.astype(F32)).astype(BF)


def norm_kernel(half, experts, wide, *refs):
    gain, router, selector, pages = refs[:4]
    parts = refs[4 : 4 + half]
    hidden_out, early = refs[4 + half : 6 + half]
    late = refs[6 + half :]
    hidden = parts[0][...]
    for part in parts[1:]:
        hidden = hidden + part[...].astype(F32)
    hidden_out[...] = hidden
    scaled = hidden * gain[...]
    rows = hidden.shape[0]
    lane = lax.broadcasted_iota(I32, (rows, 128), 1)
    stats = jnp.where(lane == 8, jnp.sum(hidden * hidden, axis=1, keepdims=True), 0.0)
    for e in range(experts):
        logit = jnp.sum(scaled * router[e : e + 1], axis=1, keepdims=True)
        stats = jnp.where(lane == e, logit, stats)
    stats = stats.T[: early.shape[0] - rows]
    scaled = scaled.astype(BF)
    early[:rows] = scaled[:, :wide]
    high, low = halves(stats)
    early[rows:] = jnp.zeros((early.shape[0] - rows, wide), BF)
    early[rows:, :rows] = high
    early[rows:, rows : 2 * rows] = low
    chosen = pick(selector[...], scaled[:, wide:]).astype(BF)
    for s in range(experts):
        late[s][:SLOTS, : chosen.shape[1]] = chosen[s * SLOTS : (s + 1) * SLOTS]
    late[2][SLOTS:] = pages[...]


def hold_kernel(x, out):
    out[...] = x[...]


def hold(x, after):
    return local_call(hold_kernel, [VMEM], (x,), [far(x.shape, x.dtype)], after=[after])[0]


def dispatch_kernel(ne, experts, *refs):
    place, selector = refs[:2]
    blocks, late, refs = refs[2 : 2 + ne], refs[2 + ne : 2 + ne + experts], refs[2 + ne + experts :]
    outs, stats_out, late_out = refs[:experts], refs[experts], refs[experts + 1]
    for t in range(experts):
        late_out[t * SLOTS : (t + 1) * SLOTS] = late[t][:SLOTS, : late_out.shape[1]]
    wide = blocks[0].shape[1]
    rows = selector.shape[1]
    stats = jnp.zeros(stats_out.shape, F32)
    for block in blocks:
        stats = stats + block[rows:, :rows].astype(F32) + block[rows:, rows : 2 * rows].astype(F32)
    stats_out[...] = stats
    inverse = lax.rsqrt(stats[stats.shape[0] // 2 :][:1] / D + EPSILON)
    scale = jnp.sum(selector[...].astype(F32) * inverse, axis=1, keepdims=True)
    high, low = halves(scale)
    lane = lax.broadcasted_iota(I32, (scale.shape[0], 128), 1)
    scale = jnp.where(lane == 0, high.astype(F32), jnp.where(lane == 1, low.astype(F32), 0.0)).astype(BF)
    for t in range(experts):
        outs[t][:, ne * wide :] = scale[t * SLOTS : (t + 1) * SLOTS]
    for s in range(ne):
        chosen = pick(selector[...], blocks[s][:rows]).astype(BF)
        columns = lanes((place[0] ^ s) * wide, wide)
        for t in range(experts):
            outs[t][:, columns] = chosen[t * SLOTS : (t + 1) * SLOTS]


def expert_kernel(ne, experts, tile, spot, *refs):
    early, late = refs[:experts], refs[experts : experts + ne]
    gate, up, down, stats = refs[experts + ne : experts + ne + 4]
    refs = refs[experts + ne + 4 :]
    late_out, early_out = refs[:ne], refs[ne : ne + experts]
    stats_out = refs[ne + experts]
    rows, pieces, active, gate_buf, up_buf, down_buf, late_buf, early_buf = refs[ne + experts + 1 : -3]
    sems, load_sems, out_sems = refs[-3:]
    place = spot[0]
    rest = late[0].shape[1]
    wide = (early[0].shape[1] - 128) // ne
    feats = wide + rest
    tiles = gate.shape[2] // tile

    def copies(f):
        columns = lanes(f * tile, tile)
        return [
            pltpu.make_async_copy(gate.at[0, :, columns], gate_buf.at[:, columns], sems.at[0, f]),
            pltpu.make_async_copy(up.at[0, :, columns], up_buf.at[:, columns], sems.at[1, f]),
        ]

    def down_copy(e):
        return pltpu.make_async_copy(down.at[0, :, lanes(e * feats, feats)], down_buf.at[e], sems.at[2, e])

    def early_copy(e, t):
        columns = lanes(e * wide, wide)
        return pltpu.make_async_copy(
            early_buf.at[t, :, columns], early_out[t].at[:, columns], out_sems.at[e, t]
        )

    def late_copy(e, s):
        return pltpu.make_async_copy(late_buf.at[e], late_out[s], out_sems.at[e, experts])

    def start(unit):
        @pl.when(unit < tiles)
        def _():
            for copy in copies(unit):
                copy.start()

        @pl.when((unit >= tiles) & (unit < tiles + ne))
        def _():
            down_copy(unit - tiles).start()

    loads = []

    def load(source, target):
        loads.append(pltpu.make_async_copy(source, target, load_sems.at[len(loads)]))

    for t in range(experts):
        at = pl.ds(t * SLOTS, SLOTS)
        load(early[t].at[:, pl.ds(ne * wide, 128)], pieces.at[at])
        for e in range(ne):
            load(early[t].at[:, pl.ds(e * wide, wide)], rows.at[at, pl.ds(e * feats, wide)])
    for s in range(ne):
        load(late[s], rows.at[:, lanes((place ^ s) * feats + wide, rest)])
    for copy in loads:
        copy.start()
    start(jnp.int32(0))
    stats_out[...] = stats[...]
    for copy in loads:
        copy.wait()
    for unit in range(1, AHEAD):
        start(jnp.int32(unit))
    scale = pieces[:, :1].astype(F32) + pieces[:, 1:2].astype(F32)

    @pl.loop(0, tiles)
    def _(f):
        for copy in copies(f):
            copy.wait()
        start(f + AHEAD)
        columns = lanes(f * tile, tile)
        gate_h = pick(rows[...], gate_buf[:, columns]) * scale
        up_h = pick(rows[...], up_buf[:, columns]) * scale
        active[:, columns] = (gate_h / (1.0 + jnp.exp(-gate_h)) * up_h).astype(BF)

    @pl.loop(0, ne)
    def _(e):
        down_copy(e).wait()
        start(e + tiles + AHEAD)
        value = pick(active[...], down_buf[e]).astype(BF)
        late_buf[e] = value[:, wide:]
        for t in range(experts):
            early_buf[t, :, lanes(e * wide, wide)] = value[t * SLOTS : (t + 1) * SLOTS, :wide]
            early_copy(e, t).start()
        for s in range(ne):

            @pl.when(e ^ place == s)
            def _():
                late_copy(e, s).start()

    @pl.loop(0, ne)
    def _(e):
        late_copy(e, 0).wait()
        for t in range(experts):
            early_copy(e, t).wait()


def expert_call(place, early, late, w_gate, w_up, w_down, stats, ne, after):
    hidden = w_gate.shape[2]
    slots, rest = late[0].shape
    experts = len(early)
    wide = (early[0].shape[1] - 128) // ne
    tile = 256 if hidden % 256 == 0 else 128
    values = local_call(
        functools.partial(expert_kernel, ne, experts, tile),
        [SMEM] + [HBM] * (experts + ne + 3) + [VMEM],
        (place, *early, *late, w_gate, w_up, w_down, stats),
        [near((slots, rest), BF)]
        + [far((slots, rest), BF)] * (ne - 1)
        + [near((SLOTS, ne * wide), BF)]
        + [far((SLOTS, ne * wide), BF)] * (experts - 1)
        + [near(stats.shape, F32)],
        [
            pltpu.VMEM((slots, D), BF),
            pltpu.VMEM((slots, 128), BF),
            pltpu.VMEM((slots, hidden), BF),
            pltpu.VMEM((D, hidden), BF),
            pltpu.VMEM((D, hidden), BF),
            pltpu.VMEM((ne, hidden, wide + rest), BF),
            pltpu.VMEM((ne, slots, rest), BF),
            pltpu.VMEM((experts, SLOTS, ne * wide), BF),
            pltpu.SemaphoreType.DMA((3, max(hidden // tile, ne))),
            pltpu.SemaphoreType.DMA((experts * (ne + 1) + ne,)),
            pltpu.SemaphoreType.DMA((ne, experts + 1)),
        ],
        vmem=60,
        out_specs=[ANY] + [HBM] * (ne - 1) + [ANY] + [HBM] * (experts - 1) + [VMEM],
        after=[after],
        flops=6 * slots * D * hidden,
        moved=6 * D * hidden,
    )
    return values[:ne], values[ne:-1], values[-1]


def weigh_kernel(ne, experts, *refs):
    place, stats, routes, slots = refs[:4]
    blocks, late = refs[4 : 4 + experts], refs[4 + experts : 4 + experts + ne]
    refs = refs[4 + experts + ne :]
    outs, late_outs, (high, low, buf, total) = refs[:ne], refs[ne : ne + experts], refs[ne + experts :]
    rows = routes.shape[1]
    logits = stats[:8] * lax.rsqrt(stats[8:9] / D + EPSILON)
    ids = lax.broadcasted_iota(I32, (8, rows), 0)
    chosen = [
        jnp.sum(jnp.where(ids == routes[top : top + 1], logits, 0.0), axis=0, keepdims=True)
        for top in range(2)
    ]
    at = lax.broadcasted_iota(I32, (experts * SLOTS, rows), 0)
    gates = jnp.zeros(at.shape, F32)
    for top in range(2):
        gate = 1.0 / (1.0 + jnp.exp(chosen[1 - top] - chosen[top]))
        gates = gates + jnp.where(at == slots[top : top + 1], gate, 0.0)
    high[...], low[...] = halves(gates.T)
    for t in range(experts):
        buf[t * SLOTS : (t + 1) * SLOTS] = blocks[t][...]
    total[...] = pick(high[...], buf[...]) + pick(low[...], buf[...])
    wide = outs[0].shape[1]
    for s in range(ne):
        outs[s][...] = total[:, lanes((place[0] ^ s) * wide, wide)].astype(outs[s].dtype)
    late_sum = late[0][...].astype(F32)
    for block in late[1:]:
        late_sum = late_sum + block[...].astype(F32)
    for t in range(experts):
        late_outs[t][...] = late_sum[t * SLOTS : (t + 1) * SLOTS].astype(BF)


def finish_kernel(ne, experts, wide, *refs):
    high, low, hidden = refs[:3]
    early, late = refs[3 : 3 + ne], refs[3 + ne : 3 + ne + experts]
    out, buf = refs[3 + ne + experts :]
    first = hidden[:, :wide]
    for block in early:
        first = first + block[...].astype(F32)
    out[:, :wide] = first
    for t in range(experts):
        buf[t * SLOTS : (t + 1) * SLOTS] = late[t][...]
    out[:, wide:] = hidden[:, wide:] + pick(high[...], buf[...]) + pick(low[...], buf[...])


def body(
    attention_out,
    residual,
    w_out,
    router_w,
    norm_gain,
    page_pool,
    page_table,
    cache_len,
    came_from,
    routes,
    w_gate,
    w_up,
    w_down,
):
    n = lax.axis_size("req")
    ne = lax.axis_size("exp")
    me = lax.axis_index("req")
    ze = lax.axis_index("exp")
    half = n // 2
    q, k = me // 2, me % 2
    rows = attention_out.shape[0]
    feats = residual.shape[1]
    kblock = D // half
    experts = n // 2
    rest = max(128, feats * PART // 8 // 128 * 128)
    wide = feats - rest
    place = ze.reshape(1).astype(I32)

    pair_place = q.reshape(1).astype(I32)
    n_pair, n_send = half * MIG, (2 * half - 1) * MIG
    n_hand = -(-(n_pair + 2 * MIG) // 16) * 16
    *attn_blocks, pair_rows, own_rows, send_row = local_call(
        functools.partial(movers_kernel, half),
        [SMEM] + [VMEM] * 3,
        (me.reshape(1).astype(I32), came_from.reshape(n, rows), attention_out, residual),
        [far((rows, kblock), BF)] * half
        + [
            far((n_pair, D + feats), BF),
            far((2 * n_pair, feats), BF),
            shape((2 * n_pair, 128), I32),
        ],
        vmem=60,
        moved=2 * MIB,
    )
    attn_blocks = [attn_blocks[0]] + [swap(attn_blocks[s], "req", 2 * s) for s in range(1, half)]
    w_other = swap(w_out, "req", 1)
    pair_rows = swap(pair_rows, "req", 1)
    *late_blocks, order = local_call(
        functools.partial(handover_kernel, half),
        [SMEM, VMEM, VMEM, VMEM],
        (pair_place, pair_rows, own_rows, came_from.reshape(n, rows)),
        [far((n_hand, feats), BF)] * half + [shape((n, rows), I32)],
        vmem=60,
        moved=MIB,
        after=[w_other],
    )
    late_blocks = [late_blocks[0]] + [swap(late_blocks[s], "req", 2 * s) for s in range(1, half)]
    came_from = order.reshape(-1)

    source = jnp.stack(
        [lax.dynamic_slice_in_dim(came_from, (2 * (q ^ t) + k) * rows, rows) for t in range(half)]
    )
    src_group, src_local = source // rows, source % rows
    src_rank = jnp.sum(
        (src_group[:, :, None] == src_group[:, None, :]) & (source[:, None, :] < source[:, :, None]),
        axis=2,
    )
    src_rel, src_par = (src_group // 2) ^ q, src_group % 2
    t_ids = jnp.arange(half, dtype=I32)[:, None]
    attn_at = jnp.where(
        src_par == k,
        src_rel * rows + src_local,
        half * rows + src_rel * n_hand + (t_ids ^ src_rel) * MIG + src_rank,
    ).reshape(-1)
    own_stays = src_group[0] == me
    own_slot = src_rel[0] * 2 * MIG + jnp.where(src_par[0] == k, 0, MIG) + src_rank[0]
    own_hand = src_rel[0] * n_hand + n_pair + jnp.where(src_par[0] == k, 0, MIG) + src_rank[0]
    own_at = jnp.where(own_stays, src_local[0], rows + own_hand)

    slot_pick, slot_of = local_call(
        functools.partial(slots_kernel, experts),
        [SMEM, VMEM],
        ((me % experts).reshape(1).astype(I32), routes.T),
        [shape((experts * SLOTS, rows), BF), shape((2, rows), I32)],
        after=[order],
    )

    total_rows = half * (rows + n_hand)
    selector = hot(attn_at, total_rows)
    resid_selector = hot(own_at, rows + half * n_hand)
    parts = local_call(
        functools.partial(project_kernel, half),
        [SMEM, HBM] + [VMEM] * 2 + [HBM] * (2 + half) + [VMEM] * half,
        (
            k.reshape(1).astype(I32),
            selector,
            resid_selector,
            residual,
            w_out,
            w_other,
            *attn_blocks,
            *late_blocks,
        ),
        [shape((rows, feats), F32)] + [shape((rows, feats), BF)] * (half - 1),
        [
            pltpu.VMEM((total_rows, kblock), BF),
            pltpu.VMEM((2,) + w_out.shape, BF),
            pltpu.VMEM(selector.shape, BF),
            pltpu.SemaphoreType.DMA((half + 3,)),
        ],
        vmem=58,
        flops=2 * half * rows * (total_rows + feats) * kblock,
        moved=6 * MIB,
    )
    parts = [parts[0]] + [swap(parts[s], "req", 2 * s) for s in range(1, half)]

    table = page_table.T
    moving = local_call(
        send_pages_kernel,
        [VMEM] + [SMEM] * 3,
        (page_pool, send_row, table, cache_len),
        [shape((n_send,) + table.shape[:1] + page_pool.shape[1:], BF)],
        moved=3 * MIB,
        after=[order],
    )[0]
    page = moving.shape[1:]
    pair_pages = swap(moving[:n_pair], "req", 1).reshape((half, MIG) + page)
    own_pages = jnp.concatenate([moving[:MIG], moving[n_pair:]], axis=0).reshape((half, MIG) + page)
    pages = jnp.concatenate([own_pages, pair_pages], axis=1)
    stages = half.bit_length() - 1
    block = pages.shape[1:]
    pages = pages.reshape((half // 2, 2) + block)
    page_rows = pages[:, 1].reshape(-1, page[-1])

    router = jnp.pad(router_w.T, ((0, 8 - experts), (0, 0)))
    late_shapes = [(SLOTS, rest)] * experts
    late_shapes[2] = (SLOTS + page_rows.shape[0], page[-1])
    normed = local_call(
        functools.partial(norm_kernel, half, experts, wide),
        [VMEM] * (4 + half),
        (norm_gain[None, :], router, slot_pick, page_rows, *parts),
        [far((rows, feats), F32), far((rows + 16, wide), BF)]
        + [far(dims, BF) for dims in late_shapes],
        flops=2 * experts * SLOTS * rows * rest,
        moved=3 * MIB,
    )
    hidden, early = normed[:2]
    late = [normed[2 + s] if s == 0 else swap(normed[2 + s], "req", s) for s in range(experts)]
    early_blocks = [early] + [swap(early, "exp", s) for s in range(1, ne)]
    came_pages = late[2][SLOTS:].reshape((half // 2,) + block)
    pages = jnp.stack([pages[:, 0], came_pages], axis=1)
    outgoing = local_call(
        functools.partial(dispatch_kernel, ne, experts),
        [SMEM] + [VMEM] * (1 + ne + experts),
        (place, slot_pick, *early_blocks, *late),
        [far((SLOTS, ne * wide + 128), BF)]
        + [near((SLOTS, ne * wide + 128), BF)] * (experts - 1)
        + [near((16, rows), F32), far((experts * SLOTS, rest), BF)],
        vmem=60,
        flops=2 * experts * SLOTS * rows * ne * wide,
        moved=3 * MIB,
    )
    late = outgoing[experts + 1]
    late_rows = [late] + [swap(late, "exp", s) for s in range(1, ne)]

    early_rows = [swap(outgoing[s], "req", s) if s else outgoing[s] for s in range(experts)]

    crossing = pages
    for bit in range(1, stages):
        pages = pages.reshape((half >> (bit + 1), 2, 1 << bit) + block)
        came_pages = swap(pages[:, 1], "req", 2 << bit)
        pages = jnp.stack([pages[:, 0], came_pages], axis=1)
    moved_pages = pages.reshape((half * 2 * MIG,) + page)

    down_late, down_early, stats = expert_call(
        place, early_rows, late_rows, w_gate, w_up, w_down, outgoing[experts], ne, crossing
    )
    late_blocks = [down_late[0]] + [swap(down_late[s], "exp", s) for s in range(1, ne)]
    near_back = hold(down_early[1], late_blocks[-1])
    early_back = [
        swap(down_early[s] if s > 1 else near_back, "req", s) if s else down_early[s]
        for s in range(experts)
    ]
    new_pages = take_pages(
        page_pool,
        moved_pages,
        jnp.where(own_stays, src_local[0], 0),
        jnp.where(own_stays, -1, own_slot),
        table,
        cache_len,
        [stats],
    )
    weighted = local_call(
        functools.partial(weigh_kernel, ne, experts),
        [SMEM] + [VMEM] * (3 + experts + ne),
        (place, stats, routes.T, slot_of, *early_back, *late_blocks),
        [shape((rows, wide), F32)]
        + [shape((rows, wide), BF)] * (ne - 1)
        + [shape((SLOTS, rest), BF)] * experts
        + [shape((rows, experts * SLOTS), BF)] * 2,
        [pltpu.VMEM((experts * SLOTS, ne * wide), BF), pltpu.VMEM((rows, ne * wide), F32)],
        flops=4 * rows * experts * SLOTS * ne * wide,
        moved=3 * MIB,
    )
    early_parts = [swap(weighted[s], "exp", s) for s in range(ne - 1, 0, -1)]
    early_parts = [weighted[0]] + early_parts[::-1]
    late_back = [
        swap(weighted[ne + s], "req", s) if s else weighted[ne] for s in range(experts)
    ]
    mixed = local_call(
        functools.partial(finish_kernel, ne, experts, wide),
        [VMEM] * (3 + ne + experts),
        (*weighted[-2:], hidden, *early_parts, *late_back),
        [shape((rows, feats), F32)],
        [pltpu.VMEM((experts * SLOTS, rest), BF)],
        flops=4 * rows * experts * SLOTS * rest,
        moved=2 * MIB,
    )[0]

    return (mixed, new_pages)


def solution(mesh):
    in_specs = (
        P("req", None),
        P("req", "exp"),
        P("req", "exp"),
        P("exp", None),
        P("exp"),
        P("req", None, "exp"),
        P("req", None),
        P("req"),
        P(),
        P("req", None),
        P("req", None, "exp"),
        P("req", None, "exp"),
        P("req", "exp", None),
    )
    out_specs = (P("req", "exp"), P("req", None, None, "exp"))
    return jax.shard_map(body, mesh=mesh, in_specs=in_specs, out_specs=out_specs, check_vma=False)
```

```python
import functools

import jax
import jax.numpy as jnp
from jax import lax
from jax.experimental import pallas as pl
from jax.experimental.pallas import tpu as pltpu
from jax.sharding import PartitionSpec as P

D = 4096
SLOTS = 64
PART = 3
AHEAD = 3
MIG = 4
EPSILON = 1e-05
BF = jnp.bfloat16
F32 = jnp.float32
I32 = jnp.int32
MIB = 2**20
VMEM = pl.BlockSpec(memory_space=pltpu.VMEM)
SMEM = pl.BlockSpec(memory_space=pltpu.SMEM)
HBM = pl.BlockSpec(memory_space=pltpu.HBM)
ANY = pl.BlockSpec(memory_space=pl.ANY)


def swap(x, axis, s):
    n = lax.axis_size(axis)
    return lax.ppermute(x, axis, [(i, i ^ s) for i in range(n)])


def hot(index, count):
    return (index[..., None] == jnp.arange(count, dtype=I32)).astype(BF)


def pick(selector, rows):
    return jnp.dot(selector, rows, preferred_element_type=F32)


def lanes(start, width):
    return pl.ds(pl.multiple_of(start, 128), width)


def local_call(kernel, in_specs, args, outs, scratch=(), vmem=16, flops=0, moved=0, after=(), out_specs=None):
    count, waits = len(args), tuple(after)

    def run(*refs):
        kernel(*refs[:count], *refs[count + len(waits) :])

    return pl.pallas_call(
        run,
        out_shape=outs,
        in_specs=list(in_specs) + [pl.BlockSpec(memory_space=pl.ANY)] * len(waits),
        out_specs=out_specs or [VMEM] * len(outs),
        scratch_shapes=list(scratch),
        compiler_params=pltpu.CompilerParams(vmem_limit_bytes=vmem * MIB),
        cost_estimate=pl.CostEstimate(flops=flops, bytes_accessed=moved, transcendentals=0),
    )(*args, *waits)


def shape(dims, dtype):
    return jax.ShapeDtypeStruct(dims, dtype)


def near(dims, dtype):
    return pltpu.VMEM(dims, dtype)


def far(dims, dtype):
    return pltpu.HBM(dims, dtype)


def page_kernel(pool, moved, rows, slot, table, length, out):
    count, pages, page_len, width = out.shape
    token = lax.broadcasted_iota(I32, (page_len, width), 0)

    @pl.loop(0, count)
    def _(j):
        at = slot[j]

        @pl.when(at >= 0)
        def _():
            for p in range(pages):
                out[j, p] = moved[at, p]

        @pl.when(at < 0)
        def _():
            i = rows[j]
            for p in range(pages):
                page = pool[table[p, i]].astype(F32)
                out[j, p] = jnp.where(token + p * page_len < length[i], page, 0.0).astype(out.dtype)


def send_pages_kernel(pool, rows, table, length, out):
    count, pages, page_len, width = out.shape
    position = lax.broadcasted_iota(I32, (page_len, width), 0)

    @pl.loop(0, count)
    def _(j):
        i = rows[j, 0]
        for p in range(pages):
            page = pool[table[p, i]].astype(F32)
            out[j, p] = jnp.where(position + p * page_len < length[i], page, 0.0).astype(out.dtype)


def take_pages(pool, moved, rows, slot, table, length, after=()):
    outs = [shape(slot.shape + table.shape[:1] + pool.shape[1:], pool.dtype)]
    args = (pool, moved, rows, slot, table, length)
    return local_call(page_kernel, [VMEM] * 2 + [SMEM] * 4, args, outs, moved=5 * MIB, after=after)[0]


def movers_kernel(half, spot, order, attention, residual, *outs):
    chip, side = spot[0] // 2, spot[0] % 2
    pair, own, row_out = outs[half:]
    for s, block in enumerate(outs[:half]):
        width = block.shape[1]
        block[...] = attention[:, lanes((chip ^ s) * width, width)]
    n, rows = order.shape
    down, across = (lax.broadcasted_iota(I32, (rows, rows), d) for d in (0, 1))
    mine = spot[0] * rows + down
    found = jnp.zeros((rows, rows), F32)
    for g in range(1, n):
        found = found + jnp.where(order[g : g + 1] == mine, float(g), 0.0)
    dest = jnp.broadcast_to(jnp.sum(found, axis=1, keepdims=True), (rows, rows))
    dest_row = dest.T
    rank = jnp.sum(jnp.where((dest == dest_row) & (down < across), 1.0, 0.0), axis=0, keepdims=True)
    rank = rank.astype(I32)
    to = dest_row[:1].astype(I32)
    far_off, core = (to >> 1) ^ chip, to & 1
    kept = jnp.where(far_off != 0, (half + far_off - 1) * MIG + rank, -1)
    slot = jnp.where(core != side, far_off * MIG + rank, kept)
    chosen = lax.broadcasted_iota(I32, (own.shape[0], rows), 0) == slot
    selector = jnp.where(chosen, 1.0, 0.0)
    numbers = lax.broadcasted_iota(I32, selector.shape, 1).astype(F32)
    number = jnp.sum(selector * numbers, axis=1, keepdims=True)
    row_out[...] = jnp.broadcast_to(number, row_out.shape).astype(I32)
    selector = selector.astype(BF)
    n_pair = pair.shape[0]
    pair[:, : attention.shape[1]] = pick(selector[:n_pair], attention[...]).astype(BF)
    moving = pick(selector, residual[...]).astype(BF)
    pair[:, attention.shape[1] :] = moving[:n_pair]
    own[...] = moving


def handover_kernel(half, place, pair, own, order, *outs):
    outs[-1][...] = order[...]
    outs = outs[:-1]
    n_pair = half * MIG
    width = own.shape[1]
    for s, out in enumerate(outs):
        first = own[n_pair + (s - 1) * MIG : n_pair + s * MIG] if s else own[:MIG]
        second = pair[s * MIG : (s + 1) * MIG, half * width :]
        blank = jnp.zeros((out.shape[0] - n_pair - 2 * MIG, width), BF)
        columns = pair[:, lanes((place[0] ^ s) * width, width)]
        out[...] = jnp.concatenate([columns, first, second, blank], axis=0)


def slots_kernel(experts, spot, routes, picked, slots):
    rows = routes.shape[1]
    ids = lax.broadcasted_iota(I32, (8, rows), 0)
    named = jnp.where((ids == routes[0:1]) | (ids == routes[1:2]), 1.0, 0.0)
    down, across = (lax.broadcasted_iota(I32, (rows, rows), d) for d in (0, 1))
    before = pick(named.astype(BF), jnp.where(down < across, 1.0, 0.0).astype(BF))
    at = lax.broadcasted_iota(I32, picked.shape, 0)
    chosen = jnp.zeros(picked.shape, F32)
    for top in range(2):
        route = routes[top : top + 1]
        rank = jnp.sum(jnp.where(ids == route, before, 0.0), axis=0, keepdims=True).astype(I32)
        slot = (route ^ spot[0]) * SLOTS + rank
        slots[top : top + 1] = slot
        chosen = chosen + jnp.where(at == slot, 1.0, 0.0)
    picked[...] = chosen.astype(BF)


def project_kernel(half, *refs):
    odd, selector_far, resid_selector_far, residual_far, own, other = refs[:6]
    blocks = refs[6 : 6 + 2 * half]
    outs = refs[6 + 2 * half : 6 + 3 * half]
    buf, weights, selector, resid_selector, residual, sems = refs[6 + 3 * half :]
    rows = residual.shape[0]
    pairs = [(selector_far, selector), (resid_selector_far, resid_selector), (residual_far, residual)]
    at = 0
    for block in blocks:
        pairs.append((block, buf.at[pl.ds(at, block.shape[0])]))
        at += block.shape[0]
    pairs += [(own, weights.at[odd[0]]), (other, weights.at[1 - odd[0]])]
    copies = [
        pltpu.make_async_copy(source, target, sems.at[c])
        for c, (source, target) in enumerate(pairs)
    ]
    for copy in copies:
        copy.start()
    copies, fetches = copies[:-2], copies[-2:]
    for copy in copies:
        copy.wait()
    picked = pick(selector[...], buf[...]).astype(BF)
    resid = pick(resid_selector[:, :rows], residual[...])
    resid = resid + pick(resid_selector[:, rows:], buf[half * rows :])
    for copy in fetches:
        copy.wait()
    depth = own.shape[0]
    product = pick(picked[:, :depth], weights[0]) + pick(picked[:, depth:], weights[1])
    outs[0][...] = resid + product[:rows]
    for t in range(1, half):
        outs[t][...] = product[t * rows : (t + 1) * rows].astype(BF)


def halves(x):
    high = x.astype(BF)
    return high, (x - high.astype(F32)).astype(BF)


def norm_kernel(half, experts, wide, *refs):
    gain, router, selector, pages = refs[:4]
    parts = refs[4 : 4 + half]
    hidden_out, early = refs[4 + half : 6 + half]
    late = refs[6 + half :]
    hidden = parts[0][...]
    for part in parts[1:]:
        hidden = hidden + part[...].astype(F32)
    hidden_out[...] = hidden
    scaled = hidden * gain[...]
    rows = hidden.shape[0]
    lane = lax.broadcasted_iota(I32, (rows, 128), 1)
    stats = jnp.where(lane == 8, jnp.sum(hidden * hidden, axis=1, keepdims=True), 0.0)
    for e in range(experts):
        logit = jnp.sum(scaled * router[e : e + 1], axis=1, keepdims=True)
        stats = jnp.where(lane == e, logit, stats)
    stats = stats.T[: early.shape[0] - rows]
    scaled = scaled.astype(BF)
    early[:rows] = scaled[:, :wide]
    high, low = halves(stats)
    early[rows:] = jnp.zeros((early.shape[0] - rows, wide), BF)
    early[rows:, :rows] = high
    early[rows:, rows : 2 * rows] = low
    chosen = pick(selector[...], scaled[:, wide:]).astype(BF)
    for s in range(experts):
        late[s][:SLOTS, : chosen.shape[1]] = chosen[s * SLOTS : (s + 1) * SLOTS]
    late[2][SLOTS:] = pages[...]


def hold_kernel(x, out):
    out[...] = x[...]


def hold(x, after):
    return local_call(hold_kernel, [VMEM], (x,), [far(x.shape, x.dtype)], after=[after])[0]


def dispatch_kernel(ne, experts, *refs):
    place, selector = refs[:2]
    blocks, late, refs = refs[2 : 2 + ne], refs[2 + ne : 2 + ne + experts], refs[2 + ne + experts :]
    outs, stats_out, late_out = refs[:experts], refs[experts], refs[experts + 1]
    for t in range(experts):
        late_out[t * SLOTS : (t + 1) * SLOTS] = late[t][:SLOTS, : late_out.shape[1]]
    wide = blocks[0].shape[1]
    rows = selector.shape[1]
    stats = jnp.zeros(stats_out.shape, F32)
    for block in blocks:
        stats = stats + block[rows:, :rows].astype(F32) + block[rows:, rows : 2 * rows].astype(F32)
    stats_out[...] = stats
    inverse = lax.rsqrt(stats[stats.shape[0] // 2 :][:1] / D + EPSILON)
    scale = jnp.sum(selector[...].astype(F32) * inverse, axis=1, keepdims=True)
    high, low = halves(scale)
    lane = lax.broadcasted_iota(I32, (scale.shape[0], 128), 1)
    scale = jnp.where(lane == 0, high.astype(F32), jnp.where(lane == 1, low.astype(F32), 0.0)).astype(BF)
    for t in range(experts):
        outs[t][:, ne * wide :] = scale[t * SLOTS : (t + 1) * SLOTS]
    for s in range(ne):
        chosen = pick(selector[...], blocks[s][:rows]).astype(BF)
        columns = lanes((place[0] ^ s) * wide, wide)
        for t in range(experts):
            outs[t][:, columns] = chosen[t * SLOTS : (t + 1) * SLOTS]


def expert_kernel(ne, experts, tile, spot, *refs):
    early, late = refs[:experts], refs[experts : experts + ne]
    gate, up, down, stats = refs[experts + ne : experts + ne + 4]
    refs = refs[experts + ne + 4 :]
    late_out, early_out = refs[:ne], refs[ne : ne + experts]
    stats_out = refs[ne + experts]
    rows, pieces, active, gate_buf, up_buf, down_buf, late_buf, early_buf = refs[ne + experts + 1 : -3]
    sems, load_sems, out_sems = refs[-3:]
    place = spot[0]
    rest = late[0].shape[1]
    wide = (early[0].shape[1] - 128) // ne
    feats = wide + rest
    tiles = gate.shape[2] // tile

    def copies(f):
        columns = lanes(f * tile, tile)
        return [
            pltpu.make_async_copy(gate.at[0, :, columns], gate_buf.at[:, columns], sems.at[0, f]),
            pltpu.make_async_copy(up.at[0, :, columns], up_buf.at[:, columns], sems.at[1, f]),
        ]

    def down_copy(e):
        return pltpu.make_async_copy(down.at[0, :, lanes(e * feats, feats)], down_buf.at[e], sems.at[2, e])

    def early_copy(e, t):
        columns = lanes(e * wide, wide)
        return pltpu.make_async_copy(
            early_buf.at[t, :, columns], early_out[t].at[:, columns], out_sems.at[e, t]
        )

    def late_copy(e, s):
        return pltpu.make_async_copy(late_buf.at[e], late_out[s], out_sems.at[e, experts])

    def start(unit):
        @pl.when(unit < tiles)
        def _():
            for copy in copies(unit):
                copy.start()

        @pl.when((unit >= tiles) & (unit < tiles + ne))
        def _():
            down_copy(unit - tiles).start()

    loads = []

    def load(source, target):
        loads.append(pltpu.make_async_copy(source, target, load_sems.at[len(loads)]))

    for t in range(experts):
        at = pl.ds(t * SLOTS, SLOTS)
        load(early[t].at[:, pl.ds(ne * wide, 128)], pieces.at[at])
        for e in range(ne):
            load(early[t].at[:, pl.ds(e * wide, wide)], rows.at[at, pl.ds(e * feats, wide)])
    for s in range(ne):
        load(late[s], rows.at[:, lanes((place ^ s) * feats + wide, rest)])
    for copy in loads:
        copy.start()
    start(jnp.int32(0))
    stats_out[...] = stats[...]
    for copy in loads:
        copy.wait()
    for unit in range(1, AHEAD):
        start(jnp.int32(unit))
    scale = pieces[:, :1].astype(F32) + pieces[:, 1:2].astype(F32)

    @pl.loop(0, tiles)
    def _(f):
        for copy in copies(f):
            copy.wait()
        start(f + AHEAD)
        columns = lanes(f * tile, tile)
        gate_h = pick(rows[...], gate_buf[:, columns]) * scale
        up_h = pick(rows[...], up_buf[:, columns]) * scale
        active[:, columns] = (gate_h / (1.0 + jnp.exp(-gate_h)) * up_h).astype(BF)

    @pl.loop(0, ne)
    def _(e):
        down_copy(e).wait()
        start(e + tiles + AHEAD)
        value = pick(active[...], down_buf[e]).astype(BF)
        late_buf[e] = value[:, wide:]
        for t in range(experts):
            early_buf[t, :, lanes(e * wide, wide)] = value[t * SLOTS : (t + 1) * SLOTS, :wide]
            early_copy(e, t).start()
        for s in range(ne):

            @pl.when(e ^ place == s)
            def _():
                late_copy(e, s).start()

    @pl.loop(0, ne)
    def _(e):
        late_copy(e, 0).wait()
        for t in range(experts):
            early_copy(e, t).wait()


def expert_call(place, early, late, w_gate, w_up, w_down, stats, ne, after):
    hidden = w_gate.shape[2]
    slots, rest = late[0].shape
    experts = len(early)
    wide = (early[0].shape[1] - 128) // ne
    tile = 256 if hidden % 256 == 0 else 128
    values = local_call(
        functools.partial(expert_kernel, ne, experts, tile),
        [SMEM] + [HBM] * (experts + ne + 3) + [VMEM],
        (place, *early, *late, w_gate, w_up, w_down, stats),
        [near((slots, rest), BF)]
        + [far((slots, rest), BF)] * (ne - 1)
        + [near((SLOTS, ne * wide), BF)]
        + [far((SLOTS, ne * wide), BF)] * (experts - 1)
        + [near(stats.shape, F32)],
        [
            pltpu.VMEM((slots, D), BF),
            pltpu.VMEM((slots, 128), BF),
            pltpu.VMEM((slots, hidden), BF),
            pltpu.VMEM((D, hidden), BF),
            pltpu.VMEM((D, hidden), BF),
            pltpu.VMEM((ne, hidden, wide + rest), BF),
            pltpu.VMEM((ne, slots, rest), BF),
            pltpu.VMEM((experts, SLOTS, ne * wide), BF),
            pltpu.SemaphoreType.DMA((3, max(hidden // tile, ne))),
            pltpu.SemaphoreType.DMA((experts * (ne + 1) + ne,)),
            pltpu.SemaphoreType.DMA((ne, experts + 1)),
        ],
        vmem=60,
        out_specs=[ANY] + [HBM] * (ne - 1) + [ANY] + [HBM] * (experts - 1) + [VMEM],
        after=[after],
        flops=6 * slots * D * hidden,
        moved=6 * D * hidden,
    )
    return values[:ne], values[ne:-1], values[-1]


def weigh_kernel(ne, experts, *refs):
    place, stats, routes, slots = refs[:4]
    blocks, late = refs[4 : 4 + experts], refs[4 + experts : 4 + experts + ne]
    refs = refs[4 + experts + ne :]
    outs, late_outs, (high, low, buf, total) = refs[:ne], refs[ne : ne + experts], refs[ne + experts :]
    rows = routes.shape[1]
    logits = stats[:8] * lax.rsqrt(stats[8:9] / D + EPSILON)
    ids = lax.broadcasted_iota(I32, (8, rows), 0)
    chosen = [
        jnp.sum(jnp.where(ids == routes[top : top + 1], logits, 0.0), axis=0, keepdims=True)
        for top in range(2)
    ]
    at = lax.broadcasted_iota(I32, (experts * SLOTS, rows), 0)
    gates = jnp.zeros(at.shape, F32)
    for top in range(2):
        gate = 1.0 / (1.0 + jnp.exp(chosen[1 - top] - chosen[top]))
        gates = gates + jnp.where(at == slots[top : top + 1], gate, 0.0)
    high[...], low[...] = halves(gates.T)
    for t in range(experts):
        buf[t * SLOTS : (t + 1) * SLOTS] = blocks[t][...]
    total[...] = pick(high[...], buf[...]) + pick(low[...], buf[...])
    wide = outs[0].shape[1]
    for s in range(ne):
        outs[s][...] = total[:, lanes((place[0] ^ s) * wide, wide)].astype(outs[s].dtype)
    late_sum = late[0][...].astype(F32)
    for block in late[1:]:
        late_sum = late_sum + block[...].astype(F32)
    for t in range(experts):
        late_outs[t][...] = late_sum[t * SLOTS : (t + 1) * SLOTS].astype(BF)


def finish_kernel(ne, experts, wide, *refs):
    high, low, hidden = refs[:3]
    early, late = refs[3 : 3 + ne], refs[3 + ne : 3 + ne + experts]
    out, buf = refs[3 + ne + experts :]
    first = hidden[:, :wide]
    for block in early:
        first = first + block[...].astype(F32)
    out[:, :wide] = first
    for t in range(experts):
        buf[t * SLOTS : (t + 1) * SLOTS] = late[t][...]
    out[:, wide:] = hidden[:, wide:] + pick(high[...], buf[...]) + pick(low[...], buf[...])


def body(
    attention_out,
    residual,
    w_out,
    router_w,
    norm_gain,
    page_pool,
    page_table,
    cache_len,
    came_from,
    routes,
    w_gate,
    w_up,
    w_down,
):
    n = lax.axis_size("req")
    ne = lax.axis_size("exp")
    me = lax.axis_index("req")
    ze = lax.axis_index("exp")
    half = n // 2
    q, k = me // 2, me % 2
    rows = attention_out.shape[0]
    feats = residual.shape[1]
    kblock = D // half
    experts = n // 2
    rest = max(128, feats * PART // 8 // 128 * 128)
    wide = feats - rest
    place = ze.reshape(1).astype(I32)

    pair_place = q.reshape(1).astype(I32)
    n_pair, n_send = half * MIG, (2 * half - 1) * MIG
    n_hand = -(-(n_pair + 2 * MIG) // 16) * 16
    *attn_blocks, pair_rows, own_rows, send_row = local_call(
        functools.partial(movers_kernel, half),
        [SMEM] + [VMEM] * 3,
        (me.reshape(1).astype(I32), came_from.reshape(n, rows), attention_out, residual),
        [far((rows, kblock), BF)] + [near((rows, kblock), BF)] * (half - 1)
        + [
            far((n_pair, D + feats), BF),
            far((2 * n_pair, feats), BF),
            shape((2 * n_pair, 128), I32),
        ],
        vmem=60,
        moved=2 * MIB,
    )
    attn_blocks = [attn_blocks[0]] + [swap(attn_blocks[s], "req", 2 * s) for s in range(1, half)]
    w_other = swap(w_out, "req", 1)
    pair_rows = swap(pair_rows, "req", 1)
    *late_blocks, order = local_call(
        functools.partial(handover_kernel, half),
        [SMEM, VMEM, VMEM, VMEM],
        (pair_place, pair_rows, own_rows, came_from.reshape(n, rows)),
        [far((n_hand, feats), BF)] * half + [shape((n, rows), I32)],
        vmem=60,
        moved=MIB,
        after=[w_other],
    )
    late_blocks = [late_blocks[0]] + [swap(late_blocks[s], "req", 2 * s) for s in range(1, half)]
    came_from = order.reshape(-1)

    source = jnp.stack(
        [lax.dynamic_slice_in_dim(came_from, (2 * (q ^ t) + k) * rows, rows) for t in range(half)]
    )
    src_group, src_local = source // rows, source % rows
    src_rank = jnp.sum(
        (src_group[:, :, None] == src_group[:, None, :]) & (source[:, None, :] < source[:, :, None]),
        axis=2,
    )
    src_rel, src_par = (src_group // 2) ^ q, src_group % 2
    t_ids = jnp.arange(half, dtype=I32)[:, None]
    attn_at = jnp.where(
        src_par == k,
        src_rel * rows + src_local,
        half * rows + src_rel * n_hand + (t_ids ^ src_rel) * MIG + src_rank,
    ).reshape(-1)
    own_stays = src_group[0] == me
    own_slot = src_rel[0] * 2 * MIG + jnp.where(src_par[0] == k, 0, MIG) + src_rank[0]
    own_hand = src_rel[0] * n_hand + n_pair + jnp.where(src_par[0] == k, 0, MIG) + src_rank[0]
    own_at = jnp.where(own_stays, src_local[0], rows + own_hand)

    slot_pick, slot_of = local_call(
        functools.partial(slots_kernel, experts),
        [SMEM, VMEM],
        ((me % experts).reshape(1).astype(I32), routes.T),
        [shape((experts * SLOTS, rows), BF), shape((2, rows), I32)],
        after=[order],
    )

    total_rows = half * (rows + n_hand)
    selector = hot(attn_at, total_rows)
    resid_selector = hot(own_at, rows + half * n_hand)
    parts = local_call(
        functools.partial(project_kernel, half),
        [SMEM] + [HBM] * (5 + 2 * half),
        (
            k.reshape(1).astype(I32),
            selector,
            resid_selector,
            residual,
            w_out,
            w_other,
            *attn_blocks,
            *late_blocks,
        ),
        [near((rows, feats), F32)] + [near((rows, feats), BF)] * (half - 1),
        [
            pltpu.VMEM((total_rows, kblock), BF),
            pltpu.VMEM((2,) + w_out.shape, BF),
            pltpu.VMEM(selector.shape, BF),
            pltpu.VMEM(resid_selector.shape, BF),
            pltpu.VMEM(residual.shape, BF),
            pltpu.SemaphoreType.DMA((2 * half + 5,)),
        ],
        vmem=58,
        flops=2 * half * rows * (total_rows + feats) * kblock,
        moved=6 * MIB,
    )
    parts = [parts[0]] + [swap(parts[s], "req", 2 * s) for s in range(1, half)]

    table = page_table.T
    moving = local_call(
        send_pages_kernel,
        [VMEM] + [SMEM] * 3,
        (page_pool, send_row, table, cache_len),
        [shape((n_send,) + table.shape[:1] + page_pool.shape[1:], BF)],
        moved=3 * MIB,
        after=[order],
    )[0]
    page = moving.shape[1:]
    pair_pages = swap(moving[:n_pair], "req", 1).reshape((half, MIG) + page)
    own_pages = jnp.concatenate([moving[:MIG], moving[n_pair:]], axis=0).reshape((half, MIG) + page)
    pages = jnp.concatenate([own_pages, pair_pages], axis=1)
    stages = half.bit_length() - 1
    block = pages.shape[1:]
    pages = pages.reshape((half // 2, 2) + block)
    page_rows = pages[:, 1].reshape(-1, page[-1])

    router = jnp.pad(router_w.T, ((0, 8 - experts), (0, 0)))
    late_shapes = [(SLOTS, rest)] * experts
    late_shapes[2] = (SLOTS + page_rows.shape[0], page[-1])
    normed = local_call(
        functools.partial(norm_kernel, half, experts, wide),
        [VMEM] * (4 + half),
        (norm_gain[None, :], router, slot_pick, page_rows, *parts),
        [far((rows, feats), F32), far((rows + 16, wide), BF)]
        + [far(dims, BF) for dims in late_shapes],
        flops=2 * experts * SLOTS * rows * rest,
        moved=3 * MIB,
    )
    hidden, early = normed[:2]
    late = [normed[2 + s] if s == 0 else swap(normed[2 + s], "req", s) for s in range(experts)]
    early_blocks = [early] + [swap(early, "exp", s) for s in range(1, ne)]
    came_pages = late[2][SLOTS:].reshape((half // 2,) + block)
    pages = jnp.stack([pages[:, 0], came_pages], axis=1)
    outgoing = local_call(
        functools.partial(dispatch_kernel, ne, experts),
        [SMEM] + [VMEM] * (1 + ne + experts),
        (place, slot_pick, *early_blocks, *late),
        [far((SLOTS, ne * wide + 128), BF)]
        + [near((SLOTS, ne * wide + 128), BF)] * (experts - 1)
        + [near((16, rows), F32), far((experts * SLOTS, rest), BF)],
        vmem=60,
        flops=2 * experts * SLOTS * rows * ne * wide,
        moved=3 * MIB,
    )
    late = outgoing[experts + 1]
    late_rows = [late] + [swap(late, "exp", s) for s in range(1, ne)]

    early_rows = [swap(outgoing[s], "req", s) if s else outgoing[s] for s in range(experts)]

    crossing = pages
    for bit in range(1, stages):
        pages = pages.reshape((half >> (bit + 1), 2, 1 << bit) + block)
        came_pages = swap(pages[:, 1], "req", 2 << bit)
        pages = jnp.stack([pages[:, 0], came_pages], axis=1)
    moved_pages = pages.reshape((half * 2 * MIG,) + page)

    down_late, down_early, stats = expert_call(
        place, early_rows, late_rows, w_gate, w_up, w_down, outgoing[experts], ne, crossing
    )
    late_blocks = [down_late[0]] + [swap(down_late[s], "exp", s) for s in range(1, ne)]
    near_back = hold(down_early[1], late_blocks[-1])
    early_back = [
        swap(down_early[s] if s > 1 else near_back, "req", s) if s else down_early[s]
        for s in range(experts)
    ]
    new_pages = take_pages(
        page_pool,
        moved_pages,
        jnp.where(own_stays, src_local[0], 0),
        jnp.where(own_stays, -1, own_slot),
        table,
        cache_len,
        [stats],
    )
    weighted = local_call(
        functools.partial(weigh_kernel, ne, experts),
        [SMEM] + [VMEM] * (3 + experts + ne),
        (place, stats, routes.T, slot_of, *early_back, *late_blocks),
        [shape((rows, wide), F32)]
        + [shape((rows, wide), BF)] * (ne - 1)
        + [shape((SLOTS, rest), BF)] * experts
        + [shape((rows, experts * SLOTS), BF)] * 2,
        [pltpu.VMEM((experts * SLOTS, ne * wide), BF), pltpu.VMEM((rows, ne * wide), F32)],
        flops=4 * rows * experts * SLOTS * ne * wide,
        moved=3 * MIB,
    )
    early_parts = [swap(weighted[s], "exp", s) for s in range(ne - 1, 0, -1)]
    early_parts = [weighted[0]] + early_parts[::-1]
    late_back = [
        swap(weighted[ne + s], "req", s) if s else weighted[ne] for s in range(experts)
    ]
    mixed = local_call(
        functools.partial(finish_kernel, ne, experts, wide),
        [VMEM] * (3 + ne + experts),
        (*weighted[-2:], hidden, *early_parts, *late_back),
        [shape((rows, feats), F32)],
        [pltpu.VMEM((experts * SLOTS, rest), BF)],
        flops=4 * rows * experts * SLOTS * rest,
        moved=2 * MIB,
    )[0]

    return (mixed, new_pages)


def solution(mesh):
    in_specs = (
        P("req", None),
        P("req", "exp"),
        P("req", "exp"),
        P("exp", None),
        P("exp"),
        P("req", None, "exp"),
        P("req", None),
        P("req"),
        P(),
        P("req", None),
        P("req", None, "exp"),
        P("req", None, "exp"),
        P("req", "exp", None),
    )
    out_specs = (P("req", "exp"), P("req", None, None, "exp"))
    return jax.shard_map(body, mesh=mesh, in_specs=in_specs, out_specs=out_specs, check_vma=False)
```

```python
import functools

import jax
import jax.numpy as jnp
from jax import lax
from jax.experimental import pallas as pl
from jax.experimental.pallas import tpu as pltpu
from jax.sharding import PartitionSpec as P

D = 4096
SLOTS = 64
PART = 3
AHEAD = 3
MIG = 4
EPSILON = 1e-05
BF = jnp.bfloat16
F32 = jnp.float32
I32 = jnp.int32
MIB = 2**20
VMEM = pl.BlockSpec(memory_space=pltpu.VMEM)
SMEM = pl.BlockSpec(memory_space=pltpu.SMEM)
HBM = pl.BlockSpec(memory_space=pltpu.HBM)
ANY = pl.BlockSpec(memory_space=pl.ANY)


def swap(x, axis, s):
    n = lax.axis_size(axis)
    return lax.ppermute(x, axis, [(i, i ^ s) for i in range(n)])


def hot(index, count):
    return (index[..., None] == jnp.arange(count, dtype=I32)).astype(BF)


def pick(selector, rows):
    return jnp.dot(selector, rows, preferred_element_type=F32)


def lanes(start, width):
    return pl.ds(pl.multiple_of(start, 128), width)


def local_call(kernel, in_specs, args, outs, scratch=(), vmem=16, flops=0, moved=0, after=(), out_specs=None):
    count, waits = len(args), tuple(after)

    def run(*refs):
        kernel(*refs[:count], *refs[count + len(waits) :])

    return pl.pallas_call(
        run,
        out_shape=outs,
        in_specs=list(in_specs) + [pl.BlockSpec(memory_space=pl.ANY)] * len(waits),
        out_specs=out_specs or [VMEM] * len(outs),
        scratch_shapes=list(scratch),
        compiler_params=pltpu.CompilerParams(vmem_limit_bytes=vmem * MIB),
        cost_estimate=pl.CostEstimate(flops=flops, bytes_accessed=moved, transcendentals=0),
    )(*args, *waits)


def shape(dims, dtype):
    return jax.ShapeDtypeStruct(dims, dtype)


def near(dims, dtype):
    return pltpu.VMEM(dims, dtype)


def far(dims, dtype):
    return pltpu.HBM(dims, dtype)


def page_kernel(pool, moved, rows, slot, table, length, out):
    count, pages, page_len, width = out.shape
    token = lax.broadcasted_iota(I32, (page_len, width), 0)

    @pl.loop(0, count)
    def _(j):
        at = slot[j]

        @pl.when(at >= 0)
        def _():
            for p in range(pages):
                out[j, p] = moved[at, p]

        @pl.when(at < 0)
        def _():
            i = rows[j]
            for p in range(pages):
                page = pool[table[p, i]].astype(F32)
                out[j, p] = jnp.where(token + p * page_len < length[i], page, 0.0).astype(out.dtype)


def send_pages_kernel(pool, rows, table, length, out):
    count, pages, page_len, width = out.shape
    position = lax.broadcasted_iota(I32, (page_len, width), 0)

    @pl.loop(0, count)
    def _(j):
        i = rows[j, 0]
        for p in range(pages):
            page = pool[table[p, i]].astype(F32)
            out[j, p] = jnp.where(position + p * page_len < length[i], page, 0.0).astype(out.dtype)


def take_pages(pool, moved, rows, slot, table, length, after=()):
    outs = [shape(slot.shape + table.shape[:1] + pool.shape[1:], pool.dtype)]
    args = (pool, moved, rows, slot, table, length)
    return local_call(page_kernel, [VMEM] * 2 + [SMEM] * 4, args, outs, moved=5 * MIB, after=after)[0]


def movers_kernel(half, spot, order, attention, residual, *outs):
    chip, side = spot[0] // 2, spot[0] % 2
    pair, own, row_out = outs[half:]
    for s, block in enumerate(outs[:half]):
        width = block.shape[1]
        block[...] = attention[:, lanes((chip ^ s) * width, width)]
    n, rows = order.shape
    down, across = (lax.broadcasted_iota(I32, (rows, rows), d) for d in (0, 1))
    mine = spot[0] * rows + down
    found = jnp.zeros((rows, rows), F32)
    for g in range(1, n):
        found = found + jnp.where(order[g : g + 1] == mine, float(g), 0.0)
    dest = jnp.broadcast_to(jnp.sum(found, axis=1, keepdims=True), (rows, rows))
    dest_row = dest.T
    rank = jnp.sum(jnp.where((dest == dest_row) & (down < across), 1.0, 0.0), axis=0, keepdims=True)
    rank = rank.astype(I32)
    to = dest_row[:1].astype(I32)
    far_off, core = (to >> 1) ^ chip, to & 1
    kept = jnp.where(far_off != 0, (half + far_off - 1) * MIG + rank, -1)
    slot = jnp.where(core != side, far_off * MIG + rank, kept)
    chosen = lax.broadcasted_iota(I32, (own.shape[0], rows), 0) == slot
    selector = jnp.where(chosen, 1.0, 0.0)
    numbers = lax.broadcasted_iota(I32, selector.shape, 1).astype(F32)
    number = jnp.sum(selector * numbers, axis=1, keepdims=True)
    row_out[...] = jnp.broadcast_to(number, row_out.shape).astype(I32)
    selector = selector.astype(BF)
    n_pair = pair.shape[0]
    pair[:, : attention.shape[1]] = pick(selector[:n_pair], attention[...]).astype(BF)
    moving = pick(selector, residual[...]).astype(BF)
    pair[:, attention.shape[1] :] = moving[:n_pair]
    own[...] = moving


def handover_kernel(half, place, pair, own, order, *outs):
    outs[-1][...] = order[...]
    outs = outs[:-1]
    n_pair = half * MIG
    width = own.shape[1]
    for s, out in enumerate(outs):
        first = own[n_pair + (s - 1) * MIG : n_pair + s * MIG] if s else own[:MIG]
        second = pair[s * MIG : (s + 1) * MIG, half * width :]
        blank = jnp.zeros((out.shape[0] - n_pair - 2 * MIG, width), BF)
        columns = pair[:, lanes((place[0] ^ s) * width, width)]
        out[...] = jnp.concatenate([columns, first, second, blank], axis=0)


def slots_kernel(experts, spot, routes, picked, slots):
    rows = routes.shape[1]
    ids = lax.broadcasted_iota(I32, (8, rows), 0)
    named = jnp.where((ids == routes[0:1]) | (ids == routes[1:2]), 1.0, 0.0)
    down, across = (lax.broadcasted_iota(I32, (rows, rows), d) for d in (0, 1))
    before = pick(named.astype(BF), jnp.where(down < across, 1.0, 0.0).astype(BF))
    at = lax.broadcasted_iota(I32, picked.shape, 0)
    chosen = jnp.zeros(picked.shape, F32)
    for top in range(2):
        route = routes[top : top + 1]
        rank = jnp.sum(jnp.where(ids == route, before, 0.0), axis=0, keepdims=True).astype(I32)
        slot = (route ^ spot[0]) * SLOTS + rank
        slots[top : top + 1] = slot
        chosen = chosen + jnp.where(at == slot, 1.0, 0.0)
    picked[...] = chosen.astype(BF)


def project_kernel(half, *refs):
    odd, selector_far, resid_selector_far, residual_far, own, other = refs[:6]
    blocks = refs[6 : 6 + 2 * half]
    outs = refs[6 + 2 * half : 6 + 3 * half]
    buf, weights, selector, resid_selector, residual, sems = refs[6 + 3 * half :]
    rows = residual.shape[0]
    pairs = [(selector_far, selector), (resid_selector_far, resid_selector), (residual_far, residual)]
    at = 0
    for block in blocks:
        pairs.append((block, buf.at[pl.ds(at, block.shape[0])]))
        at += block.shape[0]
    pairs += [(own, weights.at[odd[0]]), (other, weights.at[1 - odd[0]])]
    copies = [
        pltpu.make_async_copy(source, target, sems.at[c])
        for c, (source, target) in enumerate(pairs)
    ]
    for copy in copies:
        copy.start()
    copies, fetches = copies[:-2], copies[-2:]
    for copy in copies:
        copy.wait()
    picked = pick(selector[...], buf[...]).astype(BF)
    resid = pick(resid_selector[:, :rows], residual[...])
    resid = resid + pick(resid_selector[:, rows:], buf[half * rows :])
    for copy in fetches:
        copy.wait()
    depth = own.shape[0]
    product = pick(picked[:, :depth], weights[0]) + pick(picked[:, depth:], weights[1])
    outs[0][...] = resid + product[:rows]
    for t in range(1, half):
        outs[t][...] = product[t * rows : (t + 1) * rows].astype(BF)


def halves(x):
    high = x.astype(BF)
    return high, (x - high.astype(F32)).astype(BF)


def norm_kernel(half, experts, wide, *refs):
    gain, router, selector, pages = refs[:4]
    parts = refs[4 : 4 + half]
    hidden_out, early = refs[4 + half : 6 + half]
    late = refs[6 + half :]
    hidden = parts[0][...]
    for part in parts[1:]:
        hidden = hidden + part[...].astype(F32)
    hidden_out[...] = hidden
    scaled = hidden * gain[...]
    rows = hidden.shape[0]
    lane = lax.broadcasted_iota(I32, (rows, 128), 1)
    stats = jnp.where(lane == 8, jnp.sum(hidden * hidden, axis=1, keepdims=True), 0.0)
    for e in range(experts):
        logit = jnp.sum(scaled * router[e : e + 1], axis=1, keepdims=True)
        stats = jnp.where(lane == e, logit, stats)
    stats = stats.T[: early.shape[0] - rows]
    scaled = scaled.astype(BF)
    early[:rows] = scaled[:, :wide]
    high, low = halves(stats)
    early[rows:] = jnp.zeros((early.shape[0] - rows, wide), BF)
    early[rows:, :rows] = high
    early[rows:, rows : 2 * rows] = low
    chosen = pick(selector[...], scaled[:, wide:]).astype(BF)
    for s in range(experts):
        late[s][:SLOTS, : chosen.shape[1]] = chosen[s * SLOTS : (s + 1) * SLOTS]
    late[2][SLOTS:] = pages[...]


def hold_kernel(x, out):
    out[...] = x[...]


def hold(x, after):
    return local_call(hold_kernel, [VMEM], (x,), [far(x.shape, x.dtype)], after=[after])[0]


def dispatch_kernel(ne, experts, *refs):
    place, selector = refs[:2]
    blocks, late, refs = refs[2 : 2 + ne], refs[2 + ne : 2 + ne + experts], refs[2 + ne + experts :]
    outs, stats_out, late_out = refs[:experts], refs[experts], refs[experts + 1]
    for t in range(experts):
        late_out[t * SLOTS : (t + 1) * SLOTS] = late[t][:SLOTS, : late_out.shape[1]]
    wide = blocks[0].shape[1]
    rows = selector.shape[1]
    stats = jnp.zeros(stats_out.shape, F32)
    for block in blocks:
        stats = stats + block[rows:, :rows].astype(F32) + block[rows:, rows : 2 * rows].astype(F32)
    stats_out[...] = stats
    inverse = lax.rsqrt(stats[stats.shape[0] // 2 :][:1] / D + EPSILON)
    scale = jnp.sum(selector[...].astype(F32) * inverse, axis=1, keepdims=True)
    high, low = halves(scale)
    lane = lax.broadcasted_iota(I32, (scale.shape[0], 128), 1)
    scale = jnp.where(lane == 0, high.astype(F32), jnp.where(lane == 1, low.astype(F32), 0.0)).astype(BF)
    for t in range(experts):
        outs[t][:, ne * wide :] = scale[t * SLOTS : (t + 1) * SLOTS]
    for s in range(ne):
        chosen = pick(selector[...], blocks[s][:rows]).astype(BF)
        columns = lanes((place[0] ^ s) * wide, wide)
        for t in range(experts):
            outs[t][:, columns] = chosen[t * SLOTS : (t + 1) * SLOTS]


def expert_kernel(ne, experts, tile, spot, *refs):
    early, late = refs[:experts], refs[experts : experts + ne]
    gate, up, down, stats = refs[experts + ne : experts + ne + 4]
    refs = refs[experts + ne + 4 :]
    late_out, early_out = refs[:ne], refs[ne : ne + experts]
    stats_out = refs[ne + experts]
    rows, pieces, active, gate_buf, up_buf, down_buf, late_buf, early_buf = refs[ne + experts + 1 : -3]
    sems, load_sems, out_sems = refs[-3:]
    place = spot[0]
    rest = late[0].shape[1]
    wide = (early[0].shape[1] - 128) // ne
    feats = wide + rest
    tiles = gate.shape[2] // tile

    def copies(f):
        columns = lanes(f * tile, tile)
        return [
            pltpu.make_async_copy(gate.at[0, :, columns], gate_buf.at[:, columns], sems.at[0, f]),
            pltpu.make_async_copy(up.at[0, :, columns], up_buf.at[:, columns], sems.at[1, f]),
        ]

    def down_copy(e):
        return pltpu.make_async_copy(down.at[0, :, lanes(e * feats, feats)], down_buf.at[e], sems.at[2, e])

    def early_copy(e, t):
        columns = lanes(e * wide, wide)
        return pltpu.make_async_copy(
            early_buf.at[t, :, columns], early_out[t].at[:, columns], out_sems.at[e, t]
        )

    def late_copy(e, s):
        return pltpu.make_async_copy(late_buf.at[e], late_out[s], out_sems.at[e, experts])

    def start(unit):
        @pl.when(unit < tiles)
        def _():
            for copy in copies(unit):
                copy.start()

        @pl.when((unit >= tiles) & (unit < tiles + ne))
        def _():
            down_copy(unit - tiles).start()

    loads = []

    def load(source, target):
        loads.append(pltpu.make_async_copy(source, target, load_sems.at[len(loads)]))

    for t in range(experts):
        at = pl.ds(t * SLOTS, SLOTS)
        load(early[t].at[:, pl.ds(ne * wide, 128)], pieces.at[at])
        for e in range(ne):
            load(early[t].at[:, pl.ds(e * wide, wide)], rows.at[at, pl.ds(e * feats, wide)])
    for s in range(ne):
        load(late[s], rows.at[:, lanes((place ^ s) * feats + wide, rest)])
    for copy in loads:
        copy.start()
    start(jnp.int32(0))
    stats_out[...] = stats[...]
    for copy in loads:
        copy.wait()
    for unit in range(1, AHEAD):
        start(jnp.int32(unit))
    scale = pieces[:, :1].astype(F32) + pieces[:, 1:2].astype(F32)

    @pl.loop(0, tiles)
    def _(f):
        for copy in copies(f):
            copy.wait()
        start(f + AHEAD)
        columns = lanes(f * tile, tile)
        gate_h = pick(rows[...], gate_buf[:, columns]) * scale
        up_h = pick(rows[...], up_buf[:, columns]) * scale
        active[:, columns] = (gate_h / (1.0 + jnp.exp(-gate_h)) * up_h).astype(BF)

    @pl.loop(0, ne)
    def _(e):
        down_copy(e).wait()
        start(e + tiles + AHEAD)
        value = pick(active[...], down_buf[e]).astype(BF)
        late_buf[e] = value[:, wide:]
        for t in range(experts):
            early_buf[t, :, lanes(e * wide, wide)] = value[t * SLOTS : (t + 1) * SLOTS, :wide]
            early_copy(e, t).start()
        for s in range(ne):

            @pl.when(e ^ place == s)
            def _():
                late_copy(e, s).start()

    @pl.loop(0, ne)
    def _(e):
        late_copy(e, 0).wait()
        for t in range(experts):
            early_copy(e, t).wait()


def expert_call(place, early, late, w_gate, w_up, w_down, stats, ne, after):
    hidden = w_gate.shape[2]
    slots, rest = late[0].shape
    experts = len(early)
    wide = (early[0].shape[1] - 128) // ne
    tile = 256 if hidden % 256 == 0 else 128
    values = local_call(
        functools.partial(expert_kernel, ne, experts, tile),
        [SMEM] + [HBM] * (experts + ne + 3) + [VMEM],
        (place, *early, *late, w_gate, w_up, w_down, stats),
        [near((slots, rest), BF)]
        + [far((slots, rest), BF)] * (ne - 1)
        + [near((SLOTS, ne * wide), BF)]
        + [far((SLOTS, ne * wide), BF)] * (experts - 1)
        + [near(stats.shape, F32)],
        [
            pltpu.VMEM((slots, D), BF),
            pltpu.VMEM((slots, 128), BF),
            pltpu.VMEM((slots, hidden), BF),
            pltpu.VMEM((D, hidden), BF),
            pltpu.VMEM((D, hidden), BF),
            pltpu.VMEM((ne, hidden, wide + rest), BF),
            pltpu.VMEM((ne, slots, rest), BF),
            pltpu.VMEM((experts, SLOTS, ne * wide), BF),
            pltpu.SemaphoreType.DMA((3, max(hidden // tile, ne))),
            pltpu.SemaphoreType.DMA((experts * (ne + 1) + ne,)),
            pltpu.SemaphoreType.DMA((ne, experts + 1)),
        ],
        vmem=60,
        out_specs=[ANY] + [HBM] * (ne - 1) + [ANY] + [HBM] * (experts - 1) + [VMEM],
        after=[after],
        flops=6 * slots * D * hidden,
        moved=6 * D * hidden,
    )
    return values[:ne], values[ne:-1], values[-1]


def weigh_kernel(ne, experts, *refs):
    place, stats, routes, slots = refs[:4]
    blocks, late = refs[4 : 4 + experts], refs[4 + experts : 4 + experts + ne]
    refs = refs[4 + experts + ne :]
    outs, late_outs, (high, low, buf, total) = refs[:ne], refs[ne : ne + experts], refs[ne + experts :]
    rows = routes.shape[1]
    logits = stats[:8] * lax.rsqrt(stats[8:9] / D + EPSILON)
    ids = lax.broadcasted_iota(I32, (8, rows), 0)
    chosen = [
        jnp.sum(jnp.where(ids == routes[top : top + 1], logits, 0.0), axis=0, keepdims=True)
        for top in range(2)
    ]
    at = lax.broadcasted_iota(I32, (experts * SLOTS, rows), 0)
    gates = jnp.zeros(at.shape, F32)
    for top in range(2):
        gate = 1.0 / (1.0 + jnp.exp(chosen[1 - top] - chosen[top]))
        gates = gates + jnp.where(at == slots[top : top + 1], gate, 0.0)
    high[...], low[...] = halves(gates.T)
    for t in range(experts):
        buf[t * SLOTS : (t + 1) * SLOTS] = blocks[t][...]
    total[...] = pick(high[...], buf[...]) + pick(low[...], buf[...])
    wide = outs[0].shape[1]
    for s in range(ne):
        outs[s][...] = total[:, lanes((place[0] ^ s) * wide, wide)].astype(outs[s].dtype)
    late_sum = late[0][...].astype(F32)
    for block in late[1:]:
        late_sum = late_sum + block[...].astype(F32)
    for t in range(experts):
        late_outs[t][...] = late_sum[t * SLOTS : (t + 1) * SLOTS].astype(BF)


def finish_kernel(ne, experts, wide, *refs):
    high, low, hidden = refs[:3]
    early, late = refs[3 : 3 + ne], refs[3 + ne : 3 + ne + experts]
    out, buf = refs[3 + ne + experts :]
    first = hidden[:, :wide]
    for block in early:
        first = first + block[...].astype(F32)
    out[:, :wide] = first
    for t in range(experts):
        buf[t * SLOTS : (t + 1) * SLOTS] = late[t][...]
    out[:, wide:] = hidden[:, wide:] + pick(high[...], buf[...]) + pick(low[...], buf[...])


def body(
    attention_out,
    residual,
    w_out,
    router_w,
    norm_gain,
    page_pool,
    page_table,
    cache_len,
    came_from,
    routes,
    w_gate,
    w_up,
    w_down,
):
    n = lax.axis_size("req")
    ne = lax.axis_size("exp")
    me = lax.axis_index("req")
    ze = lax.axis_index("exp")
    half = n // 2
    q, k = me // 2, me % 2
    rows = attention_out.shape[0]
    feats = residual.shape[1]
    kblock = D // half
    experts = n // 2
    rest = max(128, feats * PART // 8 // 128 * 128)
    wide = feats - rest
    place = ze.reshape(1).astype(I32)

    pair_place = q.reshape(1).astype(I32)
    n_pair, n_send = half * MIG, (2 * half - 1) * MIG
    n_hand = -(-(n_pair + 2 * MIG) // 16) * 16
    *attn_blocks, pair_rows, own_rows, send_row = local_call(
        functools.partial(movers_kernel, half),
        [SMEM] + [VMEM] * 3,
        (me.reshape(1).astype(I32), came_from.reshape(n, rows), attention_out, residual),
        [far((rows, kblock), BF)] + [near((rows, kblock), BF)] * (half - 1)
        + [
            near((n_pair, D + feats), BF),
            near((2 * n_pair, feats), BF),
            shape((2 * n_pair, 128), I32),
        ],
        vmem=60,
        moved=2 * MIB,
    )
    attn_blocks = [attn_blocks[0]] + [swap(attn_blocks[s], "req", 2 * s) for s in range(1, half)]
    w_other = swap(w_out, "req", 1)
    pair_rows = swap(pair_rows, "req", 1)
    *late_blocks, order = local_call(
        functools.partial(handover_kernel, half),
        [SMEM, VMEM, VMEM, VMEM],
        (pair_place, pair_rows, own_rows, came_from.reshape(n, rows)),
        [near((n_hand, feats), BF)] * half + [near((n, rows), I32)],
        vmem=30,
        moved=MIB,
        after=[w_other],
    )
    late_blocks = [late_blocks[0]] + [swap(late_blocks[s], "req", 2 * s) for s in range(1, half)]
    came_from = order.reshape(-1)

    source = jnp.stack(
        [lax.dynamic_slice_in_dim(came_from, (2 * (q ^ t) + k) * rows, rows) for t in range(half)]
    )
    src_group, src_local = source // rows, source % rows
    src_rank = jnp.sum(
        (src_group[:, :, None] == src_group[:, None, :]) & (source[:, None, :] < source[:, :, None]),
        axis=2,
    )
    src_rel, src_par = (src_group // 2) ^ q, src_group % 2
    t_ids = jnp.arange(half, dtype=I32)[:, None]
    attn_at = jnp.where(
        src_par == k,
        src_rel * rows + src_local,
        half * rows + src_rel * n_hand + (t_ids ^ src_rel) * MIG + src_rank,
    ).reshape(-1)
    own_stays = src_group[0] == me
    own_slot = src_rel[0] * 2 * MIG + jnp.where(src_par[0] == k, 0, MIG) + src_rank[0]
    own_hand = src_rel[0] * n_hand + n_pair + jnp.where(src_par[0] == k, 0, MIG) + src_rank[0]
    own_at = jnp.where(own_stays, src_local[0], rows + own_hand)

    slot_pick, slot_of = local_call(
        functools.partial(slots_kernel, experts),
        [SMEM, VMEM],
        ((me % experts).reshape(1).astype(I32), routes.T),
        [shape((experts * SLOTS, rows), BF), shape((2, rows), I32)],
        after=[order],
    )

    total_rows = half * (rows + n_hand)
    selector = hot(attn_at, total_rows)
    resid_selector = hot(own_at, rows + half * n_hand)
    parts = local_call(
        functools.partial(project_kernel, half),
        [SMEM] + [HBM] * (5 + 2 * half),
        (
            k.reshape(1).astype(I32),
            selector,
            resid_selector,
            residual,
            w_out,
            w_other,
            *attn_blocks,
            *late_blocks,
        ),
        [near((rows, feats), F32)] + [near((rows, feats), BF)] * (half - 1),
        [
            pltpu.VMEM((total_rows, kblock), BF),
            pltpu.VMEM((2,) + w_out.shape, BF),
            pltpu.VMEM(selector.shape, BF),
            pltpu.VMEM(resid_selector.shape, BF),
            pltpu.VMEM(residual.shape, BF),
            pltpu.SemaphoreType.DMA((2 * half + 5,)),
        ],
        vmem=58,
        flops=2 * half * rows * (total_rows + feats) * kblock,
        moved=6 * MIB,
    )
    parts = [parts[0]] + [swap(parts[s], "req", 2 * s) for s in range(1, half)]

    table = page_table.T
    moving = local_call(
        send_pages_kernel,
        [VMEM] + [SMEM] * 3,
        (page_pool, send_row, table, cache_len),
        [shape((n_send,) + table.shape[:1] + page_pool.shape[1:], BF)],
        moved=3 * MIB,
        after=[order],
    )[0]
    page = moving.shape[1:]
    pair_pages = swap(moving[:n_pair], "req", 1).reshape((half, MIG) + page)
    own_pages = jnp.concatenate([moving[:MIG], moving[n_pair:]], axis=0).reshape((half, MIG) + page)
    pages = jnp.concatenate([own_pages, pair_pages], axis=1)
    stages = half.bit_length() - 1
    block = pages.shape[1:]
    pages = pages.reshape((half // 2, 2) + block)
    page_rows = pages[:, 1].reshape(-1, page[-1])

    router = jnp.pad(router_w.T, ((0, 8 - experts), (0, 0)))
    late_shapes = [(SLOTS, rest)] * experts
    late_shapes[2] = (SLOTS + page_rows.shape[0], page[-1])
    normed = local_call(
        functools.partial(norm_kernel, half, experts, wide),
        [VMEM] * (4 + half),
        (norm_gain[None, :], router, slot_pick, page_rows, *parts),
        [far((rows, feats), F32), far((rows + 16, wide), BF)]
        + [far(dims, BF) for dims in late_shapes],
        flops=2 * experts * SLOTS * rows * rest,
        moved=3 * MIB,
    )
    hidden, early = normed[:2]
    late = [normed[2 + s] if s == 0 else swap(normed[2 + s], "req", s) for s in range(experts)]
    early_blocks = [early] + [swap(early, "exp", s) for s in range(1, ne)]
    came_pages = late[2][SLOTS:].reshape((half // 2,) + block)
    pages = jnp.stack([pages[:, 0], came_pages], axis=1)
    outgoing = local_call(
        functools.partial(dispatch_kernel, ne, experts),
        [SMEM] + [VMEM] * (1 + ne + experts),
        (place, slot_pick, *early_blocks, *late),
        [far((SLOTS, ne * wide + 128), BF)]
        + [near((SLOTS, ne * wide + 128), BF)] * (experts - 1)
        + [near((16, rows), F32), far((experts * SLOTS, rest), BF)],
        vmem=60,
        flops=2 * experts * SLOTS * rows * ne * wide,
        moved=3 * MIB,
    )
    late = outgoing[experts + 1]
    late_rows = [late] + [swap(late, "exp", s) for s in range(1, ne)]

    early_rows = [swap(outgoing[s], "req", s) if s else outgoing[s] for s in range(experts)]

    crossing = pages
    for bit in range(1, stages):
        pages = pages.reshape((half >> (bit + 1), 2, 1 << bit) + block)
        came_pages = swap(pages[:, 1], "req", 2 << bit)
        pages = jnp.stack([pages[:, 0], came_pages], axis=1)
    moved_pages = pages.reshape((half * 2 * MIG,) + page)

    down_late, down_early, stats = expert_call(
        place, early_rows, late_rows, w_gate, w_up, w_down, outgoing[experts], ne, crossing
    )
    late_blocks = [down_late[0]] + [swap(down_late[s], "exp", s) for s in range(1, ne)]
    near_back = hold(down_early[1], late_blocks[-1])
    early_back = [
        swap(down_early[s] if s > 1 else near_back, "req", s) if s else down_early[s]
        for s in range(experts)
    ]
    new_pages = take_pages(
        page_pool,
        moved_pages,
        jnp.where(own_stays, src_local[0], 0),
        jnp.where(own_stays, -1, own_slot),
        table,
        cache_len,
        [stats],
    )
    weighted = local_call(
        functools.partial(weigh_kernel, ne, experts),
        [SMEM] + [VMEM] * (3 + experts + ne),
        (place, stats, routes.T, slot_of, *early_back, *late_blocks),
        [near((rows, wide), F32)]
        + [near((rows, wide), BF)] * (ne - 1)
        + [near((SLOTS, rest), BF)] * experts
        + [shape((rows, experts * SLOTS), BF)] * 2,
        [pltpu.VMEM((experts * SLOTS, ne * wide), BF), pltpu.VMEM((rows, ne * wide), F32)],
        flops=4 * rows * experts * SLOTS * ne * wide,
        moved=3 * MIB,
    )
    early_parts = [swap(weighted[s], "exp", s) for s in range(ne - 1, 0, -1)]
    early_parts = [weighted[0]] + early_parts[::-1]
    late_back = [
        swap(weighted[ne + s], "req", s) if s else weighted[ne] for s in range(experts)
    ]
    mixed = local_call(
        functools.partial(finish_kernel, ne, experts, wide),
        [VMEM] * (3 + ne + experts),
        (*weighted[-2:], hidden, *early_parts, *late_back),
        [shape((rows, feats), F32)],
        [pltpu.VMEM((experts * SLOTS, rest), BF)],
        flops=4 * rows * experts * SLOTS * rest,
        moved=2 * MIB,
    )[0]

    return (mixed, new_pages)


def solution(mesh):
    in_specs = (
        P("req", None),
        P("req", "exp"),
        P("req", "exp"),
        P("exp", None),
        P("exp"),
        P("req", None, "exp"),
        P("req", None),
        P("req"),
        P(),
        P("req", None),
        P("req", None, "exp"),
        P("req", None, "exp"),
        P("req", "exp", None),
    )
    out_specs = (P("req", "exp"), P("req", None, None, "exp"))
    return jax.shard_map(body, mesh=mesh, in_specs=in_specs, out_specs=out_specs, check_vma=False)
```
